512 devices in a mesh: seq: 128 (over z, y, core), tp: 4 (over x).
Axes of the slice: x: 4, y: 8, z: 8, core: 2. Of those that a mesh axis runs over, the one named last changes fastest.
Arguments:
- query_in: bfloat16 [16384, 1024], P('seq', 'tp'), may hold values from -6 to 6
- key_in: bfloat16 [16384, 1024], P('seq', 'tp'), may hold values from -6 to 6
- value_in: bfloat16 [16384, 1024], P('seq', 'tp'), may hold values from -6 to 6
- short_weight: float32 [3, 7, 1024], P(None, None, 'tp'), may hold values from -2 to 2
- residue: float32 [16, 1024], P(None, 'tp'), may hold values from -1.5 to 1.5
- rate: float32 [16, 1024], P(None, 'tp'), may hold values from 1e-05 to 0.05
- skip: float32 [1024], P('tp'), may hold values from -4 to 4
- out_weight: bfloat16 [1024, 4096], P('tp'), may hold values from -0.1875 to 0.1875
Outputs:
- mixed: bfloat16 [16384, 4096], P('seq', 'tp')
The draws below stay inside these ranges and needn't reach their ends.
All inputs are finite; a program needn't handle non-finite values.
Results may differ from the reference program's by a relative error of at most 0.0049.
Values may be sent and summed in bfloat16 or wider, within the bound.
No kernel may reach another device: no remote copies, remote signals or barrier semaphores. Data moves between devices by JAX's collectives and lax.ppermute only.
A program may use at most 64 MiB of HBM per device.

```python
import math
import jax
import jax.numpy as jnp
from jax import lax

D = 4096
SLAB = 1024
ORDER = 16
KERNEL = 7
TOKENS = 16384


def level_of(stream_key, shape, split, least, high):
    gain, own = 1.0, jax.random.fold_in(stream_key, 6)
    for dim, parts in split:
        steps = jnp.exp(jax.random.uniform(jax.random.fold_in(own, dim), (parts,), jnp.float32, least / len(split), high / len(split)))
        gain = gain * jnp.repeat(steps, shape[dim] // parts).reshape([-1 if axis == dim else 1 for axis in range(len(shape))])
    return gain


def noise(own_key, shape, width, most, pieces=(), kind=jnp.bfloat16):
    array = jax.random.normal(own_key, shape, jnp.float32) * width
    if len(pieces) > 0:
        array = level_of(own_key, shape, pieces, -0.22, 0.18) * array
    return jnp.clip(array, min=-most, max=most).astype(kind)


def setup_inputs(seed: int = 0) -> dict:
    seeds = jax.random.split(jax.random.key(seed), 9)
    query_in = noise(seeds[0], (TOKENS, SLAB), 1.0, 6.0, ((0, 128), (1, 4)))
    key_in = noise(seeds[1], (TOKENS, SLAB), 1.0, 6.0, ((0, 128), (1, 4)))
    value_in = noise(seeds[2], (TOKENS, SLAB), 1.0, 6.0, ((0, 128), (1, 4)))
    short_weight = noise(seeds[3], (3, KERNEL, SLAB), KERNEL ** -0.5, 2.0, ((2, 4),), jnp.float32)
    residue = noise(seeds[4], (ORDER, SLAB), ORDER ** -0.5, 1.5, ((1, 4),), jnp.float32)
    rate = jnp.clip(jnp.exp(math.log(0.05) - 8.517193 * jax.random.uniform(seeds[5], (ORDER, SLAB), jnp.float32) ** level_of(seeds[5], (ORDER, SLAB), ((1, 4),), -0.2, 0.2)), 9.999999747378752e-06, 0.05)
    skip = noise(seeds[6], (SLAB,), 1.0, 4.0, ((0, 4),), jnp.float32)
    out_weight = noise(seeds[7], (SLAB, D), SLAB ** -0.5, 0.1875, ((0, 4),))
    return {"query_in": query_in, "key_in": key_in, "value_in": value_in, "short_weight": short_weight, "residue": residue, "rate": rate, "skip": skip, "out_weight": out_weight}


def short_conv(signal, weights):
    taps = weights.shape[0]
    rows_here = signal.shape[0]
    padded = jnp.concatenate([jnp.zeros((taps - 1, signal.shape[1]), jnp.float32), signal.astype(jnp.float32)], axis=0)
    total = jnp.zeros((rows_here, signal.shape[1]), jnp.float32)
    for offset in range(taps):
        total = total + weights[offset] * padded[taps - 1 - offset:taps - 1 - offset + rows_here]
    return total

def mode_spectrum(rate_block, residue_block, length):
    period = 2 * length
    indices = jnp.arange(period, dtype=jnp.int32)
    angles = (2.0 * math.pi / period * indices.astype(jnp.float32))[:, None]
    parity = (1 - 2 * (indices % 2)).astype(jnp.float32)[:, None]
    spec_real = jnp.zeros((period, rate_block.shape[1]), jnp.float32)
    spec_imag = jnp.zeros((period, rate_block.shape[1]), jnp.float32)
    for order_index in range(rate_block.shape[0]):
        decay = rate_block[order_index]
        retain = jnp.exp(-decay)
        amplitude = residue_block[order_index] * jnp.sqrt(-jnp.expm1(-2.0 * decay))
        leftover = jnp.exp(-decay * length)
        numerator = amplitude * (1.0 - leftover * parity)
        below_real = -jnp.expm1(-decay) + 2.0 * retain * jnp.sin(0.5 * angles) ** 2
        below_imag = retain * jnp.sin(angles)
        below_norm = below_real * below_real + below_imag * below_imag
        spec_real = spec_real + numerator * below_real / below_norm
        spec_imag = spec_imag - numerator * below_imag / below_norm
    return (spec_real, spec_imag)

def reference(query_in, key_in, value_in, short_weight, residue, rate, skip, out_weight):
    queries = short_conv(query_in, short_weight[0])
    keys = short_conv(key_in, short_weight[1])
    values = short_conv(value_in, short_weight[2])
    gated = keys * values
    block = math.gcd(SLAB, 128)
    blocks = SLAB // block

    def block_conv(inputs):
        gated_block, rate_block, residue_block = inputs
        spec_real, spec_imag = mode_spectrum(rate_block, residue_block, TOKENS)
        forward = jnp.fft.fft(gated_block, n=2 * TOKENS, axis=0)
        inverse = jnp.fft.ifft(forward * lax.complex(spec_real, spec_imag), axis=0)
        return jnp.real(inverse[:TOKENS])
    stacked = (gated.reshape(TOKENS, blocks, block).transpose(1, 0, 2), rate.reshape(ORDER, blocks, block).transpose(1, 0, 2), residue.reshape(ORDER, blocks, block).transpose(1, 0, 2))
    longconv = lax.map(block_conv, stacked).transpose(1, 0, 2).reshape(TOKENS, SLAB)
    hyena = (queries * (longconv + skip * gated)).astype(jnp.bfloat16)
    return jnp.dot(hyena, out_weight, preferred_element_type=jnp.float32).astype(jnp.bfloat16)
```

```python
import math

import jax
import jax.numpy as jnp
from jax import lax
from jax.experimental import pallas as pl
from jax.experimental.pallas import tpu as pltpu
from jax.sharding import Mesh, PartitionSpec as P

F32 = jnp.float32
BF16 = jnp.bfloat16
LANES = 128
SUBS = 8
RIM = 16


def shape(dims, dtype):
    return jax.ShapeDtypeStruct(dims, dtype)


def call(body, outs, scratch=(), flops=0, name=None):
    return pl.pallas_call(
        body,
        out_shape=outs,
        scratch_shapes=list(scratch),
        name=name,
    )


def row_of(ref, m, lanes):
    return ref[pl.ds(m, 1), lanes]


def wide(row):
    return jnp.broadcast_to(row, (SUBS, LANES))


def gate_body(q_ref, k_ref, v_ref, rim_ref, taps_ref, rate_ref, query_ref, gated_ref, begin_ref, state_ref, pad, held):
    rows, channels = q_ref.shape
    modes = rate_ref.shape[0]
    taps = taps_ref.shape[1]
    steps = rows // SUBS
    for i, ref in enumerate((q_ref, k_ref, v_ref)):
        pad[i, pl.ds(0, RIM), :] = rim_ref[pl.ds(i * RIM, RIM), :].astype(F32)
        pad[i, pl.ds(RIM, rows), :] = ref[...].astype(F32)
    block = 32
    for half in range(channels // LANES):
        lanes = pl.ds(half * LANES, LANES)
        for r in range(0, rows, block):
            sums = []
            for i in range(3):
                total = jnp.zeros((block, LANES), F32)
                for t in range(taps):
                    total = total + taps_ref[i, pl.ds(t, 1), lanes] * pad[i, pl.ds(RIM + r - t, block), lanes]
                sums.append(total)
            query_ref[half, pl.ds(r, block), :] = sums[0]
            gated_ref[half, pl.ds(r, block), :] = sums[1] * sums[2]
    sub = lax.broadcasted_iota(jnp.int32, (SUBS, LANES), 0)
    for half in range(channels // LANES):
        lanes = pl.ds(half * LANES, LANES)
        rates = [row_of(rate_ref, m, lanes) for m in range(modes)]
        retain = [wide(jnp.exp(-x)) for x in rates]
        state = [jnp.zeros((SUBS, LANES), F32) for _ in range(modes)]
        for step in range(steps):
            g = gated_ref[half, pl.ds(step, SUBS, stride=steps), :]
            state = [a * s + g for a, s in zip(retain, state)]
        for m in range(modes):
            s = state[m]
            for d in (1, 2, 4):
                drop = wide(jnp.exp(-(steps * d) * rates[m]))
                s = s + jnp.where(sub >= d, drop * pltpu.roll(s, d, 0), 0.0)
            held[pl.ds(m, 1), lanes] = s[SUBS - 1 :]
            begin_ref[m, :, lanes] = jnp.where(sub >= 1, pltpu.roll(s, 1, 0), 0.0)
    whole = held[...]
    for i in range(state_ref.shape[0]):
        state_ref[i] = whole


def plane_body(own, rows, parts_ref, rate_ref, before_ref, total_ref):
    me = lax.axis_index(own[0]) * 2 + lax.axis_index(own[1])
    drop = jnp.exp(-rows * rate_ref[...])
    before = jnp.zeros(rate_ref.shape, F32)
    total = jnp.zeros(rate_ref.shape, F32)
    for i in range(parts_ref.shape[0]):
        part = parts_ref[i]
        before = jnp.where(i < me, before * drop + part, before)
        total = total * drop + part
    before_ref[...] = before
    for i in range(total_ref.shape[0]):
        total_ref[i] = total


def mix_body(own, rows_plane, query_ref, gated_ref, begin_ref, before_ref, planes_ref, rate_ref, amp_ref, skip_ref, weight_ref, out_ref, hyena, carry):
    halves, rows, _ = query_ref.shape
    modes = rate_ref.shape[0]
    steps = rows // SUBS
    z = lax.axis_index(own[0])
    me = lax.axis_index(own[1]) * 2 + lax.axis_index(own[2])
    drop = jnp.exp(-rows_plane * rate_ref[...])
    behind = jnp.zeros(rate_ref.shape, F32)
    for i in range(planes_ref.shape[0]):
        behind = jnp.where(i < z, behind * drop + planes_ref[i], behind)
    carry[...] = before_ref[...] + jnp.exp(-(rows * me).astype(F32) * rate_ref[...]) * behind
    sub = lax.broadcasted_iota(jnp.int32, (SUBS, LANES), 0).astype(F32)
    for half in range(halves):
        lanes = pl.ds(half * LANES, LANES)
        rates = [row_of(rate_ref, m, lanes) for m in range(modes)]
        retain = [wide(jnp.exp(-x)) for x in rates]
        amp = [wide(row_of(amp_ref, m, lanes)) for m in range(modes)]
        skip = wide(row_of(skip_ref, 0, lanes))
        state = [
            begin_ref[m, :, lanes] + jnp.exp(-(steps * sub) * rates[m]) * row_of(carry, m, lanes)
            for m in range(modes)
        ]
        for step in range(steps):
            at = pl.ds(step, SUBS, stride=steps)
            g = gated_ref[half, at, :]
            state = [a * s + g for a, s in zip(retain, state)]
            terms = [a * s for a, s in zip(amp, state)] + [skip * g]
            while len(terms) > 1:
                terms = [x + y for x, y in zip(terms[::2], terms[1::2])] + terms[len(terms) // 2 * 2 :]
            hyena[half, at, :] = query_ref[half, at, :] * terms[0]
    left = jnp.concatenate([hyena[half].astype(BF16) for half in range(halves)], axis=1)
    width = out_ref.shape[2]
    block = 512
    for i in range(out_ref.shape[0]):
        for c in range(0, width, block):
            out_ref[i, :, pl.ds(c, block)] = jnp.dot(
                left, weight_ref[:, pl.ds(i * width + c, block)], preferred_element_type=F32
            ).astype(BF16)


def sum_body(parts_ref, out_ref):
    total = parts_ref[0].astype(F32)
    for i in range(1, parts_ref.shape[0]):
        total = total + parts_ref[i].astype(F32)
    out_ref[...] = total.astype(BF16)


def local(query_in, key_in, value_in, short_weight, residue, rate, skip, out_weight):
    rows, channels = query_in.shape
    modes = rate.shape[0]
    planes = lax.axis_size("z")
    plane = lax.axis_size("y") * lax.axis_size("core")
    parts = lax.axis_size("tp")
    width = out_weight.shape[1] // parts
    order = ("z", "y", "core")
    devices = planes * plane
    rims = jnp.concatenate([x[rows - RIM :] for x in (query_in, key_in, value_in)], axis=0)
    rims = lax.ppermute(rims, order, [(i, i + 1) for i in range(devices - 1)])
    amplitude = residue * jnp.sqrt(-jnp.expm1(-2.0 * rate))
    queries, gated, begin, states = call(
        gate_body,
        (
            shape((channels // LANES, rows, LANES), F32),
            shape((channels // LANES, rows, LANES), F32),
            shape((modes, SUBS, channels), F32),
            shape((plane, modes, channels), F32),
        ),
        (pltpu.VMEM((3, RIM + rows, channels), F32), pltpu.VMEM((modes, channels), F32)),
        name="gate",
    )(query_in, key_in, value_in, rims, short_weight, rate)
    states = lax.all_to_all(states, ("y", "core"), 0, 0, tiled=True)
    before, totals = call(
        lambda *refs: plane_body(("y", "core"), rows, *refs),
        (shape((modes, channels), F32), shape((planes, modes, channels), F32)),
        name="plane",
    )(states, rate)
    totals = lax.all_to_all(totals, "z", 0, 0, tiled=True)
    partial = call(
        lambda *refs: mix_body(order, rows * plane, *refs),
        shape((parts, rows, width), BF16),
        (pltpu.VMEM((channels // LANES, rows, LANES), F32), pltpu.VMEM((modes, channels), F32)),
        name="mix",
    )(queries, gated, begin, before, totals, rate, amplitude, skip.reshape(1, -1), out_weight)
    partial = lax.all_to_all(partial, "tp", 0, 0, tiled=True)
    return call(sum_body, shape((rows, width), BF16), name="total")(partial)


def solution(mesh):
    fine = Mesh(mesh.devices.reshape(8, 8, 2, 4), ("z", "y", "core", "tp"))
    seq = ("z", "y", "core")
    in_specs = (
        P(seq, "tp"),
        P(seq, "tp"),
        P(seq, "tp"),
        P(None, None, "tp"),
        P(None, "tp"),
        P(None, "tp"),
        P("tp"),
        P("tp", None),
    )
    return jax.shard_map(local, mesh=fine, in_specs=in_specs, out_specs=P(seq, "tp"), check_vma=False)
```

```python
import jax
import jax.numpy as jnp
from jax import lax
from jax.experimental import pallas as pl
from jax.experimental.pallas import tpu as pltpu
from jax.sharding import Mesh, PartitionSpec as P

F32 = jnp.float32
BF16 = jnp.bfloat16
LANES = 128
SUBS = 8
RIM = 16
HEAD = 8
MIB = 1 << 20


def shape(dims, dtype):
    return jax.ShapeDtypeStruct(dims, dtype)


VMEM = pl.BlockSpec(memory_space=pltpu.VMEM)
HBM = pl.BlockSpec(memory_space=pltpu.HBM)


def call(body, specs, outs, name, scratch=(), mib=4):
    return pl.pallas_call(
        body,
        in_specs=specs,
        out_specs=jax.tree.map(lambda _: VMEM, outs),
        out_shape=outs,
        scratch_shapes=list(scratch),
        compiler_params=pltpu.CompilerParams(vmem_limit_bytes=mib * MIB),
        name=name,
    )


def fetch(sources, targets, sems):
    copies = [pltpu.make_async_copy(s, t, sems.at[i]) for i, (s, t) in enumerate(zip(sources, targets))]
    for copy in copies:
        copy.start()
    return copies


def row_of(ref, m, lanes):
    return ref[pl.ds(m, 1), lanes]


def wide(row):
    return jnp.broadcast_to(row, (SUBS, LANES))


def one_minus_exp(x):
    series = 1.0 / 362880.0
    for n in (40320, 5040, 720, 120, 24, 6, 2, 1):
        series = 1.0 / n - x * series
    return jnp.where(x < 0.25, x * series, 1.0 - jnp.exp(-x))


def rim_body(q_ref, k_ref, v_ref, out_ref, sems):
    rows = q_ref.shape[0]
    refs = (q_ref, k_ref, v_ref)
    copies = fetch(
        [ref.at[pl.ds(rows - RIM, RIM), :] for ref in refs],
        [out_ref.at[pl.ds(i * RIM, RIM), :] for i in range(3)],
        sems,
    )
    for copy in copies:
        copy.wait()


def gate_body(
    q_hbm, k_hbm, v_hbm, taps_hbm, rate_hbm, residue_hbm,
    query_ref, gated_ref, begin_ref, state_ref, head_ref, taps_ref, rate_ref, amp_ref,
    streams, residue_ref, pad, sems,
):
    _, rows, channels = streams.shape
    modes = rate_ref.shape[0]
    taps = taps_ref.shape[1]
    steps = rows // SUBS
    copies = fetch(
        (q_hbm, k_hbm, v_hbm, taps_hbm, rate_hbm, residue_hbm),
        (streams.at[0], streams.at[1], streams.at[2], taps_ref, rate_ref, residue_ref),
        sems,
    )
    for copy in copies:
        copy.wait()
    amp_ref[...] = residue_ref[...] * jnp.sqrt(one_minus_exp(2.0 * rate_ref[...]))
    for i in range(3):
        pad[i, pl.ds(0, HEAD), :] = jnp.zeros((HEAD, channels), F32)
        pad[i, pl.ds(HEAD, rows), :] = streams[i].astype(F32)
    block = 32
    for half in range(channels // LANES):
        lanes = pl.ds(half * LANES, LANES)
        for r in range(0, rows, block):
            sums = []
            for i in range(3):
                total = jnp.zeros((block, LANES), F32)
                for t in range(taps):
                    total = total + taps_ref[i, pl.ds(t, 1), lanes] * pad[i, pl.ds(HEAD + r - t, block), lanes]
                sums.append(total)
                if r == 0:
                    head_ref[i, :, lanes] = total[:HEAD]
            query_ref[half, pl.ds(r, block), :] = sums[0]
            gated_ref[half, pl.ds(r, block), :] = sums[1] * sums[2]
    sub = lax.broadcasted_iota(jnp.int32, (SUBS, LANES), 0)
    for half in range(channels // LANES):
        lanes = pl.ds(half * LANES, LANES)
        rates = [row_of(rate_ref, m, lanes) for m in range(modes)]
        retain = [wide(jnp.exp(-x)) for x in rates]
        state = [jnp.zeros((SUBS, LANES), F32) for _ in range(modes)]
        for step in range(steps):
            g = gated_ref[half, pl.ds(step, SUBS, stride=steps), :]
            state = [a * s + g for a, s in zip(retain, state)]
        for m in range(modes):
            s = state[m]
            for d in (1, 2, 4):
                drop = wide(jnp.exp(-(steps * d) * rates[m]))
                s = s + jnp.where(sub >= d, drop * pltpu.roll(s, d, 0), 0.0)
            state_ref[pl.ds(m, 1), lanes] = s[SUBS - 1 :]
            begin_ref[m, :, lanes] = jnp.where(sub >= 1, pltpu.roll(s, 1, 0), 0.0)


def join_body(rows, rim_ref, head_ref, taps_ref, rate_ref, state_ref, out_ref, late_ref, top_ref, pad):
    modes, channels = rate_ref.shape
    taps = taps_ref.shape[1]
    sums = []
    for i in range(3):
        pad[i, pl.ds(0, HEAD), :] = rim_ref[pl.ds(i * RIM, RIM), :].astype(F32)[RIM - HEAD :]
        pad[i, pl.ds(HEAD, HEAD), :] = jnp.zeros((HEAD, channels), F32)
        total = head_ref[i]
        for t in range(1, taps):
            total = total + taps_ref[i, pl.ds(t, 1), :] * pad[i, pl.ds(HEAD - t, HEAD), :]
        sums.append(total)
    gated = sums[1] * sums[2]
    top_ref[0] = sums[0]
    top_ref[1] = gated
    more = gated - head_ref[1] * head_ref[2]
    rate = rate_ref[...]
    retain = jnp.exp(-rate)
    late = jnp.broadcast_to(more[:1], rate.shape)
    for i in range(1, taps - 1):
        late = retain * late + more[i : i + 1]
    late_ref[...] = late
    whole = state_ref[...] + jnp.exp(-(rows - taps + 1) * rate) * late
    for i in range(out_ref.shape[0]):
        out_ref[i] = whole


def plane_body(rows, parts_ref, rate_ref, before_ref, total_ref):
    me = lax.axis_index("y") * lax.axis_size("core") + lax.axis_index("core")
    drop = jnp.exp(-rows * rate_ref[...])
    before = jnp.zeros(rate_ref.shape, F32)
    total = jnp.zeros(rate_ref.shape, F32)
    for i in range(parts_ref.shape[0]):
        part = parts_ref[i]
        before = jnp.where(i < me, before * drop + part, before)
        total = total * drop + part
    before_ref[...] = before
    for i in range(total_ref.shape[0]):
        total_ref[i] = total


def mix_body(
    taps, plane_rows, query_ref, gated_ref, begin_ref, late_ref, top_ref, before_ref, planes_ref, rate_ref, amp_ref,
    skip_hbm, weight_hbm, out_ref, hyena, carry, skip_ref, weight, sems,
):
    halves, rows, _ = query_ref.shape
    modes = rate_ref.shape[0]
    steps = rows // SUBS
    parts, _, width = out_ref.shape
    copies = fetch(
        [skip_hbm] + [weight_hbm.at[:, pl.ds(i * width, width)] for i in range(parts)],
        [skip_ref] + [weight.at[i] for i in range(parts)],
        sems,
    )
    z = lax.axis_index("z")
    me = lax.axis_index("y") * lax.axis_size("core") + lax.axis_index("core")
    rate = rate_ref[...]
    drop = jnp.exp(-plane_rows * rate)
    behind = jnp.zeros(rate.shape, F32)
    for i in range(planes_ref.shape[0]):
        behind = jnp.where(i < z, behind * drop + planes_ref[i], behind)
    carried = before_ref[...] + jnp.exp(-(rows * me).astype(F32) * rate) * behind
    carry[0] = carried
    carry[1] = carried + jnp.exp((taps - 1) * rate) * late_ref[...]
    sub = lax.broadcasted_iota(jnp.int32, (SUBS, LANES), 0)
    ahead = sub.astype(F32) * float(steps)
    copies[0].wait()
    for half in range(halves):
        lanes = pl.ds(half * LANES, LANES)
        rates = [row_of(rate_ref, m, lanes) for m in range(modes)]
        retain = [wide(jnp.exp(-x)) for x in rates]
        amp = [wide(row_of(amp_ref, m, lanes)) for m in range(modes)]
        skip = wide(row_of(skip_ref, 0, lanes))
        state = [
            begin_ref[m, :, lanes]
            + jnp.exp(-ahead * rates[m])
            * jnp.where(sub >= 1, row_of(carry.at[1], m, lanes), row_of(carry.at[0], m, lanes))
            for m in range(modes)
        ]
        for step in range(steps):
            at = pl.ds(step, SUBS, stride=steps)
            g = gated_ref[half, at, :]
            query = query_ref[half, at, :]
            if step < taps - 1:
                query = jnp.where(sub >= 1, query, top_ref[0, pl.ds(step, 1), lanes])
                g = jnp.where(sub >= 1, g, top_ref[1, pl.ds(step, 1), lanes])
            state = [a * s + g for a, s in zip(retain, state)]
            terms = [a * s for a, s in zip(amp, state)] + [skip * g]
            while len(terms) > 1:
                terms = [x + y for x, y in zip(terms[::2], terms[1::2])] + terms[len(terms) // 2 * 2 :]
            hyena[half, at, :] = query * terms[0]
    left = jnp.concatenate([hyena[half].astype(BF16) for half in range(halves)], axis=1)
    block = 512
    for i in range(parts):
        copies[1 + i].wait()
        for c in range(0, width, block):
            out_ref[i, :, pl.ds(c, block)] = jnp.dot(
                left, weight[i, :, pl.ds(c, block)], preferred_element_type=F32
            ).astype(BF16)


def sum_body(parts_ref, out_ref):
    total = parts_ref[0].astype(F32)
    for i in range(1, parts_ref.shape[0]):
        total = total + parts_ref[i].astype(F32)
    out_ref[...] = total.astype(BF16)


def local(query_in, key_in, value_in, short_weight, residue, rate, skip, out_weight):
    rows, channels = query_in.shape
    modes = rate.shape[0]
    taps = short_weight.shape[1]
    planes = lax.axis_size("z")
    plane = lax.axis_size("y") * lax.axis_size("core")
    parts = lax.axis_size("tp")
    width = out_weight.shape[1] // parts
    order = ("z", "y", "core")
    devices = planes * plane
    by_half = (channels // LANES, rows, LANES)
    skip = skip.reshape(1, -1)
    query_in, key_in, value_in, short_weight, residue, rate, skip, out_weight = (
        pltpu.with_memory_space_constraint(x, pltpu.HBM)
        for x in (query_in, key_in, value_in, short_weight, residue, rate, skip, out_weight)
    )
    rims = call(
        rim_body, [HBM] * 3, shape((3 * RIM, channels), BF16), "rims", [pltpu.SemaphoreType.DMA((3,))]
    )(query_in, key_in, value_in)
    rims = lax.ppermute(rims, order, [(i, i + 1) for i in range(devices - 1)])
    queries, gated, begin, states, heads, taps_here, rate, amplitude = call(
        gate_body,
        [HBM] * 6,
        (
            shape(by_half, F32),
            shape(by_half, F32),
            shape((modes, SUBS, channels), F32),
            shape((modes, channels), F32),
            shape((3, HEAD, channels), F32),
            shape(short_weight.shape, F32),
            shape((modes, channels), F32),
            shape((modes, channels), F32),
        ),
        "gate",
        [
            pltpu.VMEM((3, rows, channels), BF16),
            pltpu.VMEM((modes, channels), F32),
            pltpu.VMEM((3, HEAD + rows, channels), F32),
            pltpu.SemaphoreType.DMA((6,)),
        ],
    )(query_in, key_in, value_in, short_weight, rate, residue)
    states, late, top = call(
        lambda *refs: join_body(rows, *refs),
        [VMEM] * 5,
        (
            shape((plane, modes, channels), F32),
            shape((modes, channels), F32),
            shape((2, HEAD, channels), F32),
        ),
        "join",
        [pltpu.VMEM((3, 2 * HEAD, channels), F32)],
    )(rims, heads, taps_here, rate, states)
    states = lax.all_to_all(states, ("y", "core"), 0, 0, tiled=True)
    before, totals = call(
        lambda *refs: plane_body(rows, *refs),
        [VMEM] * 2,
        (shape((modes, channels), F32), shape((planes, modes, channels), F32)),
        "plane",
    )(states, rate)
    totals = lax.all_to_all(totals, "z", 0, 0, tiled=True)
    partial = call(
        lambda *refs: mix_body(taps, rows * plane, *refs),
        [VMEM] * 9 + [HBM] * 2,
        shape((parts, rows, width), BF16),
        "mix",
        [
            pltpu.VMEM(by_half, F32),
            pltpu.VMEM((2, modes, channels), F32),
            pltpu.VMEM((1, channels), F32),
            pltpu.VMEM((parts, channels, width), BF16),
            pltpu.SemaphoreType.DMA((1 + parts,)),
        ],
        8,
    )(queries, gated, begin, late, top, before, totals, rate, amplitude, skip, out_weight)
    partial = lax.all_to_all(partial, "tp", 0, 0, tiled=True)
    return call(sum_body, [VMEM], shape((rows, width), BF16), "total")(partial)


def solution(mesh):
    fine = Mesh(mesh.devices.reshape(8, 8, 2, 4), ("z", "y", "core", "tp"))
    seq = ("z", "y", "core")
    in_specs = (
        P(seq, "tp"),
        P(seq, "tp"),
        P(seq, "tp"),
        P(None, None, "tp"),
        P(None, "tp"),
        P(None, "tp"),
        P("tp"),
        P("tp", None),
    )
    return jax.shard_map(local, mesh=fine, in_specs=in_specs, out_specs=P(seq, "tp"), check_vma=False)
```

```python
import jax
import jax.numpy as jnp
from jax import lax
from jax.experimental import pallas as pl
from jax.experimental.pallas import tpu as pltpu
from jax.sharding import Mesh, PartitionSpec as P

F32 = jnp.float32
BF16 = jnp.bfloat16
LANES = 128
SUBS = 8
RIM = 16
HEAD = 8
MIB = 1 << 20


def shape(dims, dtype):
    return jax.ShapeDtypeStruct(dims, dtype)


VMEM = pl.BlockSpec(memory_space=pltpu.VMEM)
HBM = pl.BlockSpec(memory_space=pltpu.HBM)


def call(body, specs, outs, name, scratch=(), mib=4):
    return pl.pallas_call(
        body,
        in_specs=specs,
        out_specs=jax.tree.map(lambda _: VMEM, outs),
        out_shape=outs,
        scratch_shapes=list(scratch),
        compiler_params=pltpu.CompilerParams(vmem_limit_bytes=mib * MIB),
        name=name,
    )


def fetch(sources, targets, sems):
    copies = [pltpu.make_async_copy(s, t, sems.at[i]) for i, (s, t) in enumerate(zip(sources, targets))]
    for copy in copies:
        copy.start()
    return copies


def row_of(ref, m, lanes):
    return ref[pl.ds(m, 1), lanes]


def wide(row):
    return jnp.broadcast_to(row, (SUBS, LANES))


def one_minus_exp(x):
    series = 1.0 / 362880.0
    for n in (40320, 5040, 720, 120, 24, 6, 2, 1):
        series = 1.0 / n - x * series
    return jnp.where(x < 0.25, x * series, 1.0 - jnp.exp(-x))


def rim_body(q_ref, k_ref, v_ref, out_ref, sems):
    rows = q_ref.shape[0]
    refs = (q_ref, k_ref, v_ref)
    copies = fetch(
        [ref.at[pl.ds(rows - RIM, RIM), :] for ref in refs],
        [out_ref.at[pl.ds(i * RIM, RIM), :] for i in range(3)],
        sems,
    )
    for copy in copies:
        copy.wait()


def gate_body(
    q_hbm, k_hbm, v_hbm, taps_hbm, rate_hbm, residue_hbm,
    query_ref, gated_ref, begin_ref, state_ref, head_ref, taps_ref, rate_ref, amp_ref,
    streams, residue_ref, pad, sems,
):
    _, rows, channels = streams.shape
    modes = rate_ref.shape[0]
    taps = taps_ref.shape[1]
    steps = rows // SUBS
    copies = fetch(
        (q_hbm, k_hbm, v_hbm, taps_hbm, rate_hbm, residue_hbm),
        (streams.at[0], streams.at[1], streams.at[2], taps_ref, rate_ref, residue_ref),
        sems,
    )
    for copy in copies:
        copy.wait()
    amp_ref[...] = residue_ref[...] * jnp.sqrt(one_minus_exp(2.0 * rate_ref[...]))
    for i in range(3):
        pad[i, pl.ds(0, HEAD), :] = jnp.zeros((HEAD, channels), F32)
        pad[i, pl.ds(HEAD, rows), :] = streams[i].astype(F32)
    block = 32
    for half in range(channels // LANES):
        lanes = pl.ds(half * LANES, LANES)
        for r in range(0, rows, block):
            sums = []
            for i in range(3):
                total = jnp.zeros((block, LANES), F32)
                for t in range(taps):
                    total = total + taps_ref[i, pl.ds(t, 1), lanes] * pad[i, pl.ds(HEAD + r - t, block), lanes]
                sums.append(total)
                if r == 0:
                    head_ref[i, :, lanes] = total[:HEAD]
            query_ref[half, pl.ds(r, block), :] = sums[0]
            gated_ref[half, pl.ds(r, block), :] = sums[1] * sums[2]
    sub = lax.broadcasted_iota(jnp.int32, (SUBS, LANES), 0)
    for half in range(channels // LANES):
        lanes = pl.ds(half * LANES, LANES)
        rates = [row_of(rate_ref, m, lanes) for m in range(modes)]
        retain = [wide(jnp.exp(-x)) for x in rates]
        state = [jnp.zeros((SUBS, LANES), F32) for _ in range(modes)]
        for step in range(steps):
            g = gated_ref[half, pl.ds(step, SUBS, stride=steps), :]
            state = [a * s + g for a, s in zip(retain, state)]
        for m in range(modes):
            s = state[m]
            for d in (1, 2, 4):
                drop = wide(jnp.exp(-(steps * d) * rates[m]))
                s = s + jnp.where(sub >= d, drop * pltpu.roll(s, d, 0), 0.0)
            state_ref[pl.ds(m, 1), lanes] = s[SUBS - 1 :]
            begin_ref[m, :, lanes] = jnp.where(sub >= 1, pltpu.roll(s, 1, 0), 0.0)


def join_body(rows, rim_ref, head_ref, taps_ref, rate_ref, state_ref, out_ref, late_ref, top_ref, pad):
    modes, channels = rate_ref.shape
    taps = taps_ref.shape[1]
    sums = []
    for i in range(3):
        pad[i, pl.ds(0, HEAD), :] = rim_ref[pl.ds(i * RIM, RIM), :].astype(F32)[RIM - HEAD :]
        pad[i, pl.ds(HEAD, HEAD), :] = jnp.zeros((HEAD, channels), F32)
        total = head_ref[i]
        for t in range(1, taps):
            total = total + taps_ref[i, pl.ds(t, 1), :] * pad[i, pl.ds(HEAD - t, HEAD), :]
        sums.append(total)
    gated = sums[1] * sums[2]
    top_ref[0] = sums[0]
    top_ref[1] = gated
    more = gated - head_ref[1] * head_ref[2]
    rate = rate_ref[...]
    retain = jnp.exp(-rate)
    late = jnp.broadcast_to(more[:1], rate.shape)
    for i in range(1, taps - 1):
        late = retain * late + more[i : i + 1]
    late_ref[...] = late
    whole = (state_ref[...] + jnp.exp(-(rows - taps + 1) * rate) * late).astype(BF16)
    for i in range(out_ref.shape[0]):
        out_ref[i] = whole


def plane_body(rows, parts_ref, rate_ref, before_ref, total_ref):
    me = lax.axis_index("y") * lax.axis_size("core") + lax.axis_index("core")
    drop = jnp.exp(-rows * rate_ref[...])
    before = jnp.zeros(rate_ref.shape, F32)
    total = jnp.zeros(rate_ref.shape, F32)
    for i in range(parts_ref.shape[0]):
        part = parts_ref[i].astype(F32)
        before = jnp.where(i < me, before * drop + part, before)
        total = total * drop + part
    before_ref[...] = before
    for i in range(total_ref.shape[0]):
        total_ref[i] = total.astype(BF16)


def mix_body(
    taps, plane_rows, query_ref, gated_ref, begin_ref, late_ref, top_ref, before_ref, planes_ref, rate_ref, amp_ref,
    skip_hbm, weight_hbm, out_ref, hyena, carry, skip_ref, weight, sems,
):
    halves, rows, _ = query_ref.shape
    modes = rate_ref.shape[0]
    steps = rows // SUBS
    parts, _, width = out_ref.shape
    copies = fetch(
        [skip_hbm] + [weight_hbm.at[:, pl.ds(i * width, width)] for i in range(parts)],
        [skip_ref] + [weight.at[i] for i in range(parts)],
        sems,
    )
    z = lax.axis_index("z")
    me = lax.axis_index("y") * lax.axis_size("core") + lax.axis_index("core")
    rate = rate_ref[...]
    drop = jnp.exp(-plane_rows * rate)
    behind = jnp.zeros(rate.shape, F32)
    for i in range(planes_ref.shape[0]):
        behind = jnp.where(i < z, behind * drop + planes_ref[i].astype(F32), behind)
    carried = before_ref[...] + jnp.exp(-(rows * me).astype(F32) * rate) * behind
    carry[0] = carried
    carry[1] = carried + jnp.exp((taps - 1) * rate) * late_ref[...]
    sub = lax.broadcasted_iota(jnp.int32, (SUBS, LANES), 0)
    ahead = sub.astype(F32) * float(steps)
    copies[0].wait()
    for half in range(halves):
        lanes = pl.ds(half * LANES, LANES)
        rates = [row_of(rate_ref, m, lanes) for m in range(modes)]
        retain = [wide(jnp.exp(-x)) for x in rates]
        amp = [wide(row_of(amp_ref, m, lanes)) for m in range(modes)]
        skip = wide(row_of(skip_ref, 0, lanes))
        state = [
            begin_ref[m, :, lanes]
            + jnp.exp(-ahead * rates[m])
            * jnp.where(sub >= 1, row_of(carry.at[1], m, lanes), row_of(carry.at[0], m, lanes))
            for m in range(modes)
        ]
        for step in range(steps):
            at = pl.ds(step, SUBS, stride=steps)
            g = gated_ref[half, at, :]
            query = query_ref[half, at, :]
            if step < taps - 1:
                query = jnp.where(sub >= 1, query, top_ref[0, pl.ds(step, 1), lanes])
                g = jnp.where(sub >= 1, g, top_ref[1, pl.ds(step, 1), lanes])
            state = [a * s + g for a, s in zip(retain, state)]
            terms = [a * s for a, s in zip(amp, state)] + [skip * g]
            while len(terms) > 1:
                terms = [x + y for x, y in zip(terms[::2], terms[1::2])] + terms[len(terms) // 2 * 2 :]
            hyena[half, at, :] = query * terms[0]
    left = jnp.concatenate([hyena[half].astype(BF16) for half in range(halves)], axis=1)
    block = 512
    for i in range(parts):
        copies[1 + i].wait()
        for c in range(0, width, block):
            out_ref[i, :, pl.ds(c, block)] = jnp.dot(
                left, weight[i, :, pl.ds(c, block)], preferred_element_type=F32
            ).astype(BF16)


def sum_body(parts_ref, out_ref):
    total = parts_ref[0].astype(F32)
    for i in range(1, parts_ref.shape[0]):
        total = total + parts_ref[i].astype(F32)
    out_ref[...] = total.astype(BF16)


def local(query_in, key_in, value_in, short_weight, residue, rate, skip, out_weight):
    rows, channels = query_in.shape
    modes = rate.shape[0]
    taps = short_weight.shape[1]
    planes = lax.axis_size("z")
    plane = lax.axis_size("y") * lax.axis_size("core")
    parts = lax.axis_size("tp")
    width = out_weight.shape[1] // parts
    order = ("z", "y", "core")
    devices = planes * plane
    by_half = (channels // LANES, rows, LANES)
    skip = skip.reshape(1, -1)
    query_in, key_in, value_in, short_weight, residue, rate, skip, out_weight = (
        pltpu.with_memory_space_constraint(x, pltpu.HBM)
        for x in (query_in, key_in, value_in, short_weight, residue, rate, skip, out_weight)
    )
    rims = call(
        rim_body, [HBM] * 3, shape((3 * RIM, channels), BF16), "rims", [pltpu.SemaphoreType.DMA((3,))]
    )(query_in, key_in, value_in)
    rims = lax.ppermute(rims, order, [(i, i + 1) for i in range(devices - 1)])
    queries, gated, begin, states, heads, taps_here, rate, amplitude = call(
        gate_body,
        [HBM] * 6,
        (
            shape(by_half, F32),
            shape(by_half, F32),
            shape((modes, SUBS, channels), F32),
            shape((modes, channels), F32),
            shape((3, HEAD, channels), F32),
            shape(short_weight.shape, F32),
            shape((modes, channels), F32),
            shape((modes, channels), F32),
        ),
        "gate",
        [
            pltpu.VMEM((3, rows, channels), BF16),
            pltpu.VMEM((modes, channels), F32),
            pltpu.VMEM((3, HEAD + rows, channels), F32),
            pltpu.SemaphoreType.DMA((6,)),
        ],
    )(query_in, key_in, value_in, short_weight, rate, residue)
    states, late, top = call(
        lambda *refs: join_body(rows, *refs),
        [VMEM] * 5,
        (
            shape((plane, modes, channels), BF16),
            shape((modes, channels), F32),
            shape((2, HEAD, channels), F32),
        ),
        "join",
        [pltpu.VMEM((3, 2 * HEAD, channels), F32)],
    )(rims, heads, taps_here, rate, states)
    states = lax.all_to_all(states, ("y", "core"), 0, 0, tiled=True)
    before, totals = call(
        lambda *refs: plane_body(rows, *refs),
        [VMEM] * 2,
        (shape((modes, channels), F32), shape((planes, modes, channels), BF16)),
        "plane",
    )(states, rate)
    totals = lax.all_to_all(totals, "z", 0, 0, tiled=True)
    partial = call(
        lambda *refs: mix_body(taps, rows * plane, *refs),
        [VMEM] * 9 + [HBM] * 2,
        shape((parts, rows, width), BF16),
        "mix",
        [
            pltpu.VMEM(by_half, F32),
            pltpu.VMEM((2, modes, channels), F32),
            pltpu.VMEM((1, channels), F32),
            pltpu.VMEM((parts, channels, width), BF16),
            pltpu.SemaphoreType.DMA((1 + parts,)),
        ],
        8,
    )(queries, gated, begin, late, top, before, totals, rate, amplitude, skip, out_weight)
    partial = lax.all_to_all(partial, "tp", 0, 0, tiled=True)
    return call(sum_body, [VMEM], shape((rows, width), BF16), "total")(partial)


def solution(mesh):
    fine = Mesh(mesh.devices.reshape(8, 8, 2, 4), ("z", "y", "core", "tp"))
    seq = ("z", "y", "core")
    in_specs = (
        P(seq, "tp"),
        P(seq, "tp"),
        P(seq, "tp"),
        P(None, None, "tp"),
        P(None, "tp"),
        P(None, "tp"),
        P("tp"),
        P("tp", None),
    )
    return jax.shard_map(local, mesh=fine, in_specs=in_specs, out_specs=P(seq, "tp"), check_vma=False)
```

```python
import jax
import jax.numpy as jnp
from jax import lax
from jax.experimental import pallas as pl
from jax.experimental.pallas import tpu as pltpu
from jax.sharding import Mesh, PartitionSpec as P

F32 = jnp.float32
BF16 = jnp.bfloat16
LANES = 128
SUBS = 8
RIM = 16
HEAD = 8
MIB = 1 << 20


def shape(dims, dtype):
    return jax.ShapeDtypeStruct(dims, dtype)


VMEM = pl.BlockSpec(memory_space=pltpu.VMEM)
HBM = pl.BlockSpec(memory_space=pltpu.HBM)


def call(body, specs, outs, name, scratch=(), mib=4):
    return pl.pallas_call(
        body,
        in_specs=specs,
        out_specs=jax.tree.map(lambda _: VMEM, outs),
        out_shape=outs,
        scratch_shapes=list(scratch),
        compiler_params=pltpu.CompilerParams(vmem_limit_bytes=mib * MIB),
        name=name,
    )


def fetch(sources, targets, sems):
    copies = [pltpu.make_async_copy(s, t, sems.at[i]) for i, (s, t) in enumerate(zip(sources, targets))]
    for copy in copies:
        copy.start()
    return copies


def row_of(ref, m, lanes):
    return ref[pl.ds(m, 1), lanes]


def wide(row):
    return jnp.broadcast_to(row, (SUBS, LANES))


def one_minus_exp(x):
    series = 1.0 / 362880.0
    for n in (40320, 5040, 720, 120, 24, 6, 2, 1):
        series = 1.0 / n - x * series
    return jnp.where(x < 0.25, x * series, 1.0 - jnp.exp(-x))


def rim_body(q_ref, k_ref, v_ref, out_ref, sems):
    rows = q_ref.shape[0]
    refs = (q_ref, k_ref, v_ref)
    copies = fetch(
        [ref.at[pl.ds(rows - RIM, RIM), :] for ref in refs],
        [out_ref.at[pl.ds(i * RIM, RIM), :] for i in range(3)],
        sems,
    )
    for copy in copies:
        copy.wait()


def gate_body(
    q_hbm, k_hbm, v_hbm, taps_hbm, rate_hbm, residue_hbm, weight_hbm,
    query_ref, gated_ref, begin_ref, state_ref, head_ref, taps_ref, rate_ref, amp_ref, *rest,
):
    *blocks, streams, residue_ref, pad, sems = rest
    here, parts = lax.axis_index("tp"), lax.axis_size("tp")
    width = blocks[0].shape[1]
    _, rows, channels = streams.shape
    modes = rate_ref.shape[0]
    taps = taps_ref.shape[1]
    steps = rows // SUBS
    copies = fetch(
        (q_hbm, k_hbm, v_hbm, taps_hbm, rate_hbm, residue_hbm),
        (streams.at[0], streams.at[1], streams.at[2], taps_ref, rate_ref, residue_ref),
        sems,
    )
    sent = fetch(
        [weight_hbm.at[:, pl.ds(lax.rem(here + d, parts) * width, width)] for d in range(1, parts)],
        blocks,
        sems.at[pl.ds(6, parts - 1)],
    )
    for copy in copies:
        copy.wait()
    amp_ref[...] = residue_ref[...] * jnp.sqrt(one_minus_exp(2.0 * rate_ref[...]))
    for i in range(3):
        pad[i, pl.ds(0, HEAD), :] = jnp.zeros((HEAD, channels), F32)
        pad[i, pl.ds(HEAD, rows), :] = streams[i].astype(F32)
    block = 32
    for half in range(channels // LANES):
        lanes = pl.ds(half * LANES, LANES)
        for r in range(0, rows, block):
            sums = []
            for i in range(3):
                total = jnp.zeros((block, LANES), F32)
                for t in range(taps):
                    total = total + taps_ref[i, pl.ds(t, 1), lanes] * pad[i, pl.ds(HEAD + r - t, block), lanes]
                sums.append(total)
                if r == 0:
                    head_ref[i, :, lanes] = total[:HEAD]
            query_ref[half, pl.ds(r, block), :] = sums[0]
            gated_ref[half, pl.ds(r, block), :] = sums[1] * sums[2]
    sub = lax.broadcasted_iota(jnp.int32, (SUBS, LANES), 0)
    for half in range(channels // LANES):
        lanes = pl.ds(half * LANES, LANES)
        rates = [row_of(rate_ref, m, lanes) for m in range(modes)]
        retain = [wide(jnp.exp(-x)) for x in rates]
        state = [jnp.zeros((SUBS, LANES), F32) for _ in range(modes)]
        for step in range(steps):
            g = gated_ref[half, pl.ds(step, SUBS, stride=steps), :]
            state = [a * s + g for a, s in zip(retain, state)]
        for m in range(modes):
            s = state[m]
            for d in (1, 2, 4):
                drop = wide(jnp.exp(-(steps * d) * rates[m]))
                s = s + jnp.where(sub >= d, drop * pltpu.roll(s, d, 0), 0.0)
            state_ref[pl.ds(m, 1), lanes] = s[SUBS - 1 :]
            begin_ref[m, :, lanes] = jnp.where(sub >= 1, pltpu.roll(s, 1, 0), 0.0)
    for copy in sent:
        copy.wait()


def join_body(rows, rim_ref, head_ref, taps_ref, rate_ref, state_ref, out_ref, late_ref, top_ref, pad):
    modes, channels = rate_ref.shape
    taps = taps_ref.shape[1]
    sums = []
    for i in range(3):
        pad[i, pl.ds(0, HEAD), :] = rim_ref[pl.ds(i * RIM, RIM), :].astype(F32)[RIM - HEAD :]
        pad[i, pl.ds(HEAD, HEAD), :] = jnp.zeros((HEAD, channels), F32)
        total = head_ref[i]
        for t in range(1, taps):
            total = total + taps_ref[i, pl.ds(t, 1), :] * pad[i, pl.ds(HEAD - t, HEAD), :]
        sums.append(total)
    gated = sums[1] * sums[2]
    top_ref[0] = sums[0]
    top_ref[1] = gated
    more = gated - head_ref[1] * head_ref[2]
    rate = rate_ref[...]
    retain = jnp.exp(-rate)
    late = jnp.broadcast_to(more[:1], rate.shape)
    for i in range(1, taps - 1):
        late = retain * late + more[i : i + 1]
    late_ref[...] = late
    whole = (state_ref[...] + jnp.exp(-(rows - taps + 1) * rate) * late).astype(BF16)
    for i in range(out_ref.shape[0]):
        out_ref[i] = whole


def plane_body(rows, parts_ref, rate_ref, before_ref, total_ref):
    me = lax.axis_index("y") * lax.axis_size("core") + lax.axis_index("core")
    drop = jnp.exp(-rows * rate_ref[...])
    before = jnp.zeros(rate_ref.shape, F32)
    total = jnp.zeros(rate_ref.shape, F32)
    for i in range(parts_ref.shape[0]):
        part = parts_ref[i].astype(F32)
        before = jnp.where(i < me, before * drop + part, before)
        total = total * drop + part
    before_ref[...] = before
    for i in range(total_ref.shape[0]):
        total_ref[i] = total.astype(BF16)


def mix_body(
    taps, plane_rows, query_ref, gated_ref, begin_ref, late_ref, top_ref, before_ref, planes_ref, rate_ref, amp_ref,
    skip_hbm, out_ref, hyena, carry, skip_ref, sems,
):
    halves, rows, _ = query_ref.shape
    modes = rate_ref.shape[0]
    steps = rows // SUBS
    copies = fetch([skip_hbm], [skip_ref], sems)
    z = lax.axis_index("z")
    me = lax.axis_index("y") * lax.axis_size("core") + lax.axis_index("core")
    rate = rate_ref[...]
    drop = jnp.exp(-plane_rows * rate)
    behind = jnp.zeros(rate.shape, F32)
    for i in range(planes_ref.shape[0]):
        behind = jnp.where(i < z, behind * drop + planes_ref[i].astype(F32), behind)
    carried = before_ref[...] + jnp.exp(-(rows * me).astype(F32) * rate) * behind
    carry[0] = carried
    carry[1] = carried + jnp.exp((taps - 1) * rate) * late_ref[...]
    sub = lax.broadcasted_iota(jnp.int32, (SUBS, LANES), 0)
    ahead = sub.astype(F32) * float(steps)
    copies[0].wait()
    for half in range(halves):
        lanes = pl.ds(half * LANES, LANES)
        rates = [row_of(rate_ref, m, lanes) for m in range(modes)]
        retain = [wide(jnp.exp(-x)) for x in rates]
        amp = [wide(row_of(amp_ref, m, lanes)) for m in range(modes)]
        skip = wide(row_of(skip_ref, 0, lanes))
        state = [
            begin_ref[m, :, lanes]
            + jnp.exp(-ahead * rates[m])
            * jnp.where(sub >= 1, row_of(carry.at[1], m, lanes), row_of(carry.at[0], m, lanes))
            for m in range(modes)
        ]
        for step in range(steps):
            at = pl.ds(step, SUBS, stride=steps)
            g = gated_ref[half, at, :]
            query = query_ref[half, at, :]
            if step < taps - 1:
                query = jnp.where(sub >= 1, query, top_ref[0, pl.ds(step, 1), lanes])
                g = jnp.where(sub >= 1, g, top_ref[1, pl.ds(step, 1), lanes])
            state = [a * s + g for a, s in zip(retain, state)]
            terms = [a * s for a, s in zip(amp, state)] + [skip * g]
            while len(terms) > 1:
                terms = [x + y for x, y in zip(terms[::2], terms[1::2])] + terms[len(terms) // 2 * 2 :]
            hyena[half, at, :] = query * terms[0]
    left = jnp.concatenate([hyena[half].astype(BF16) for half in range(halves)], axis=1)
    for i in range(out_ref.shape[0]):
        out_ref[i] = left


def project_body(left_ref, weight_hbm, *rest):
    *others, out_ref, own, sem = rest
    parts, _, _ = left_ref.shape
    width = out_ref.shape[1]
    here = lax.axis_index("tp")
    copy = pltpu.make_async_copy(weight_hbm.at[:, pl.ds(here * width, width)], own, sem)
    copy.start()
    block = 512
    for c in range(0, width, block):
        at = pl.ds(c, block)
        total = jnp.zeros((out_ref.shape[0], block), F32)
        for d in range(1, parts):
            total += jnp.dot(
                left_ref[lax.rem(here + parts - d, parts)], others[d - 1][:, at], preferred_element_type=F32
            )
        if c == 0:
            copy.wait()
        total += jnp.dot(left_ref[here], own[:, at], preferred_element_type=F32)
        out_ref[:, at] = total.astype(BF16)


def local(query_in, key_in, value_in, short_weight, residue, rate, skip, out_weight):
    rows, channels = query_in.shape
    modes = rate.shape[0]
    taps = short_weight.shape[1]
    planes = lax.axis_size("z")
    plane = lax.axis_size("y") * lax.axis_size("core")
    parts = lax.axis_size("tp")
    width = out_weight.shape[1] // parts
    order = ("z", "y", "core")
    devices = planes * plane
    by_half = (channels // LANES, rows, LANES)
    skip = skip.reshape(1, -1)
    query_in, key_in, value_in, short_weight, residue, rate, skip, out_weight = (
        pltpu.with_memory_space_constraint(x, pltpu.HBM)
        for x in (query_in, key_in, value_in, short_weight, residue, rate, skip, out_weight)
    )
    rims = call(
        rim_body, [HBM] * 3, shape((3 * RIM, channels), BF16), "rims", [pltpu.SemaphoreType.DMA((3,))]
    )(query_in, key_in, value_in)
    rims = lax.ppermute(rims, order, [(i, i + 1) for i in range(devices - 1)])
    queries, gated, begin, states, heads, taps_here, rate, amplitude, *blocks = call(
        gate_body,
        [HBM] * 7,
        (
            shape(by_half, F32),
            shape(by_half, F32),
            shape((modes, SUBS, channels), F32),
            shape((modes, channels), F32),
            shape((3, HEAD, channels), F32),
            shape(short_weight.shape, F32),
            shape((modes, channels), F32),
            shape((modes, channels), F32),
            *[shape((channels, width), BF16)] * (parts - 1),
        ),
        "gate",
        [
            pltpu.VMEM((3, rows, channels), BF16),
            pltpu.VMEM((modes, channels), F32),
            pltpu.VMEM((3, HEAD + rows, channels), F32),
            pltpu.SemaphoreType.DMA((6 + parts - 1,)),
        ],
    )(query_in, key_in, value_in, short_weight, rate, residue, out_weight)
    blocks = [
        lax.ppermute(block, "tp", [(i, (i + d) % parts) for i in range(parts)])
        for d, block in enumerate(blocks, start=1)
    ]
    states, late, top = call(
        lambda *refs: join_body(rows, *refs),
        [VMEM] * 5,
        (
            shape((plane, modes, channels), BF16),
            shape((modes, channels), F32),
            shape((2, HEAD, channels), F32),
        ),
        "join",
        [pltpu.VMEM((3, 2 * HEAD, channels), F32)],
    )(rims, heads, taps_here, rate, states)
    states = lax.all_to_all(states, ("y", "core"), 0, 0, tiled=True)
    before, totals = call(
        lambda *refs: plane_body(rows, *refs),
        [VMEM] * 2,
        (shape((modes, channels), F32), shape((planes, modes, channels), BF16)),
        "plane",
    )(states, rate)
    totals = lax.all_to_all(totals, "z", 0, 0, tiled=True)
    hyena = call(
        lambda *refs: mix_body(taps, rows * plane, *refs),
        [VMEM] * 9 + [HBM],
        shape((parts, rows, channels), BF16),
        "mix",
        [
            pltpu.VMEM(by_half, F32),
            pltpu.VMEM((2, modes, channels), F32),
            pltpu.VMEM((1, channels), F32),
            pltpu.SemaphoreType.DMA((1,)),
        ],
    )(queries, gated, begin, late, top, before, totals, rate, amplitude, skip)
    hyena = lax.all_to_all(hyena, "tp", 0, 0, tiled=True)
    return call(
        project_body,
        [VMEM, HBM] + [VMEM] * (parts - 1),
        shape((rows, width), BF16),
        "project",
        [pltpu.VMEM((channels, width), BF16), pltpu.SemaphoreType.DMA],
    )(hyena, out_weight, *blocks)


def solution(mesh):
    fine = Mesh(mesh.devices.reshape(8, 8, 2, 4), ("z", "y", "core", "tp"))
    seq = ("z", "y", "core")
    in_specs = (
        P(seq, "tp"),
        P(seq, "tp"),
        P(seq, "tp"),
        P(None, None, "tp"),
        P(None, "tp"),
        P(None, "tp"),
        P("tp"),
        P("tp", None),
    )
    return jax.shard_map(local, mesh=fine, in_specs=in_specs, out_specs=P(seq, "tp"), check_vma=False)
```

```python
import jax
import jax.numpy as jnp
from jax import lax
from jax.experimental import pallas as pl
from jax.experimental.pallas import tpu as pltpu
from jax.sharding import Mesh, PartitionSpec as P

F32 = jnp.float32
BF16 = jnp.bfloat16
LANES = 128
SUBS = 8
RIM = 16
HEAD = 8
MIB = 1 << 20


def shape(dims, dtype):
    return jax.ShapeDtypeStruct(dims, dtype)


VMEM = pl.BlockSpec(memory_space=pltpu.VMEM)
HBM = pl.BlockSpec(memory_space=pltpu.HBM)


def call(body, specs, outs, name, scratch=(), mib=4, out_spec=VMEM):
    return pl.pallas_call(
        body,
        in_specs=specs,
        out_specs=jax.tree.map(lambda _: out_spec, outs),
        out_shape=outs,
        scratch_shapes=list(scratch),
        compiler_params=pltpu.CompilerParams(vmem_limit_bytes=mib * MIB),
        name=name,
    )


def fetch(sources, targets, sems):
    copies = [pltpu.make_async_copy(s, t, sems.at[i]) for i, (s, t) in enumerate(zip(sources, targets))]
    for copy in copies:
        copy.start()
    return copies


def row_of(ref, m, lanes):
    return ref[pl.ds(m, 1), lanes]


def wide(row):
    return jnp.broadcast_to(row, (SUBS, LANES))


def one_minus_exp(x):
    series = 1.0 / 362880.0
    for n in (40320, 5040, 720, 120, 24, 6, 2, 1):
        series = 1.0 / n - x * series
    return jnp.where(x < 0.25, x * series, 1.0 - jnp.exp(-x))


def rim_body(q_ref, k_ref, v_ref, out_ref, sems):
    rows = q_ref.shape[0]
    refs = (q_ref, k_ref, v_ref)
    copies = fetch(
        [ref.at[pl.ds(rows - RIM, RIM), :] for ref in refs],
        [out_ref.at[pl.ds(i * RIM, RIM), :] for i in range(3)],
        sems,
    )
    for copy in copies:
        copy.wait()


def gate_body(
    q_hbm, k_hbm, v_hbm, taps_hbm, rate_hbm, residue_hbm,
    query_ref, gated_ref, begin_ref, state_ref, head_ref, taps_ref, rate_ref, amp_ref,
    streams, residue_ref, pad, sems,
):
    _, rows, channels = streams.shape
    modes = rate_ref.shape[0]
    taps = taps_ref.shape[1]
    steps = rows // SUBS
    copies = fetch(
        (q_hbm, k_hbm, v_hbm, taps_hbm, rate_hbm, residue_hbm),
        (streams.at[0], streams.at[1], streams.at[2], taps_ref, rate_ref, residue_ref),
        sems,
    )
    for copy in copies:
        copy.wait()
    amp_ref[...] = residue_ref[...] * jnp.sqrt(one_minus_exp(2.0 * rate_ref[...]))
    for i in range(3):
        pad[i, pl.ds(0, HEAD), :] = jnp.zeros((HEAD, channels), F32)
        pad[i, pl.ds(HEAD, rows), :] = streams[i].astype(F32)
    block = 32
    for half in range(channels // LANES):
        lanes = pl.ds(half * LANES, LANES)
        for r in range(0, rows, block):
            sums = []
            for i in range(3):
                total = jnp.zeros((block, LANES), F32)
                for t in range(taps):
                    total = total + taps_ref[i, pl.ds(t, 1), lanes] * pad[i, pl.ds(HEAD + r - t, block), lanes]
                sums.append(total)
                if r == 0:
                    head_ref[i, :, lanes] = total[:HEAD]
            query_ref[half, pl.ds(r, block), :] = sums[0]
            gated_ref[half, pl.ds(r, block), :] = sums[1] * sums[2]
    sub = lax.broadcasted_iota(jnp.int32, (SUBS, LANES), 0)
    for half in range(channels // LANES):
        lanes = pl.ds(half * LANES, LANES)
        rates = [row_of(rate_ref, m, lanes) for m in range(modes)]
        retain = [wide(jnp.exp(-x)) for x in rates]
        state = [jnp.zeros((SUBS, LANES), F32) for _ in range(modes)]
        for step in range(steps):
            g = gated_ref[half, pl.ds(step, SUBS, stride=steps), :]
            state = [a * s + g for a, s in zip(retain, state)]
        for m in range(modes):
            s = state[m]
            for d in (1, 2, 4):
                drop = wide(jnp.exp(-(steps * d) * rates[m]))
                s = s + jnp.where(sub >= d, drop * pltpu.roll(s, d, 0), 0.0)
            state_ref[pl.ds(m, 1), lanes] = s[SUBS - 1 :]
            begin_ref[m, :, lanes] = jnp.where(sub >= 1, pltpu.roll(s, 1, 0), 0.0)

def join_body(
    rows, rim_ref, head_ref, taps_ref, rate_ref, state_ref, weight_hbm, out_ref, late_ref, top_ref, *rest
):
    *blocks, pad, sems = rest
    here, parts = lax.axis_index("tp"), lax.axis_size("tp")
    width = blocks[0].shape[1]
    core = lax.axis_index("core")
    height = blocks[1].shape[0]
    side = lax.rem(here + jnp.where(core == 0, 1, parts - 1), parts)
    across = lax.rem(here + 2, parts)
    sent = fetch(
        (
            weight_hbm.at[:, pl.ds(pl.multiple_of(side * width, LANES), width)],
            weight_hbm.at[
                pl.ds(pl.multiple_of(core * height, height), height),
                pl.ds(pl.multiple_of(across * width, LANES), width),
            ],
        ),
        blocks,
        sems,
    )
    modes, channels = rate_ref.shape
    taps = taps_ref.shape[1]
    sums = []
    for i in range(3):
        pad[i, pl.ds(0, HEAD), :] = rim_ref[pl.ds(i * RIM, RIM), :].astype(F32)[RIM - HEAD :]
        pad[i, pl.ds(HEAD, HEAD), :] = jnp.zeros((HEAD, channels), F32)
        total = head_ref[i]
        for t in range(1, taps):
            total = total + taps_ref[i, pl.ds(t, 1), :] * pad[i, pl.ds(HEAD - t, HEAD), :]
        sums.append(total)
    gated = sums[1] * sums[2]
    top_ref[0] = sums[0]
    top_ref[1] = gated
    more = gated - head_ref[1] * head_ref[2]
    rate = rate_ref[...]
    retain = jnp.exp(-rate)
    late = jnp.broadcast_to(more[:1], rate.shape)
    for i in range(1, taps - 1):
        late = retain * late + more[i : i + 1]
    late_ref[...] = late
    whole = (state_ref[...] + jnp.exp(-(rows - taps + 1) * rate) * late).astype(BF16)
    for i in range(out_ref.shape[0]):
        out_ref[i] = whole
    for copy in sent:
        copy.wait()


def plane_body(rows, parts_ref, rate_ref, before_ref, total_ref):
    me = lax.axis_index("y") * lax.axis_size("core") + lax.axis_index("core")
    drop = jnp.exp(-rows * rate_ref[...])
    before = jnp.zeros(rate_ref.shape, F32)
    total = jnp.zeros(rate_ref.shape, F32)
    for i in range(parts_ref.shape[0]):
        part = parts_ref[i].astype(F32)
        before = jnp.where(i < me, before * drop + part, before)
        total = total * drop + part
    before_ref[...] = before
    for i in range(total_ref.shape[0]):
        total_ref[i] = total.astype(BF16)


def mix_body(
    taps, plane_rows, query_ref, gated_ref, begin_ref, late_ref, top_ref, before_ref, planes_ref, rate_ref, amp_ref,
    skip_hbm, out_ref, hyena, carry, skip_ref, sems,
):
    halves, rows, _ = query_ref.shape
    modes = rate_ref.shape[0]
    steps = rows // SUBS
    copies = fetch([skip_hbm], [skip_ref], sems)
    z = lax.axis_index("z")
    me = lax.axis_index("y") * lax.axis_size("core") + lax.axis_index("core")
    rate = rate_ref[...]
    drop = jnp.exp(-plane_rows * rate)
    behind = jnp.zeros(rate.shape, F32)
    for i in range(planes_ref.shape[0]):
        behind = jnp.where(i < z, behind * drop + planes_ref[i].astype(F32), behind)
    carried = before_ref[...] + jnp.exp(-(rows * me).astype(F32) * rate) * behind
    carry[0] = carried
    carry[1] = carried + jnp.exp((taps - 1) * rate) * late_ref[...]
    sub = lax.broadcasted_iota(jnp.int32, (SUBS, LANES), 0)
    ahead = sub.astype(F32) * float(steps)
    copies[0].wait()
    for half in range(halves):
        lanes = pl.ds(half * LANES, LANES)
        rates = [row_of(rate_ref, m, lanes) for m in range(modes)]
        retain = [wide(jnp.exp(-x)) for x in rates]
        amp = [wide(row_of(amp_ref, m, lanes)) for m in range(modes)]
        skip = wide(row_of(skip_ref, 0, lanes))
        state = [
            begin_ref[m, :, lanes]
            + jnp.exp(-ahead * rates[m])
            * jnp.where(sub >= 1, row_of(carry.at[1], m, lanes), row_of(carry.at[0], m, lanes))
            for m in range(modes)
        ]
        for step in range(steps):
            at = pl.ds(step, SUBS, stride=steps)
            g = gated_ref[half, at, :]
            query = query_ref[half, at, :]
            if step < taps - 1:
                query = jnp.where(sub >= 1, query, top_ref[0, pl.ds(step, 1), lanes])
                g = jnp.where(sub >= 1, g, top_ref[1, pl.ds(step, 1), lanes])
            state = [a * s + g for a, s in zip(retain, state)]
            terms = [a * s for a, s in zip(amp, state)] + [skip * g]
            while len(terms) > 1:
                terms = [x + y for x, y in zip(terms[::2], terms[1::2])] + terms[len(terms) // 2 * 2 :]
            hyena[half, at, :] = query * terms[0]
    left = jnp.concatenate([hyena[half].astype(BF16) for half in range(halves)], axis=1)
    for i in range(out_ref.shape[0]):
        out_ref[i] = left


def project_body(left_ref, weight_hbm, side_ref, half_ref, swap_side_ref, swap_half_ref, out_hbm, own, done, sems):
    parts = left_ref.shape[0]
    here = lax.axis_index("tp")
    core = lax.axis_index("core")
    blocks, _, block = done.shape
    width = own.shape[1]
    height = half_ref.shape[0]
    fetched = pltpu.make_async_copy(weight_hbm.at[:, pl.ds(here * width, width)], own, sems.at[blocks])
    fetched.start()
    behind, ahead = lax.rem(here + parts - 1, parts), lax.rem(here + 1, parts)
    across = lax.rem(here + 2, parts)
    mine = pl.ds(pl.multiple_of(core * height, height), height)
    mates = pl.ds(pl.multiple_of((1 - core) * height, height), height)
    pairs = [
        (left_ref[jnp.where(core == 0, behind, ahead)], side_ref),
        (left_ref[jnp.where(core == 0, ahead, behind)], swap_side_ref),
        (left_ref[across, :, mine], half_ref),
        (left_ref[across, :, mates], swap_half_ref),
        (left_ref[here], own),
    ]
    copies = []
    for b in range(blocks):
        at = pl.ds(b * block, block)
        total = jnp.zeros(done.shape[1:], F32)
        for left, right in pairs:
            if b == 0 and right is own:
                fetched.wait()
            total += jnp.dot(left, right[:, at], preferred_element_type=F32)
        done[b] = total.astype(BF16)
        copies.append(pltpu.make_async_copy(done.at[b], out_hbm.at[:, at], sems.at[b]))
        copies[-1].start()
    for copy in copies:
        copy.wait()


def local(query_in, key_in, value_in, short_weight, residue, rate, skip, out_weight):
    rows, channels = query_in.shape
    modes = rate.shape[0]
    taps = short_weight.shape[1]
    planes = lax.axis_size("z")
    plane = lax.axis_size("y") * lax.axis_size("core")
    parts = lax.axis_size("tp")
    width = out_weight.shape[1] // parts
    order = ("z", "y", "core")
    devices = planes * plane
    by_half = (channels // LANES, rows, LANES)
    skip = skip.reshape(1, -1)
    query_in, key_in, value_in, short_weight, residue, rate, skip, out_weight = (
        pltpu.with_memory_space_constraint(x, pltpu.HBM)
        for x in (query_in, key_in, value_in, short_weight, residue, rate, skip, out_weight)
    )
    rims = call(
        rim_body, [HBM] * 3, shape((3 * RIM, channels), BF16), "rims", [pltpu.SemaphoreType.DMA((3,))]
    )(query_in, key_in, value_in)
    rims = lax.ppermute(rims, order, [(i, i + 1) for i in range(devices - 1)])
    queries, gated, begin, states, heads, taps_here, rate, amplitude = call(
        gate_body,
        [HBM] * 6,
        (
            shape(by_half, F32),
            shape(by_half, F32),
            shape((modes, SUBS, channels), F32),
            shape((modes, channels), F32),
            shape((3, HEAD, channels), F32),
            shape(short_weight.shape, F32),
            shape((modes, channels), F32),
            shape((modes, channels), F32),
        ),
        "gate",
        [
            pltpu.VMEM((3, rows, channels), BF16),
            pltpu.VMEM((modes, channels), F32),
            pltpu.VMEM((3, HEAD + rows, channels), F32),
            pltpu.SemaphoreType.DMA((6,)),
        ],
    )(query_in, key_in, value_in, short_weight, rate, residue)
    states, late, top, *blocks = call(
        lambda *refs: join_body(rows, *refs),
        [VMEM] * 5 + [HBM],
        (
            shape((plane, modes, channels), BF16),
            shape((modes, channels), F32),
            shape((2, HEAD, channels), F32),
            shape((channels, width), BF16),
            shape((channels // 2, width), BF16),
        ),
        "join",
        [pltpu.VMEM((3, 2 * HEAD, channels), F32), pltpu.SemaphoreType.DMA((2,))],
    )(rims, heads, taps_here, rate, states, out_weight)
    side, half = blocks
    cores = lax.axis_size("core")
    places = [(c, t) for c in range(cores) for t in range(parts)]
    side = lax.ppermute(
        side, ("core", "tp"), [(c * parts + t, c * parts + (t + (1 if c == 0 else -1)) % parts) for c, t in places]
    )
    half = lax.ppermute(half, "tp", [(t, (t + 2) % parts) for t in range(parts)])
    swapped = [lax.ppermute(x, "core", [(c, cores - 1 - c) for c in range(cores)]) for x in (side, half)]
    states = lax.all_to_all(states, ("y", "core"), 0, 0, tiled=True)
    before, totals = call(
        lambda *refs: plane_body(rows, *refs),
        [VMEM] * 2,
        (shape((modes, channels), F32), shape((planes, modes, channels), BF16)),
        "plane",
    )(states, rate)
    totals = lax.all_to_all(totals, "z", 0, 0, tiled=True)
    hyena = call(
        lambda *refs: mix_body(taps, rows * plane, *refs),
        [VMEM] * 9 + [HBM],
        shape((parts, rows, channels), BF16),
        "mix",
        [
            pltpu.VMEM(by_half, F32),
            pltpu.VMEM((2, modes, channels), F32),
            pltpu.VMEM((1, channels), F32),
            pltpu.SemaphoreType.DMA((1,)),
        ],
    )(queries, gated, begin, late, top, before, totals, rate, amplitude, skip)
    hyena = lax.all_to_all(hyena, "tp", 0, 0, tiled=True)
    block = 256
    return call(
        project_body,
        [VMEM, HBM] + [VMEM] * 4,
        shape((rows, width), BF16),
        "project",
        [
            pltpu.VMEM((channels, width), BF16),
            pltpu.VMEM((width // block, rows, block), BF16),
            pltpu.SemaphoreType.DMA((width // block + 1,)),
        ],
        out_spec=HBM,
    )(hyena, out_weight, side, half, *swapped)


def solution(mesh):
    fine = Mesh(mesh.devices.reshape(8, 8, 2, 4), ("z", "y", "core", "tp"))
    seq = ("z", "y", "core")
    in_specs = (
        P(seq, "tp"),
        P(seq, "tp"),
        P(seq, "tp"),
        P(None, None, "tp"),
        P(None, "tp"),
        P(None, "tp"),
        P("tp"),
        P("tp", None),
    )
    return jax.shard_map(local, mesh=fine, in_specs=in_specs, out_specs=P(seq, "tp"), check_vma=False)
```

```python
import jax
import jax.numpy as jnp
from jax import lax
from jax.experimental import pallas as pl
from jax.experimental.pallas import tpu as pltpu
from jax.sharding import Mesh, PartitionSpec as P

F32 = jnp.float32
BF16 = jnp.bfloat16
LANES = 128
SUBS = 8
RIM = 16
HEAD = 8
MIB = 1 << 20


def shape(dims, dtype):
    return jax.ShapeDtypeStruct(dims, dtype)


VMEM = pl.BlockSpec(memory_space=pltpu.VMEM)
ANY = pl.BlockSpec(memory_space=pl.ANY)
HBM = pl.BlockSpec(memory_space=pltpu.HBM)


def call(body, specs, outs, name, scratch=(), mib=4, out_spec=VMEM, aliases=None):
    return pl.pallas_call(
        body,
        in_specs=specs,
        out_specs=out_spec if isinstance(out_spec, tuple) else jax.tree.map(lambda _: out_spec, outs),
        input_output_aliases=aliases or {},
        out_shape=outs,
        scratch_shapes=list(scratch),
        compiler_params=pltpu.CompilerParams(vmem_limit_bytes=mib * MIB),
        name=name,
    )


def fetch(sources, targets, sems):
    copies = [pltpu.make_async_copy(s, t, sems.at[i]) for i, (s, t) in enumerate(zip(sources, targets))]
    for copy in copies:
        copy.start()
    return copies


def row_of(ref, m, lanes):
    return ref[pl.ds(m, 1), lanes]


def wide(row):
    return jnp.broadcast_to(row, (SUBS, LANES))


def one_minus_exp(x):
    series = 1.0 / 362880.0
    for n in (40320, 5040, 720, 120, 24, 6, 2, 1):
        series = 1.0 / n - x * series
    return jnp.where(x < 0.25, x * series, 1.0 - jnp.exp(-x))


def rim_body(q_ref, k_ref, v_ref, out_ref, sems):
    rows = q_ref.shape[0]
    refs = (q_ref, k_ref, v_ref)
    copies = fetch(
        [ref.at[pl.ds(rows - RIM, RIM), :] for ref in refs],
        [out_ref.at[pl.ds(i * RIM, RIM), :] for i in range(3)],
        sems,
    )
    for copy in copies:
        copy.wait()


def gate_body(
    q_hbm, k_hbm, v_hbm, taps_hbm, rate_hbm, residue_hbm, skip_hbm, weight_hbm,
    query_ref, gated_ref, begin_ref, state_ref, head_ref, taps_ref, rate_ref, amp_ref, skip_ref, *rest,
):
    *blocks, streams, residue_ref, pad, sems = rest
    here, parts = lax.axis_index("tp"), lax.axis_size("tp")
    width = blocks[0].shape[1]
    _, rows, channels = streams.shape
    modes = rate_ref.shape[0]
    taps = taps_ref.shape[1]
    steps = rows // SUBS
    copies = fetch(
        (q_hbm, k_hbm, v_hbm, taps_hbm, rate_hbm, residue_hbm, skip_hbm),
        (streams.at[0], streams.at[1], streams.at[2], taps_ref, rate_ref, residue_ref, skip_ref),
        sems,
    )
    sent = fetch(
        [weight_hbm.at[:, pl.ds(lax.rem(here + d, parts) * width, width)] for d in range(1, parts)],
        blocks,
        sems.at[pl.ds(7, parts - 1)],
    )
    for copy in copies:
        copy.wait()
    amp_ref[...] = residue_ref[...] * jnp.sqrt(one_minus_exp(2.0 * rate_ref[...]))
    for i in range(3):
        pad[i, pl.ds(0, HEAD), :] = jnp.zeros((HEAD, channels), F32)
        pad[i, pl.ds(HEAD, rows), :] = streams[i].astype(F32)
    block = 32
    for half in range(channels // LANES):
        lanes = pl.ds(half * LANES, LANES)
        for r in range(0, rows, block):
            sums = []
            for i in range(3):
                total = jnp.zeros((block, LANES), F32)
                for t in range(taps):
                    total = total + taps_ref[i, pl.ds(t, 1), lanes] * pad[i, pl.ds(HEAD + r - t, block), lanes]
                sums.append(total)
                if r == 0:
                    head_ref[i, :, lanes] = total[:HEAD]
            query_ref[half, pl.ds(r, block), :] = sums[0]
            gated_ref[half, pl.ds(r, block), :] = sums[1] * sums[2]
    sub = lax.broadcasted_iota(jnp.int32, (SUBS, LANES), 0)
    for half in range(channels // LANES):
        lanes = pl.ds(half * LANES, LANES)
        rates = [row_of(rate_ref, m, lanes) for m in range(modes)]
        retain = [wide(jnp.exp(-x)) for x in rates]
        state = [jnp.zeros((SUBS, LANES), F32) for _ in range(modes)]
        for step in range(steps):
            g = gated_ref[half, pl.ds(step, SUBS, stride=steps), :]
            state = [a * s + g for a, s in zip(retain, state)]
        for m in range(modes):
            s = state[m]
            for d in (1, 2, 4):
                drop = wide(jnp.exp(-(steps * d) * rates[m]))
                s = s + jnp.where(sub >= d, drop * pltpu.roll(s, d, 0), 0.0)
            state_ref[pl.ds(m, 1), lanes] = s[SUBS - 1 :]
            begin_ref[m, :, lanes] = jnp.where(sub >= 1, pltpu.roll(s, 1, 0), 0.0)
    for copy in sent:
        copy.wait()


def join_body(rows, rim_ref, head_ref, taps_ref, rate_ref, state_ref, out_ref, late_ref, top_ref, pad):
    modes, channels = rate_ref.shape
    taps = taps_ref.shape[1]
    sums = []
    for i in range(3):
        pad[i, pl.ds(0, HEAD), :] = rim_ref[pl.ds(i * RIM, RIM), :].astype(F32)[RIM - HEAD :]
        pad[i, pl.ds(HEAD, HEAD), :] = jnp.zeros((HEAD, channels), F32)
        total = head_ref[i]
        for t in range(1, taps):
            total = total + taps_ref[i, pl.ds(t, 1), :] * pad[i, pl.ds(HEAD - t, HEAD), :]
        sums.append(total)
    gated = sums[1] * sums[2]
    top_ref[0] = sums[0]
    top_ref[1] = gated
    more = gated - head_ref[1] * head_ref[2]
    rate = rate_ref[...]
    retain = jnp.exp(-rate)
    late = jnp.broadcast_to(more[:1], rate.shape)
    for i in range(1, taps - 1):
        late = retain * late + more[i : i + 1]
    late_ref[...] = late
    whole = (state_ref[...] + jnp.exp(-(rows - taps + 1) * rate) * late).astype(BF16)
    for i in range(out_ref.shape[0]):
        out_ref[i] = whole


def plane_body(rows, parts_ref, rate_ref, before_ref, total_ref):
    me = lax.axis_index("y") * lax.axis_size("core") + lax.axis_index("core")
    drop = jnp.exp(-rows * rate_ref[...])
    before = jnp.zeros(rate_ref.shape, F32)
    total = jnp.zeros(rate_ref.shape, F32)
    for i in range(parts_ref.shape[0]):
        part = parts_ref[i].astype(F32)
        before = jnp.where(i < me, before * drop + part, before)
        total = total * drop + part
    before_ref[...] = before
    for i in range(total_ref.shape[0]):
        total_ref[i] = total.astype(BF16)


def mix_body(
    taps, plane_rows, query_ref, gated_ref, begin_ref, late_ref, top_ref, before_ref, planes_ref, rate_ref, amp_ref,
    skip_ref, weight_hbm, out_ref, own_ref, hyena, carry, sem,
):
    halves, rows, _ = query_ref.shape
    modes = rate_ref.shape[0]
    steps = rows // SUBS
    width = own_ref.shape[1]
    own = pltpu.make_async_copy(weight_hbm.at[:, pl.ds(lax.axis_index("tp") * width, width)], own_ref, sem)
    own.start()
    z = lax.axis_index("z")
    me = lax.axis_index("y") * lax.axis_size("core") + lax.axis_index("core")
    rate = rate_ref[...]
    drop = jnp.exp(-plane_rows * rate)
    behind = jnp.zeros(rate.shape, F32)
    for i in range(planes_ref.shape[0]):
        behind = jnp.where(i < z, behind * drop + planes_ref[i].astype(F32), behind)
    carried = before_ref[...] + jnp.exp(-(rows * me).astype(F32) * rate) * behind
    carry[0] = carried
    carry[1] = carried + jnp.exp((taps - 1) * rate) * late_ref[...]
    sub = lax.broadcasted_iota(jnp.int32, (SUBS, LANES), 0)
    ahead = sub.astype(F32) * float(steps)
    for half in range(halves):
        lanes = pl.ds(half * LANES, LANES)
        rates = [row_of(rate_ref, m, lanes) for m in range(modes)]
        retain = [wide(jnp.exp(-x)) for x in rates]
        amp = [wide(row_of(amp_ref, m, lanes)) for m in range(modes)]
        skip = wide(row_of(skip_ref, 0, lanes))
        state = [
            begin_ref[m, :, lanes]
            + jnp.exp(-ahead * rates[m])
            * jnp.where(sub >= 1, row_of(carry.at[1], m, lanes), row_of(carry.at[0], m, lanes))
            for m in range(modes)
        ]
        for step in range(steps):
            at = pl.ds(step, SUBS, stride=steps)
            g = gated_ref[half, at, :]
            query = query_ref[half, at, :]
            if step < taps - 1:
                query = jnp.where(sub >= 1, query, top_ref[0, pl.ds(step, 1), lanes])
                g = jnp.where(sub >= 1, g, top_ref[1, pl.ds(step, 1), lanes])
            state = [a * s + g for a, s in zip(retain, state)]
            terms = [a * s for a, s in zip(amp, state)] + [skip * g]
            while len(terms) > 1:
                terms = [x + y for x, y in zip(terms[::2], terms[1::2])] + terms[len(terms) // 2 * 2 :]
            hyena[half, at, :] = query * terms[0]
    left = jnp.concatenate([hyena[half].astype(BF16) for half in range(halves)], axis=1)
    for i in range(out_ref.shape[0]):
        out_ref[i] = left
    own.wait()


def project_body(left_ref, own_ref, *rest):
    *others, out_hbm, done, sems = rest
    parts = left_ref.shape[0]
    here = lax.axis_index("tp")
    blocks, _, block = done.shape
    copies = []
    for b in range(blocks):
        at = pl.ds(b * block, block)
        total = jnp.dot(left_ref[here], own_ref[:, at], preferred_element_type=F32)
        for d in range(1, parts):
            total += jnp.dot(
                left_ref[lax.rem(here + parts - d, parts)], others[d - 1][:, at], preferred_element_type=F32
            )
        done[b] = total.astype(BF16)
        copies.append(pltpu.make_async_copy(done.at[b], out_hbm.at[:, at], sems.at[b]))
        copies[-1].start()
    for copy in copies:
        copy.wait()


def local(query_in, key_in, value_in, short_weight, residue, rate, skip, out_weight):
    rows, channels = query_in.shape
    modes = rate.shape[0]
    taps = short_weight.shape[1]
    planes = lax.axis_size("z")
    plane = lax.axis_size("y") * lax.axis_size("core")
    parts = lax.axis_size("tp")
    width = out_weight.shape[1] // parts
    order = ("z", "y", "core")
    devices = planes * plane
    by_half = (channels // LANES, rows, LANES)
    skip = skip.reshape(1, -1)
    query_in, key_in, value_in, short_weight, residue, rate, skip, out_weight = (
        pltpu.with_memory_space_constraint(x, pltpu.HBM)
        for x in (query_in, key_in, value_in, short_weight, residue, rate, skip, out_weight)
    )
    rims = call(
        rim_body, [HBM] * 3, shape((3 * RIM, channels), BF16), "rims", [pltpu.SemaphoreType.DMA((3,))]
    )(query_in, key_in, value_in)
    rims = lax.ppermute(rims, order, [(i, i + 1) for i in range(devices - 1)])
    queries, gated, begin, states, heads, taps_here, rate, amplitude, skip, *blocks = call(
        gate_body,
        [HBM] * 8,
        (
            shape(by_half, F32),
            shape(by_half, F32),
            shape((modes, SUBS, channels), F32),
            shape((modes, channels), F32),
            shape((3, HEAD, channels), F32),
            shape(short_weight.shape, F32),
            shape((modes, channels), F32),
            shape((modes, channels), F32),
            shape((1, channels), F32),
            *[shape((channels, width), BF16)] * (parts - 1),
        ),
        "gate",
        [
            pltpu.VMEM((3, rows, channels), BF16),
            pltpu.VMEM((modes, channels), F32),
            pltpu.VMEM((3, HEAD + rows, channels), F32),
            pltpu.SemaphoreType.DMA((7 + parts - 1,)),
        ],
    )(query_in, key_in, value_in, short_weight, rate, residue, skip, out_weight)
    blocks = [
        lax.ppermute(block, "tp", [(i, (i + d) % parts) for i in range(parts)])
        for d, block in enumerate(blocks, start=1)
    ]
    states, late, top = call(
        lambda *refs: join_body(rows, *refs),
        [VMEM] * 5,
        (
            shape((plane, modes, channels), BF16),
            shape((modes, channels), F32),
            shape((2, HEAD, channels), F32),
        ),
        "join",
        [pltpu.VMEM((3, 2 * HEAD, channels), F32)],
    )(rims, heads, taps_here, rate, states)
    states = lax.all_to_all(states, ("y", "core"), 0, 0, tiled=True)
    before, totals = call(
        lambda *refs: plane_body(rows, *refs),
        [VMEM] * 2,
        (shape((modes, channels), F32), shape((planes, modes, channels), BF16)),
        "plane",
    )(states, rate)
    totals = lax.all_to_all(totals, "z", 0, 0, tiled=True)
    hyena, own = call(
        lambda *refs: mix_body(taps, rows * plane, *refs),
        [VMEM] * 10 + [HBM],
        (shape((parts, rows, channels), BF16), shape((channels, width), BF16)),
        "mix",
        [
            pltpu.VMEM(by_half, F32),
            pltpu.VMEM((2, modes, channels), F32),
            pltpu.SemaphoreType.DMA,
        ],
    )(queries, gated, begin, late, top, before, totals, rate, amplitude, skip, out_weight)
    hyena = lax.all_to_all(hyena, "tp", 0, 0, tiled=True)
    block = 256
    return call(
        project_body,
        [VMEM] * (2 + len(blocks)),
        shape((rows, width), BF16),
        "project",
        [pltpu.VMEM((width // block, rows, block), BF16), pltpu.SemaphoreType.DMA((width // block,))],
        out_spec=HBM,
    )(hyena, own, *blocks)


def solution(mesh):
    fine = Mesh(mesh.devices.reshape(8, 8, 2, 4), ("z", "y", "core", "tp"))
    seq = ("z", "y", "core")
    in_specs = (
        P(seq, "tp"),
        P(seq, "tp"),
        P(seq, "tp"),
        P(None, None, "tp"),
        P(None, "tp"),
        P(None, "tp"),
        P("tp"),
        P("tp", None),
    )
    return jax.shard_map(local, mesh=fine, in_specs=in_specs, out_specs=P(seq, "tp"), check_vma=False)
```

```python
import jax
import jax.numpy as jnp
from jax import lax
from jax.experimental import pallas as pl
from jax.experimental.pallas import tpu as pltpu
from jax.sharding import Mesh, PartitionSpec as P

F32 = jnp.float32
BF16 = jnp.bfloat16
LANES = 128
SUBS = 8
RIM = 16
HEAD = 8
MIB = 1 << 20
RATE = 1.15e9
EARLY = 3


def shape(dims, dtype):
    return jax.ShapeDtypeStruct(dims, dtype)


VMEM = pl.BlockSpec(memory_space=pltpu.VMEM)
ANY = pl.BlockSpec(memory_space=pl.ANY)
HBM = pl.BlockSpec(memory_space=pltpu.HBM)


def call(body, specs, outs, name, scratch=(), mib=4, out_spec=VMEM, aliases=None, us=0):
    return pl.pallas_call(
        body,
        in_specs=specs,
        out_specs=out_spec if isinstance(out_spec, tuple) else jax.tree.map(lambda _: out_spec, outs),
        input_output_aliases=aliases or {},
        cost_estimate=pl.CostEstimate(flops=int(us * RATE), bytes_accessed=0, transcendentals=0) if us else None,
        out_shape=outs,
        scratch_shapes=list(scratch),
        compiler_params=pltpu.CompilerParams(vmem_limit_bytes=mib * MIB),
        name=name,
    )


def fetch(sources, targets, sems):
    copies = [pltpu.make_async_copy(s, t, sems.at[i]) for i, (s, t) in enumerate(zip(sources, targets))]
    for copy in copies:
        copy.start()
    return copies


def row_of(ref, m, lanes):
    return ref[pl.ds(m, 1), lanes]


def wide(row):
    return jnp.broadcast_to(row, (SUBS, LANES))


def one_minus_exp(x):
    series = 1.0 / 362880.0
    for n in (40320, 5040, 720, 120, 24, 6, 2, 1):
        series = 1.0 / n - x * series
    return jnp.where(x < 0.25, x * series, 1.0 - jnp.exp(-x))


def rim_body(q_ref, k_ref, v_ref, out_ref, sems):
    rows = q_ref.shape[0]
    refs = (q_ref, k_ref, v_ref)
    copies = fetch(
        [ref.at[pl.ds(rows - RIM, RIM), :] for ref in refs],
        [out_ref.at[pl.ds(i * RIM, RIM), :] for i in range(3)],
        sems,
    )
    for copy in copies:
        copy.wait()


def gate_body(
    q_hbm, k_hbm, v_hbm, taps_hbm, rate_hbm, residue_hbm, skip_hbm, weight_hbm,
    query_ref, gated_ref, begin_ref, state_ref, head_ref, taps_ref, rate_ref, amp_ref, skip_ref, *rest,
):
    *blocks, streams, residue_ref, pad, sems = rest
    here, parts = lax.axis_index("tp"), lax.axis_size("tp")
    width = blocks[0].shape[1]
    _, rows, channels = streams.shape
    modes = rate_ref.shape[0]
    taps = taps_ref.shape[1]
    steps = rows // SUBS
    copies = fetch(
        (q_hbm, k_hbm, v_hbm, taps_hbm, rate_hbm, residue_hbm, skip_hbm),
        (streams.at[0], streams.at[1], streams.at[2], taps_ref, rate_ref, residue_ref, skip_ref),
        sems,
    )
    is_early = lax.axis_index("z") < EARLY
    views = [weight_hbm.at[:, pl.ds(lax.rem(here + d, parts) * width, width)] for d in range(1, parts)]
    height = blocks[1].shape[0]
    mine = pl.ds(pl.multiple_of(lax.axis_index("core") * height, height), height)
    across = pltpu.make_async_copy(
        weight_hbm.at[mine, pl.ds(lax.rem(here + 2, parts) * width, width)], blocks[1], sems.at[7]
    )
    across.start()

    def sides(targets):
        return [pltpu.make_async_copy(v, t, sems.at[8 + i]) for i, (v, t) in enumerate(zip(views[::2], targets))]

    @pl.when(is_early)
    def _():
        for copy in sides((blocks[0], blocks[2])):
            copy.start()

    @pl.when(jnp.logical_not(is_early))
    def _():
        for copy in sides((blocks[3], blocks[4])):
            copy.start()

    for copy in copies:
        copy.wait()
    amp_ref[...] = residue_ref[...] * jnp.sqrt(one_minus_exp(2.0 * rate_ref[...]))
    for i in range(3):
        pad[i, pl.ds(0, HEAD), :] = jnp.zeros((HEAD, channels), F32)
        pad[i, pl.ds(HEAD, rows), :] = streams[i].astype(F32)
    block = 32
    for half in range(channels // LANES):
        lanes = pl.ds(half * LANES, LANES)
        for r in range(0, rows, block):
            sums = []
            for i in range(3):
                total = jnp.zeros((block, LANES), F32)
                for t in range(taps):
                    total = total + taps_ref[i, pl.ds(t, 1), lanes] * pad[i, pl.ds(HEAD + r - t, block), lanes]
                sums.append(total)
                if r == 0:
                    head_ref[i, :, lanes] = total[:HEAD]
            query_ref[half, pl.ds(r, block), :] = sums[0]
            gated_ref[half, pl.ds(r, block), :] = sums[1] * sums[2]
    sub = lax.broadcasted_iota(jnp.int32, (SUBS, LANES), 0)
    for half in range(channels // LANES):
        lanes = pl.ds(half * LANES, LANES)
        rates = [row_of(rate_ref, m, lanes) for m in range(modes)]
        retain = [wide(jnp.exp(-x)) for x in rates]
        state = [jnp.zeros((SUBS, LANES), F32) for _ in range(modes)]
        for step in range(steps):
            g = gated_ref[half, pl.ds(step, SUBS, stride=steps), :]
            state = [a * s + g for a, s in zip(retain, state)]
        for m in range(modes):
            s = state[m]
            for d in (1, 2, 4):
                drop = wide(jnp.exp(-(steps * d) * rates[m]))
                s = s + jnp.where(sub >= d, drop * pltpu.roll(s, d, 0), 0.0)
            state_ref[pl.ds(m, 1), lanes] = s[SUBS - 1 :]
            begin_ref[m, :, lanes] = jnp.where(sub >= 1, pltpu.roll(s, 1, 0), 0.0)
    across.wait()
    for copy in sides((blocks[0], blocks[2])):
        copy.wait()


def join_body(rows, rim_ref, head_ref, taps_ref, rate_ref, state_ref, *rest):
    out_ref, late_ref, top_ref, pad = *rest[3:6], rest[-1]
    modes, channels = rate_ref.shape
    taps = taps_ref.shape[1]
    sums = []
    for i in range(3):
        pad[i, pl.ds(0, HEAD), :] = rim_ref[pl.ds(i * RIM, RIM), :].astype(F32)[RIM - HEAD :]
        pad[i, pl.ds(HEAD, HEAD), :] = jnp.zeros((HEAD, channels), F32)
        total = head_ref[i]
        for t in range(1, taps):
            total = total + taps_ref[i, pl.ds(t, 1), :] * pad[i, pl.ds(HEAD - t, HEAD), :]
        sums.append(total)
    gated = sums[1] * sums[2]
    top_ref[0] = sums[0]
    top_ref[1] = gated
    more = gated - head_ref[1] * head_ref[2]
    rate = rate_ref[...]
    retain = jnp.exp(-rate)
    late = jnp.broadcast_to(more[:1], rate.shape)
    for i in range(1, taps - 1):
        late = retain * late + more[i : i + 1]
    late_ref[...] = late
    whole = (state_ref[...] + jnp.exp(-(rows - taps + 1) * rate) * late).astype(BF16)
    for i in range(out_ref.shape[0]):
        out_ref[i] = whole


def plane_body(rows, parts_ref, rate_ref, _a, _b, before_ref, total_ref, _same_a, _same_b):
    me = lax.axis_index("y") * lax.axis_size("core") + lax.axis_index("core")
    drop = jnp.exp(-rows * rate_ref[...])
    before = jnp.zeros(rate_ref.shape, F32)
    total = jnp.zeros(rate_ref.shape, F32)
    for i in range(parts_ref.shape[0]):
        part = parts_ref[i].astype(F32)
        before = jnp.where(i < me, before * drop + part, before)
        total = total * drop + part
    before_ref[...] = before
    for i in range(total_ref.shape[0]):
        total_ref[i] = total.astype(BF16)


def mix_body(
    taps, plane_rows, query_ref, gated_ref, begin_ref, late_ref, top_ref, before_ref, planes_ref, rate_ref, amp_ref,
    skip_ref, weight_hbm, _a, _b, _c, out_ref, own_ref, _same_a, _same_b, _same_c, hyena, carry, sem,
):
    halves, rows, _ = query_ref.shape
    modes = rate_ref.shape[0]
    steps = rows // SUBS
    width = own_ref.shape[1]
    own = pltpu.make_async_copy(weight_hbm.at[:, pl.ds(lax.axis_index("tp") * width, width)], own_ref, sem)
    own.start()
    z = lax.axis_index("z")
    me = lax.axis_index("y") * lax.axis_size("core") + lax.axis_index("core")
    rate = rate_ref[...]
    drop = jnp.exp(-plane_rows * rate)
    behind = jnp.zeros(rate.shape, F32)
    for i in range(planes_ref.shape[0]):
        behind = jnp.where(i < z, behind * drop + planes_ref[i].astype(F32), behind)
    carried = before_ref[...] + jnp.exp(-(rows * me).astype(F32) * rate) * behind
    carry[0] = carried
    carry[1] = carried + jnp.exp((taps - 1) * rate) * late_ref[...]
    sub = lax.broadcasted_iota(jnp.int32, (SUBS, LANES), 0)
    ahead = sub.astype(F32) * float(steps)
    for half in range(halves):
        lanes = pl.ds(half * LANES, LANES)
        rates = [row_of(rate_ref, m, lanes) for m in range(modes)]
        retain = [wide(jnp.exp(-x)) for x in rates]
        amp = [wide(row_of(amp_ref, m, lanes)) for m in range(modes)]
        skip = wide(row_of(skip_ref, 0, lanes))
        state = [
            begin_ref[m, :, lanes]
            + jnp.exp(-ahead * rates[m])
            * jnp.where(sub >= 1, row_of(carry.at[1], m, lanes), row_of(carry.at[0], m, lanes))
            for m in range(modes)
        ]
        for step in range(steps):
            at = pl.ds(step, SUBS, stride=steps)
            g = gated_ref[half, at, :]
            query = query_ref[half, at, :]
            if step < taps - 1:
                query = jnp.where(sub >= 1, query, top_ref[0, pl.ds(step, 1), lanes])
                g = jnp.where(sub >= 1, g, top_ref[1, pl.ds(step, 1), lanes])
            state = [a * s + g for a, s in zip(retain, state)]
            terms = [a * s for a, s in zip(amp, state)] + [skip * g]
            while len(terms) > 1:
                terms = [x + y for x, y in zip(terms[::2], terms[1::2])] + terms[len(terms) // 2 * 2 :]
            hyena[half, at, :] = query * terms[0]
    left = jnp.concatenate([hyena[half].astype(BF16) for half in range(halves)], axis=1)
    for i in range(out_ref.shape[0]):
        out_ref[i] = left
    own.wait()


def project_body(
    left_ref, own_ref, side_ref, half_ref, other_ref, late_side_ref, late_other_ref, other_half_ref, out_hbm, done, sems
):
    parts = left_ref.shape[0]
    here = lax.axis_index("tp")
    core = lax.axis_index("core")
    blocks, _, block = done.shape
    height = half_ref.shape[0]

    def rows_of(core):
        return pl.ds(pl.multiple_of(core * height, height), height)

    def run(side, other):
        across = left_ref.at[lax.rem(here + 2, parts)]
        pairs = [
            (left_ref[here], own_ref),
            (left_ref[lax.rem(here + parts - 1, parts)], side),
            (left_ref[lax.rem(here + 1, parts)], other),
            (across[:, rows_of(core)], half_ref),
            (across[:, rows_of(1 - core)], other_half_ref),
        ]
        copies = []
        for b in range(blocks):
            at = pl.ds(b * block, block)
            total = jnp.zeros(done.shape[1:], F32)
            for left, right in pairs:
                total += jnp.dot(left, right[:, at], preferred_element_type=F32)
            done[b] = total.astype(BF16)
            copies.append(pltpu.make_async_copy(done.at[b], out_hbm.at[:, at], sems.at[b]))
            copies[-1].start()
        for copy in copies:
            copy.wait()

    early = lax.axis_index("z") < EARLY

    @pl.when(early)
    def _():
        run(side_ref, other_ref)

    @pl.when(jnp.logical_not(early))
    def _():
        run(late_side_ref, late_other_ref)


def sent_on(block, d, planes):
    parts = lax.axis_size("tp")
    plane = lax.axis_size("y") * lax.axis_size("core")
    route = [
        ((z * plane + i) * parts + t, (z * plane + i) * parts + (t + d) % parts)
        for z in planes
        for i in range(plane)
        for t in range(parts)
    ]
    return lax.ppermute(block, ("z", "y", "core", "tp"), route)


def local(query_in, key_in, value_in, short_weight, residue, rate, skip, out_weight):
    rows, channels = query_in.shape
    modes = rate.shape[0]
    taps = short_weight.shape[1]
    planes = lax.axis_size("z")
    plane = lax.axis_size("y") * lax.axis_size("core")
    parts = lax.axis_size("tp")
    width = out_weight.shape[1] // parts
    order = ("z", "y", "core")
    devices = planes * plane
    by_half = (channels // LANES, rows, LANES)
    block_shapes = [pltpu.HBM((r, width), BF16) for r in (channels, channels // 2, channels)]
    skip = skip.reshape(1, -1)
    query_in, key_in, value_in, short_weight, residue, rate, skip, out_weight = (
        pltpu.with_memory_space_constraint(x, pltpu.HBM)
        for x in (query_in, key_in, value_in, short_weight, residue, rate, skip, out_weight)
    )
    rims = call(
        rim_body, [HBM] * 3, shape((3 * RIM, channels), BF16), "rims", [pltpu.SemaphoreType.DMA((3,))]
    )(query_in, key_in, value_in)
    rims = lax.ppermute(rims, order, [(i, i + 1) for i in range(devices - 1)])
    queries, gated, begin, states, heads, taps_here, rate, amplitude, skip, *blocks = call(
        gate_body,
        [HBM] * 8,
        (
            shape(by_half, F32),
            shape(by_half, F32),
            shape((modes, SUBS, channels), F32),
            shape((modes, channels), F32),
            shape((3, HEAD, channels), F32),
            shape(short_weight.shape, F32),
            shape((modes, channels), F32),
            shape((modes, channels), F32),
            shape((1, channels), F32),
            *block_shapes,
            *block_shapes[::2],
        ),
        "gate",
        [
            pltpu.VMEM((3, rows, channels), BF16),
            pltpu.VMEM((modes, channels), F32),
            pltpu.VMEM((3, HEAD + rows, channels), F32),
            pltpu.SemaphoreType.DMA((10,)),
        ],
        out_spec=(*[VMEM] * 9, *[HBM] * 5),
    )(query_in, key_in, value_in, short_weight, rate, residue, skip, out_weight)
    begin = pltpu.with_memory_space_constraint(begin, pltpu.VMEM)
    states, late, top, *blocks[:3] = call(
        lambda *refs: join_body(rows, *refs),
        [VMEM] * 5 + [ANY] * 3,
        (
            shape((plane, modes, channels), BF16),
            shape((modes, channels), F32),
            shape((2, HEAD, channels), F32),
            *block_shapes,
        ),
        "join",
        [pltpu.VMEM((3, 2 * HEAD, channels), F32)],
        out_spec=(VMEM, VMEM, VMEM, *[ANY] * 3),
        aliases={5 + i: 3 + i for i in range(3)},
    )(rims, heads, taps_here, rate, states, *blocks[:3])
    early = [sent_on(block, d, range(EARLY if d != 2 else planes)) for d, block in enumerate(blocks[:3], start=1)]
    states = lax.all_to_all(states, ("y", "core"), 0, 0, tiled=True)
    before, totals, *blocks = call(
        lambda *refs: plane_body(rows, *refs),
        [VMEM] * 2 + [ANY] * 2,
        (
            shape((modes, channels), F32),
            shape((planes, modes, channels), BF16),
            *block_shapes[::2],
        ),
        "plane",
        us=2,
        out_spec=(VMEM, VMEM, ANY, ANY),
        aliases={2: 2, 3: 3},
    )(states, rate, *blocks[3:])
    later = [sent_on(block, d, range(EARLY, planes)) for d, block in zip((1, 3), blocks)]
    before = pltpu.with_memory_space_constraint(before, pltpu.VMEM)
    totals = lax.all_to_all(totals, "z", 0, 0, tiled=True)
    hyena, own, *early = call(
        lambda *refs: mix_body(taps, rows * plane, *refs),
        [VMEM] * 10 + [HBM] + [ANY] * 3,
        (shape((parts, rows, channels), BF16), shape((channels, width), BF16), *[shape(x.shape, BF16) for x in block_shapes]),
        "mix",
        [
            pltpu.VMEM(by_half, F32),
            pltpu.VMEM((2, modes, channels), F32),
            pltpu.SemaphoreType.DMA,
        ],
        out_spec=(VMEM, VMEM, ANY, ANY, ANY),
        aliases={11: 2, 12: 3, 13: 4},
        us=2,
    )(queries, gated, begin, late, top, before, totals, rate, amplitude, skip, out_weight, *early)
    other_half = lax.ppermute(early[1], "core", [(0, 1), (1, 0)])
    hyena = lax.all_to_all(hyena, "tp", 0, 0, tiled=True)
    block = 256
    return call(
        project_body,
        [VMEM] * 8,
        shape((rows, width), BF16),
        "project",
        [pltpu.VMEM((width // block, rows, block), BF16), pltpu.SemaphoreType.DMA((width // block,))],
        out_spec=HBM,
    )(hyena, own, *early, *later, other_half)


def solution(mesh):
    fine = Mesh(mesh.devices.reshape(8, 8, 2, 4), ("z", "y", "core", "tp"))
    seq = ("z", "y", "core")
    in_specs = (
        P(seq, "tp"),
        P(seq, "tp"),
        P(seq, "tp"),
        P(None, None, "tp"),
        P(None, "tp"),
        P(None, "tp"),
        P("tp"),
        P("tp", None),
    )
    return jax.shard_map(local, mesh=fine, in_specs=in_specs, out_specs=P(seq, "tp"), check_vma=False)
```

```python
import jax
import jax.numpy as jnp
from jax import lax
from jax.experimental import pallas as pl
from jax.experimental.pallas import tpu as pltpu
from jax.sharding import Mesh, PartitionSpec as P

F32 = jnp.float32
BF16 = jnp.bfloat16
LANES = 128
SUBS = 8
RIM = 16
HEAD = 8
MIB = 1 << 20
RATE = 1.15e9


def shape(dims, dtype):
    return jax.ShapeDtypeStruct(dims, dtype)


VMEM = pl.BlockSpec(memory_space=pltpu.VMEM)
ANY = pl.BlockSpec(memory_space=pl.ANY)
HBM = pl.BlockSpec(memory_space=pltpu.HBM)


def call(body, specs, outs, name, scratch=(), mib=4, out_spec=VMEM, aliases=None, us=0):
    return pl.pallas_call(
        body,
        in_specs=specs,
        out_specs=out_spec if isinstance(out_spec, tuple) else jax.tree.map(lambda _: out_spec, outs),
        input_output_aliases=aliases or {},
        cost_estimate=pl.CostEstimate(flops=int(us * RATE), bytes_accessed=0, transcendentals=0) if us else None,
        out_shape=outs,
        scratch_shapes=list(scratch),
        compiler_params=pltpu.CompilerParams(vmem_limit_bytes=mib * MIB),
        name=name,
    )


def fetch(sources, targets, sems):
    copies = [pltpu.make_async_copy(s, t, sems.at[i]) for i, (s, t) in enumerate(zip(sources, targets))]
    for copy in copies:
        copy.start()
    return copies


def row_of(ref, m, lanes):
    return ref[pl.ds(m, 1), lanes]


def wide(row):
    return jnp.broadcast_to(row, (SUBS, LANES))


def one_minus_exp(x):
    series = 1.0 / 362880.0
    for n in (40320, 5040, 720, 120, 24, 6, 2, 1):
        series = 1.0 / n - x * series
    return jnp.where(x < 0.25, x * series, 1.0 - jnp.exp(-x))


def rim_body(q_ref, k_ref, v_ref, out_ref, sems):
    rows = q_ref.shape[0]
    refs = (q_ref, k_ref, v_ref)
    copies = fetch(
        [ref.at[pl.ds(rows - RIM, RIM), :] for ref in refs],
        [out_ref.at[pl.ds(i * RIM, RIM), :] for i in range(3)],
        sems,
    )
    for copy in copies:
        copy.wait()


def gate_body(
    q_hbm, k_hbm, v_hbm, taps_hbm, rate_hbm, residue_hbm, skip_hbm, weight_hbm,
    query_ref, gated_ref, begin_ref, state_ref, head_ref, taps_ref, rate_ref, amp_ref, skip_ref, *rest,
):
    *blocks, streams, residue_ref, pad, sems = rest
    here, parts = lax.axis_index("tp"), lax.axis_size("tp")
    width = blocks[0].shape[1]
    _, rows, channels = streams.shape
    modes = rate_ref.shape[0]
    taps = taps_ref.shape[1]
    steps = rows // SUBS
    copies = fetch(
        (q_hbm, k_hbm, v_hbm, taps_hbm, rate_hbm, residue_hbm, skip_hbm),
        (streams.at[0], streams.at[1], streams.at[2], taps_ref, rate_ref, residue_ref, skip_ref),
        sems,
    )
    sent = fetch(
        [weight_hbm.at[:, pl.ds(lax.rem(here + d, parts) * width, width)] for d in range(1, parts)],
        blocks,
        sems.at[pl.ds(7, parts - 1)],
    )
    for copy in copies:
        copy.wait()
    amp_ref[...] = residue_ref[...] * jnp.sqrt(one_minus_exp(2.0 * rate_ref[...]))
    for i in range(3):
        pad[i, pl.ds(0, HEAD), :] = jnp.zeros((HEAD, channels), F32)
        pad[i, pl.ds(HEAD, rows), :] = streams[i].astype(F32)
    block = 32
    for half in range(channels // LANES):
        lanes = pl.ds(half * LANES, LANES)
        for r in range(0, rows, block):
            sums = []
            for i in range(3):
                total = jnp.zeros((block, LANES), F32)
                for t in range(taps):
                    total = total + taps_ref[i, pl.ds(t, 1), lanes] * pad[i, pl.ds(HEAD + r - t, block), lanes]
                sums.append(total)
                if r == 0:
                    head_ref[i, :, lanes] = total[:HEAD]
            query_ref[half, pl.ds(r, block), :] = sums[0]
            gated_ref[half, pl.ds(r, block), :] = sums[1] * sums[2]
    sub = lax.broadcasted_iota(jnp.int32, (SUBS, LANES), 0)
    for half in range(channels // LANES):
        lanes = pl.ds(half * LANES, LANES)
        rates = [row_of(rate_ref, m, lanes) for m in range(modes)]
        retain = [wide(jnp.exp(-x)) for x in rates]
        state = [jnp.zeros((SUBS, LANES), F32) for _ in range(modes)]
        for step in range(steps):
            g = gated_ref[half, pl.ds(step, SUBS, stride=steps), :]
            state = [a * s + g for a, s in zip(retain, state)]
        for m in range(modes):
            s = state[m]
            for d in (1, 2, 4):
                drop = wide(jnp.exp(-(steps * d) * rates[m]))
                s = s + jnp.where(sub >= d, drop * pltpu.roll(s, d, 0), 0.0)
            state_ref[pl.ds(m, 1), lanes] = s[SUBS - 1 :]
            begin_ref[m, :, lanes] = jnp.where(sub >= 1, pltpu.roll(s, 1, 0), 0.0)
    for copy in sent:
        copy.wait()


def join_body(rows, rim_ref, head_ref, taps_ref, rate_ref, state_ref, out_ref, late_ref, top_ref, pad):
    modes, channels = rate_ref.shape
    taps = taps_ref.shape[1]
    sums = []
    for i in range(3):
        pad[i, pl.ds(0, HEAD), :] = rim_ref[pl.ds(i * RIM, RIM), :].astype(F32)[RIM - HEAD :]
        pad[i, pl.ds(HEAD, HEAD), :] = jnp.zeros((HEAD, channels), F32)
        total = head_ref[i]
        for t in range(1, taps):
            total = total + taps_ref[i, pl.ds(t, 1), :] * pad[i, pl.ds(HEAD - t, HEAD), :]
        sums.append(total)
    gated = sums[1] * sums[2]
    top_ref[0] = sums[0]
    top_ref[1] = gated
    more = gated - head_ref[1] * head_ref[2]
    rate = rate_ref[...]
    retain = jnp.exp(-rate)
    late = jnp.broadcast_to(more[:1], rate.shape)
    for i in range(1, taps - 1):
        late = retain * late + more[i : i + 1]
    late_ref[...] = late
    whole = (state_ref[...] + jnp.exp(-(rows - taps + 1) * rate) * late).astype(BF16)
    for i in range(out_ref.shape[0]):
        out_ref[i] = whole


def plane_body(rows, parts_ref, rate_ref, _block, before_ref, total_ref, _same_block):
    me = lax.axis_index("y") * lax.axis_size("core") + lax.axis_index("core")
    drop = jnp.exp(-rows * rate_ref[...])
    before = jnp.zeros(rate_ref.shape, F32)
    total = jnp.zeros(rate_ref.shape, F32)
    for i in range(parts_ref.shape[0]):
        part = parts_ref[i].astype(F32)
        before = jnp.where(i < me, before * drop + part, before)
        total = total * drop + part
    before_ref[...] = before
    for i in range(total_ref.shape[0]):
        total_ref[i] = total.astype(BF16)


def mix_body(
    taps, plane_rows, query_ref, gated_ref, begin_ref, late_ref, top_ref, before_ref, planes_ref, rate_ref, amp_ref,
    skip_ref, weight_hbm, out_ref, own_ref, hyena, carry, sem,
):
    halves, rows, _ = query_ref.shape
    modes = rate_ref.shape[0]
    steps = rows // SUBS
    width = own_ref.shape[1]
    own = pltpu.make_async_copy(weight_hbm.at[:, pl.ds(lax.axis_index("tp") * width, width)], own_ref, sem)
    own.start()
    z = lax.axis_index("z")
    me = lax.axis_index("y") * lax.axis_size("core") + lax.axis_index("core")
    rate = rate_ref[...]
    drop = jnp.exp(-plane_rows * rate)
    behind = jnp.zeros(rate.shape, F32)
    for i in range(planes_ref.shape[0]):
        behind = jnp.where(i < z, behind * drop + planes_ref[i].astype(F32), behind)
    carried = before_ref[...] + jnp.exp(-(rows * me).astype(F32) * rate) * behind
    carry[0] = carried
    carry[1] = carried + jnp.exp((taps - 1) * rate) * late_ref[...]
    sub = lax.broadcasted_iota(jnp.int32, (SUBS, LANES), 0)
    ahead = sub.astype(F32) * float(steps)
    for half in range(halves):
        lanes = pl.ds(half * LANES, LANES)
        rates = [row_of(rate_ref, m, lanes) for m in range(modes)]
        retain = [wide(jnp.exp(-x)) for x in rates]
        amp = [wide(row_of(amp_ref, m, lanes)) for m in range(modes)]
        skip = wide(row_of(skip_ref, 0, lanes))
        state = [
            begin_ref[m, :, lanes]
            + jnp.exp(-ahead * rates[m])
            * jnp.where(sub >= 1, row_of(carry.at[1], m, lanes), row_of(carry.at[0], m, lanes))
            for m in range(modes)
        ]
        for step in range(steps):
            at = pl.ds(step, SUBS, stride=steps)
            g = gated_ref[half, at, :]
            query = query_ref[half, at, :]
            if step < taps - 1:
                query = jnp.where(sub >= 1, query, top_ref[0, pl.ds(step, 1), lanes])
                g = jnp.where(sub >= 1, g, top_ref[1, pl.ds(step, 1), lanes])
            state = [a * s + g for a, s in zip(retain, state)]
            terms = [a * s for a, s in zip(amp, state)] + [skip * g]
            while len(terms) > 1:
                terms = [x + y for x, y in zip(terms[::2], terms[1::2])] + terms[len(terms) // 2 * 2 :]
            hyena[half, at, :] = query * terms[0]
    left = jnp.concatenate([hyena[half].astype(BF16) for half in range(halves)], axis=1)
    for i in range(out_ref.shape[0]):
        out_ref[i] = left
    own.wait()


def order_body(left_ref, _side, _across, out_ref, _same_side, _same_across):
    parts, _, channels = left_ref.shape
    here = lax.axis_index("tp")
    for d in range(parts):
        out_ref[:, pl.ds(d * channels, channels)] = left_ref[lax.rem(here + parts - d, parts)]


def project_body(left_ref, *rest):
    *rights, out_hbm, done, sems = rest
    blocks, _, block = done.shape
    channels = rights[0].shape[0]
    copies = []
    for b in range(blocks):
        at = pl.ds(b * block, block)
        total = jnp.zeros(done.shape[1:], F32)
        for d, right in enumerate(rights):
            total += jnp.dot(left_ref[:, pl.ds(d * channels, channels)], right[:, at], preferred_element_type=F32)
        done[b] = total.astype(BF16)
        copies.append(pltpu.make_async_copy(done.at[b], out_hbm.at[:, at], sems.at[b]))
        copies[-1].start()
    for copy in copies:
        copy.wait()


def local(query_in, key_in, value_in, short_weight, residue, rate, skip, out_weight):
    rows, channels = query_in.shape
    modes = rate.shape[0]
    taps = short_weight.shape[1]
    planes = lax.axis_size("z")
    plane = lax.axis_size("y") * lax.axis_size("core")
    parts = lax.axis_size("tp")
    width = out_weight.shape[1] // parts
    order = ("z", "y", "core")
    devices = planes * plane
    by_half = (channels // LANES, rows, LANES)
    skip = skip.reshape(1, -1)
    query_in, key_in, value_in, short_weight, residue, rate, skip, out_weight = (
        pltpu.with_memory_space_constraint(x, pltpu.HBM)
        for x in (query_in, key_in, value_in, short_weight, residue, rate, skip, out_weight)
    )
    rims = call(
        rim_body, [HBM] * 3, shape((3 * RIM, channels), BF16), "rims", [pltpu.SemaphoreType.DMA((3,))]
    )(query_in, key_in, value_in)
    rims = lax.ppermute(rims, order, [(i, i + 1) for i in range(devices - 1)])
    queries, gated, begin, states, heads, taps_here, rate, amplitude, skip, *blocks = call(
        gate_body,
        [HBM] * 8,
        (
            shape(by_half, F32),
            shape(by_half, F32),
            shape((modes, SUBS, channels), F32),
            shape((modes, channels), F32),
            shape((3, HEAD, channels), F32),
            shape(short_weight.shape, F32),
            shape((modes, channels), F32),
            shape((modes, channels), F32),
            shape((1, channels), F32),
            *[shape((channels, width), BF16)] * (parts - 1),
        ),
        "gate",
        [
            pltpu.VMEM((3, rows, channels), BF16),
            pltpu.VMEM((modes, channels), F32),
            pltpu.VMEM((3, HEAD + rows, channels), F32),
            pltpu.SemaphoreType.DMA((7 + parts - 1,)),
        ],
    )(query_in, key_in, value_in, short_weight, rate, residue, skip, out_weight)
    def to_next(block, d):
        return lax.ppermute(block, "tp", [(i, (i + d) % parts) for i in range(parts)])

    blocks = [to_next(blocks[0], 1), to_next(blocks[1], 2), blocks[2]]
    states, late, top = call(
        lambda *refs: join_body(rows, *refs),
        [VMEM] * 5,
        (
            shape((plane, modes, channels), BF16),
            shape((modes, channels), F32),
            shape((2, HEAD, channels), F32),
        ),
        "join",
        [pltpu.VMEM((3, 2 * HEAD, channels), F32)],
    )(rims, heads, taps_here, rate, states)
    states = lax.all_to_all(states, ("y", "core"), 0, 0, tiled=True)
    before, totals, blocks[2] = call(
        lambda *refs: plane_body(rows, *refs),
        [VMEM] * 2 + [ANY],
        (shape((modes, channels), F32), shape((planes, modes, channels), BF16), shape((channels, width), BF16)),
        "plane",
        out_spec=(VMEM, VMEM, ANY),
        aliases={2: 2},
    )(states, rate, blocks[2])
    blocks[2] = to_next(blocks[2], 3)
    totals = lax.all_to_all(totals, "z", 0, 0, tiled=True)
    hyena, own = call(
        lambda *refs: mix_body(taps, rows * plane, *refs),
        [VMEM] * 10 + [HBM],
        (shape((parts, rows, channels), BF16), shape((channels, width), BF16)),
        "mix",
        [
            pltpu.VMEM(by_half, F32),
            pltpu.VMEM((2, modes, channels), F32),
            pltpu.SemaphoreType.DMA,
        ],
    )(queries, gated, begin, late, top, before, totals, rate, amplitude, skip, out_weight)
    hyena = lax.all_to_all(hyena, "tp", 0, 0, tiled=True)
    hyena, *blocks[:2] = call(
        order_body,
        [VMEM] + [ANY] * 2,
        (shape((rows, parts * channels), BF16), *[shape((channels, width), BF16)] * 2),
        "order",
        out_spec=(VMEM, ANY, ANY),
        aliases={1: 1, 2: 2},
        us=2,
    )(hyena, *blocks[:2])
    block = 256
    return call(
        project_body,
        [VMEM] * 5,
        shape((rows, width), BF16),
        "project",
        [pltpu.VMEM((width // block, rows, block), BF16), pltpu.SemaphoreType.DMA((width // block,))],
        out_spec=HBM,
    )(hyena, own, *blocks)


def solution(mesh):
    fine = Mesh(mesh.devices.reshape(8, 8, 2, 4), ("z", "y", "core", "tp"))
    seq = ("z", "y", "core")
    in_specs = (
        P(seq, "tp"),
        P(seq, "tp"),
        P(seq, "tp"),
        P(None, None, "tp"),
        P(None, "tp"),
        P(None, "tp"),
        P("tp"),
        P("tp", None),
    )
    return jax.shard_map(local, mesh=fine, in_specs=in_specs, out_specs=P(seq, "tp"), check_vma=False)
```

```python
import jax
import jax.numpy as jnp
from jax import lax
from jax.experimental import pallas as pl
from jax.experimental.pallas import tpu as pltpu
from jax.sharding import Mesh, PartitionSpec as P

F32 = jnp.float32
BF16 = jnp.bfloat16
LANES = 128
SUBS = 8
RIM = 16
HEAD = 8
MIB = 1 << 20
RATE = 1.15e9


def shape(dims, dtype):
    return jax.ShapeDtypeStruct(dims, dtype)


VMEM = pl.BlockSpec(memory_space=pltpu.VMEM)
ANY = pl.BlockSpec(memory_space=pl.ANY)
HBM = pl.BlockSpec(memory_space=pltpu.HBM)


def call(body, specs, outs, name, scratch=(), mib=4, out_spec=VMEM, aliases=None, us=0):
    return pl.pallas_call(
        body,
        in_specs=specs,
        out_specs=out_spec if isinstance(out_spec, tuple) else jax.tree.map(lambda _: out_spec, outs),
        input_output_aliases=aliases or {},
        cost_estimate=pl.CostEstimate(flops=int(us * RATE), bytes_accessed=0, transcendentals=0) if us else None,
        out_shape=outs,
        scratch_shapes=list(scratch),
        compiler_params=pltpu.CompilerParams(vmem_limit_bytes=mib * MIB),
        name=name,
    )


def fetch(sources, targets, sems):
    copies = [pltpu.make_async_copy(s, t, sems.at[i]) for i, (s, t) in enumerate(zip(sources, targets))]
    for copy in copies:
        copy.start()
    return copies


def row_of(ref, m, lanes):
    return ref[pl.ds(m, 1), lanes]


def wide(row):
    return jnp.broadcast_to(row, (SUBS, LANES))


def one_minus_exp(x):
    series = 1.0 / 362880.0
    for n in (40320, 5040, 720, 120, 24, 6, 2, 1):
        series = 1.0 / n - x * series
    return jnp.where(x < 0.25, x * series, 1.0 - jnp.exp(-x))


def rim_body(q_ref, k_ref, v_ref, out_ref, sems):
    rows = q_ref.shape[0]
    refs = (q_ref, k_ref, v_ref)
    copies = fetch(
        [ref.at[pl.ds(rows - RIM, RIM), :] for ref in refs],
        [out_ref.at[pl.ds(i * RIM, RIM), :] for i in range(3)],
        sems,
    )
    for copy in copies:
        copy.wait()


def gate_body(
    q_hbm, k_hbm, v_hbm, taps_hbm, rate_hbm, residue_hbm, skip_hbm, weight_hbm,
    query_ref, gated_ref, begin_ref, state_ref, head_ref, taps_ref, rate_ref, amp_ref, skip_ref, *rest,
):
    *blocks, streams, residue_ref, pad, held, sems = rest
    here, parts = lax.axis_index("tp"), lax.axis_size("tp")
    width = held.shape[2]
    _, rows, channels = streams.shape
    modes = rate_ref.shape[0]
    taps = taps_ref.shape[1]
    steps = rows // SUBS
    copies = fetch(
        (q_hbm, k_hbm, v_hbm, taps_hbm, rate_hbm, residue_hbm, skip_hbm),
        (streams.at[0], streams.at[1], streams.at[2], taps_ref, rate_ref, residue_ref, skip_ref),
        sems,
    )
    sent = fetch(
        [weight_hbm.at[:, pl.ds(lax.rem(here + d, parts) * width, width)] for d in range(1, parts)],
        [held.at[d] for d in range(parts - 1)],
        sems.at[pl.ds(7, parts - 1)],
    )
    for copy in copies:
        copy.wait()
    amp_ref[...] = residue_ref[...] * jnp.sqrt(one_minus_exp(2.0 * rate_ref[...]))
    for i in range(3):
        pad[i, pl.ds(0, HEAD), :] = jnp.zeros((HEAD, channels), F32)
        pad[i, pl.ds(HEAD, rows), :] = streams[i].astype(F32)
    block = 32
    for half in range(channels // LANES):
        lanes = pl.ds(half * LANES, LANES)
        for r in range(0, rows, block):
            sums = []
            for i in range(3):
                total = jnp.zeros((block, LANES), F32)
                for t in range(taps):
                    total = total + taps_ref[i, pl.ds(t, 1), lanes] * pad[i, pl.ds(HEAD + r - t, block), lanes]
                sums.append(total)
                if r == 0:
                    head_ref[i, :, lanes] = total[:HEAD]
            query_ref[half, pl.ds(r, block), :] = sums[0]
            gated_ref[half, pl.ds(r, block), :] = sums[1] * sums[2]
    for copy in sent:
        copy.wait()
    sent = fetch([held.at[d] for d in range(parts - 1)], blocks, sems.at[pl.ds(7, parts - 1)])
    sub = lax.broadcasted_iota(jnp.int32, (SUBS, LANES), 0)
    for half in range(channels // LANES):
        lanes = pl.ds(half * LANES, LANES)
        rates = [row_of(rate_ref, m, lanes) for m in range(modes)]
        retain = [wide(jnp.exp(-x)) for x in rates]
        state = [jnp.zeros((SUBS, LANES), F32) for _ in range(modes)]
        for step in range(steps):
            g = gated_ref[half, pl.ds(step, SUBS, stride=steps), :]
            state = [a * s + g for a, s in zip(retain, state)]
        for m in range(modes):
            s = state[m]
            for d in (1, 2, 4):
                drop = wide(jnp.exp(-(steps * d) * rates[m]))
                s = s + jnp.where(sub >= d, drop * pltpu.roll(s, d, 0), 0.0)
            state_ref[pl.ds(m, 1), lanes] = s[SUBS - 1 :]
            begin_ref[m, :, lanes] = jnp.where(sub >= 1, pltpu.roll(s, 1, 0), 0.0)
    for copy in sent:
        copy.wait()


def join_body(rows, rim_ref, head_ref, taps_ref, rate_ref, state_ref, out_ref, late_ref, top_ref, pad):
    modes, channels = rate_ref.shape
    taps = taps_ref.shape[1]
    sums = []
    for i in range(3):
        pad[i, pl.ds(0, HEAD), :] = rim_ref[pl.ds(i * RIM, RIM), :].astype(F32)[RIM - HEAD :]
        pad[i, pl.ds(HEAD, HEAD), :] = jnp.zeros((HEAD, channels), F32)
        total = head_ref[i]
        for t in range(1, taps):
            total = total + taps_ref[i, pl.ds(t, 1), :] * pad[i, pl.ds(HEAD - t, HEAD), :]
        sums.append(total)
    gated = sums[1] * sums[2]
    top_ref[0] = sums[0]
    top_ref[1] = gated
    more = gated - head_ref[1] * head_ref[2]
    rate = rate_ref[...]
    retain = jnp.exp(-rate)
    late = jnp.broadcast_to(more[:1], rate.shape)
    for i in range(1, taps - 1):
        late = retain * late + more[i : i + 1]
    late_ref[...] = late
    whole = (state_ref[...] + jnp.exp(-(rows - taps + 1) * rate) * late).astype(BF16)
    for i in range(out_ref.shape[0]):
        out_ref[i] = whole


def plane_body(rows, parts_ref, rate_ref, _a, _b, before_ref, total_ref, _same_a, _same_b):
    me = lax.axis_index("y") * lax.axis_size("core") + lax.axis_index("core")
    drop = jnp.exp(-rows * rate_ref[...])
    before = jnp.zeros(rate_ref.shape, F32)
    total = jnp.zeros(rate_ref.shape, F32)
    for i in range(parts_ref.shape[0]):
        part = parts_ref[i].astype(F32)
        before = jnp.where(i < me, before * drop + part, before)
        total = total * drop + part
    before_ref[...] = before
    for i in range(total_ref.shape[0]):
        total_ref[i] = total.astype(BF16)


def mix_body(
    taps, plane_rows, query_ref, gated_ref, begin_ref, late_ref, top_ref, before_ref, planes_ref, rate_ref, amp_ref,
    skip_ref, weight_hbm, out_ref, own_ref, hyena, carry, sem,
):
    halves, rows, _ = query_ref.shape
    modes = rate_ref.shape[0]
    steps = rows // SUBS
    width = own_ref.shape[1]
    own = pltpu.make_async_copy(weight_hbm.at[:, pl.ds(lax.axis_index("tp") * width, width)], own_ref, sem)
    own.start()
    z = lax.axis_index("z")
    me = lax.axis_index("y") * lax.axis_size("core") + lax.axis_index("core")
    rate = rate_ref[...]
    drop = jnp.exp(-plane_rows * rate)
    behind = jnp.zeros(rate.shape, F32)
    for i in range(planes_ref.shape[0]):
        behind = jnp.where(i < z, behind * drop + planes_ref[i].astype(F32), behind)
    carried = before_ref[...] + jnp.exp(-(rows * me).astype(F32) * rate) * behind
    carry[0] = carried
    carry[1] = carried + jnp.exp((taps - 1) * rate) * late_ref[...]
    sub = lax.broadcasted_iota(jnp.int32, (SUBS, LANES), 0)
    ahead = sub.astype(F32) * float(steps)
    for half in range(halves):
        lanes = pl.ds(half * LANES, LANES)
        rates = [row_of(rate_ref, m, lanes) for m in range(modes)]
        retain = [wide(jnp.exp(-x)) for x in rates]
        amp = [wide(row_of(amp_ref, m, lanes)) for m in range(modes)]
        skip = wide(row_of(skip_ref, 0, lanes))
        state = [
            begin_ref[m, :, lanes]
            + jnp.exp(-ahead * rates[m])
            * jnp.where(sub >= 1, row_of(carry.at[1], m, lanes), row_of(carry.at[0], m, lanes))
            for m in range(modes)
        ]
        for step in range(steps):
            at = pl.ds(step, SUBS, stride=steps)
            g = gated_ref[half, at, :]
            query = query_ref[half, at, :]
            if step < taps - 1:
                query = jnp.where(sub >= 1, query, top_ref[0, pl.ds(step, 1), lanes])
                g = jnp.where(sub >= 1, g, top_ref[1, pl.ds(step, 1), lanes])
            state = [a * s + g for a, s in zip(retain, state)]
            terms = [a * s for a, s in zip(amp, state)] + [skip * g]
            while len(terms) > 1:
                terms = [x + y for x, y in zip(terms[::2], terms[1::2])] + terms[len(terms) // 2 * 2 :]
            hyena[half, at, :] = query * terms[0]
    left = jnp.concatenate([hyena[half].astype(BF16) for half in range(halves)], axis=1)
    for i in range(out_ref.shape[0]):
        out_ref[i] = left
    own.wait()


def order_body(left_ref, _across, out_ref, _same_across):
    parts, _, channels = left_ref.shape
    here = lax.axis_index("tp")
    for d in range(parts):
        out_ref[:, pl.ds(d * channels, channels)] = left_ref[lax.rem(here + parts - d, parts)]


def project_body(left_ref, *rest):
    *rights, out_hbm, done, sems = rest
    blocks, _, block = done.shape
    channels = rights[0].shape[0]
    copies = []
    for b in range(blocks):
        at = pl.ds(b * block, block)
        total = jnp.zeros(done.shape[1:], F32)
        for d, right in enumerate(rights):
            total += jnp.dot(left_ref[:, pl.ds(d * channels, channels)], right[:, at], preferred_element_type=F32)
        done[b] = total.astype(BF16)
        copies.append(pltpu.make_async_copy(done.at[b], out_hbm.at[:, at], sems.at[b]))
        copies[-1].start()
    for copy in copies:
        copy.wait()


def local(query_in, key_in, value_in, short_weight, residue, rate, skip, out_weight):
    rows, channels = query_in.shape
    modes = rate.shape[0]
    taps = short_weight.shape[1]
    planes = lax.axis_size("z")
    plane = lax.axis_size("y") * lax.axis_size("core")
    parts = lax.axis_size("tp")
    width = out_weight.shape[1] // parts
    order = ("z", "y", "core")
    devices = planes * plane
    by_half = (channels // LANES, rows, LANES)
    skip = skip.reshape(1, -1)
    query_in, key_in, value_in, short_weight, residue, rate, skip, out_weight = (
        pltpu.with_memory_space_constraint(x, pltpu.HBM)
        for x in (query_in, key_in, value_in, short_weight, residue, rate, skip, out_weight)
    )
    rims = call(
        rim_body, [HBM] * 3, shape((3 * RIM, channels), BF16), "rims", [pltpu.SemaphoreType.DMA((3,))]
    )(query_in, key_in, value_in)
    rims = lax.ppermute(rims, order, [(i, i + 1) for i in range(devices - 1)])
    queries, gated, begin, states, heads, taps_here, rate, amplitude, skip, *blocks = call(
        gate_body,
        [HBM] * 8,
        (
            shape(by_half, F32),
            shape(by_half, F32),
            shape((modes, SUBS, channels), F32),
            shape((modes, channels), F32),
            shape((3, HEAD, channels), F32),
            shape(short_weight.shape, F32),
            shape((modes, channels), F32),
            shape((modes, channels), F32),
            shape((1, channels), F32),
            *[pltpu.HBM((channels, width), BF16)] * (parts - 1),
        ),
        "gate",
        [
            pltpu.VMEM((3, rows, channels), BF16),
            pltpu.VMEM((modes, channels), F32),
            pltpu.VMEM((3, HEAD + rows, channels), F32),
            pltpu.VMEM((parts - 1, channels, width), BF16),
            pltpu.SemaphoreType.DMA((7 + parts - 1,)),
        ],
        out_spec=(*[VMEM] * 9, *[HBM] * (parts - 1)),
    )(query_in, key_in, value_in, short_weight, rate, residue, skip, out_weight)
    def to_next(block, d):
        return lax.ppermute(block, "tp", [(i, (i + d) % parts) for i in range(parts)])

    blocks[1] = to_next(blocks[1], 2)
    states, late, top = call(
        lambda *refs: join_body(rows, *refs),
        [VMEM] * 5,
        (
            shape((plane, modes, channels), BF16),
            shape((modes, channels), F32),
            shape((2, HEAD, channels), F32),
        ),
        "join",
        [pltpu.VMEM((3, 2 * HEAD, channels), F32)],
    )(rims, heads, taps_here, rate, states)
    states = lax.all_to_all(states, ("y", "core"), 0, 0, tiled=True)
    before, totals, *blocks[::2] = call(
        lambda *refs: plane_body(rows, *refs),
        [VMEM] * 2 + [ANY] * 2,
        (
            shape((modes, channels), F32),
            shape((planes, modes, channels), BF16),
            *[pltpu.HBM((channels, width), BF16)] * 2,
        ),
        "plane",
        out_spec=(VMEM, VMEM, ANY, ANY),
        aliases={2: 2, 3: 3},
    )(states, rate, *blocks[::2])
    blocks[0], blocks[2] = to_next(blocks[0], 1), to_next(blocks[2], 3)
    totals = lax.all_to_all(totals, "z", 0, 0, tiled=True)
    hyena, own = call(
        lambda *refs: mix_body(taps, rows * plane, *refs),
        [VMEM] * 10 + [HBM],
        (shape((parts, rows, channels), BF16), shape((channels, width), BF16)),
        "mix",
        [
            pltpu.VMEM(by_half, F32),
            pltpu.VMEM((2, modes, channels), F32),
            pltpu.SemaphoreType.DMA,
        ],
    )(queries, gated, begin, late, top, before, totals, rate, amplitude, skip, out_weight)
    hyena = lax.all_to_all(hyena, "tp", 0, 0, tiled=True)
    hyena, blocks[1] = call(
        order_body,
        [VMEM, ANY],
        (shape((rows, parts * channels), BF16), shape((channels, width), BF16)),
        "order",
        out_spec=(VMEM, ANY),
        aliases={1: 1},
        us=2,
    )(hyena, blocks[1])
    block = 256
    return call(
        project_body,
        [VMEM] * 5,
        shape((rows, width), BF16),
        "project",
        [pltpu.VMEM((width // block, rows, block), BF16), pltpu.SemaphoreType.DMA((width // block,))],
        out_spec=HBM,
    )(hyena, own, *blocks)


def solution(mesh):
    fine = Mesh(mesh.devices.reshape(8, 8, 2, 4), ("z", "y", "core", "tp"))
    seq = ("z", "y", "core")
    in_specs = (
        P(seq, "tp"),
        P(seq, "tp"),
        P(seq, "tp"),
        P(None, None, "tp"),
        P(None, "tp"),
        P(None, "tp"),
        P("tp"),
        P("tp", None),
    )
    return jax.shard_map(local, mesh=fine, in_specs=in_specs, out_specs=P(seq, "tp"), check_vma=False)
```

```python
import jax
import jax.numpy as jnp
from jax import lax
from jax.experimental import pallas as pl
from jax.experimental.pallas import tpu as pltpu
from jax.sharding import Mesh, PartitionSpec as P

F32 = jnp.float32
BF16 = jnp.bfloat16
LANES = 128
SUBS = 8
RIM = 16
HEAD = 8
MIB = 1 << 20
RATE = 1.15e9


def shape(dims, dtype):
    return jax.ShapeDtypeStruct(dims, dtype)


VMEM = pl.BlockSpec(memory_space=pltpu.VMEM)
ANY = pl.BlockSpec(memory_space=pl.ANY)
HBM = pl.BlockSpec(memory_space=pltpu.HBM)


def call(body, specs, outs, name, scratch=(), mib=4, out_spec=VMEM, aliases=None, us=0):
    return pl.pallas_call(
        body,
        in_specs=specs,
        out_specs=out_spec if isinstance(out_spec, tuple) else jax.tree.map(lambda _: out_spec, outs),
        input_output_aliases=aliases or {},
        cost_estimate=pl.CostEstimate(flops=int(us * RATE), bytes_accessed=0, transcendentals=0) if us else None,
        out_shape=outs,
        scratch_shapes=list(scratch),
        compiler_params=pltpu.CompilerParams(vmem_limit_bytes=mib * MIB),
        name=name,
    )


def fetch(sources, targets, sems):
    copies = [pltpu.make_async_copy(s, t, sems.at[i]) for i, (s, t) in enumerate(zip(sources, targets))]
    for copy in copies:
        copy.start()
    return copies


def row_of(ref, m, lanes):
    return ref[pl.ds(m, 1), lanes]


def wide(row):
    return jnp.broadcast_to(row, (SUBS, LANES))


def one_minus_exp(x):
    series = 1.0 / 362880.0
    for n in (40320, 5040, 720, 120, 24, 6, 2, 1):
        series = 1.0 / n - x * series
    return jnp.where(x < 0.25, x * series, 1.0 - jnp.exp(-x))


def rim_body(q_ref, k_ref, v_ref, out_ref, sems):
    rows = q_ref.shape[0]
    refs = (q_ref, k_ref, v_ref)
    copies = fetch(
        [ref.at[pl.ds(rows - RIM, RIM), :] for ref in refs],
        [out_ref.at[pl.ds(i * RIM, RIM), :] for i in range(3)],
        sems,
    )
    for copy in copies:
        copy.wait()


def gate_body(
    q_hbm, k_hbm, v_hbm, taps_hbm, rate_hbm, residue_hbm, skip_hbm, weight_hbm,
    query_ref, gated_ref, begin_ref, state_ref, head_ref, taps_ref, rate_ref, amp_ref, skip_ref, *rest,
):
    *blocks, streams, residue_ref, pad, sems = rest
    here, parts = lax.axis_index("tp"), lax.axis_size("tp")
    width = blocks[0].shape[1]
    _, rows, channels = streams.shape
    modes = rate_ref.shape[0]
    taps = taps_ref.shape[1]
    steps = rows // SUBS
    copies = fetch(
        (q_hbm, k_hbm, v_hbm, taps_hbm, rate_hbm, residue_hbm, skip_hbm),
        (streams.at[0], streams.at[1], streams.at[2], taps_ref, rate_ref, residue_ref, skip_ref),
        sems,
    )
    sent = fetch(
        [weight_hbm.at[:, pl.ds(lax.rem(here + d, parts) * width, width)] for d in range(1, parts)],
        blocks,
        sems.at[pl.ds(7, parts - 1)],
    )
    for copy in copies:
        copy.wait()
    amp_ref[...] = residue_ref[...] * jnp.sqrt(one_minus_exp(2.0 * rate_ref[...]))
    for i in range(3):
        pad[i, pl.ds(0, HEAD), :] = jnp.zeros((HEAD, channels), F32)
        pad[i, pl.ds(HEAD, rows), :] = streams[i].astype(F32)
    block = 32
    for half in range(channels // LANES):
        lanes = pl.ds(half * LANES, LANES)
        for r in range(0, rows, block):
            sums = []
            for i in range(3):
                total = jnp.zeros((block, LANES), F32)
                for t in range(taps):
                    total = total + taps_ref[i, pl.ds(t, 1), lanes] * pad[i, pl.ds(HEAD + r - t, block), lanes]
                sums.append(total)
                if r == 0:
                    head_ref[i, :, lanes] = total[:HEAD]
            query_ref[half, pl.ds(r, block), :] = sums[0]
            gated_ref[half, pl.ds(r, block), :] = sums[1] * sums[2]
    sub = lax.broadcasted_iota(jnp.int32, (SUBS, LANES), 0)
    for half in range(channels // LANES):
        lanes = pl.ds(half * LANES, LANES)
        rates = [row_of(rate_ref, m, lanes) for m in range(modes)]
        retain = [wide(jnp.exp(-x)) for x in rates]
        state = [jnp.zeros((SUBS, LANES), F32) for _ in range(modes)]
        for step in range(steps):
            g = gated_ref[half, pl.ds(step, SUBS, stride=steps), :]
            state = [a * s + g for a, s in zip(retain, state)]
        for m in range(modes):
            s = state[m]
            for d in (1, 2, 4):
                drop = wide(jnp.exp(-(steps * d) * rates[m]))
                s = s + jnp.where(sub >= d, drop * pltpu.roll(s, d, 0), 0.0)
            state_ref[pl.ds(m, 1), lanes] = s[SUBS - 1 :]
            begin_ref[m, :, lanes] = jnp.where(sub >= 1, pltpu.roll(s, 1, 0), 0.0)
    for copy in sent:
        copy.wait()


def join_body(rows, rim_ref, head_ref, taps_ref, rate_ref, state_ref, out_hbm, late_ref, top_ref, pad, whole, sems):
    modes, channels = rate_ref.shape
    taps = taps_ref.shape[1]
    sums = []
    for i in range(3):
        pad[i, pl.ds(0, HEAD), :] = rim_ref[pl.ds(i * RIM, RIM), :].astype(F32)[RIM - HEAD :]
        pad[i, pl.ds(HEAD, HEAD), :] = jnp.zeros((HEAD, channels), F32)
        total = head_ref[i]
        for t in range(1, taps):
            total = total + taps_ref[i, pl.ds(t, 1), :] * pad[i, pl.ds(HEAD - t, HEAD), :]
        sums.append(total)
    gated = sums[1] * sums[2]
    more = gated - head_ref[1] * head_ref[2]
    rate = rate_ref[...]
    retain = jnp.exp(-rate)
    late = jnp.broadcast_to(more[:1], rate.shape)
    for i in range(1, taps - 1):
        late = retain * late + more[i : i + 1]
    whole[...] = (state_ref[...] + jnp.exp(-(rows - taps + 1) * rate) * late).astype(BF16)
    peers = out_hbm.shape[0]
    copies = fetch([whole] * peers, [out_hbm.at[i] for i in range(peers)], sems)
    top_ref[0] = sums[0]
    top_ref[1] = gated
    late_ref[...] = late
    for copy in copies:
        copy.wait()


def plane_body(rows, parts_ref, rate_ref, _block, before_ref, total_hbm, _same_block, held, sems):
    me = lax.axis_index("y") * lax.axis_size("core") + lax.axis_index("core")
    drop = jnp.exp(-rows * rate_ref[...])
    total = jnp.zeros(rate_ref.shape, F32)
    for i in range(parts_ref.shape[0]):
        total = total * drop + parts_ref[i].astype(F32)
    held[...] = total.astype(BF16)
    planes = total_hbm.shape[0]
    copies = fetch([held] * planes, [total_hbm.at[i] for i in range(planes)], sems)
    before = jnp.zeros(rate_ref.shape, F32)
    for i in range(parts_ref.shape[0]):
        before = jnp.where(i < me, before * drop + parts_ref[i].astype(F32), before)
    before_ref[...] = before
    for copy in copies:
        copy.wait()


def mix_body(
    taps, plane_rows, query_ref, gated_ref, begin_ref, late_ref, top_ref, before_ref, planes_ref, rate_ref, amp_ref,
    skip_ref, weight_hbm, out_hbm, own_ref, hyena, left, carry, sem, sems,
):
    halves, rows, _ = query_ref.shape
    modes = rate_ref.shape[0]
    steps = rows // SUBS
    width = own_ref.shape[1]
    own = pltpu.make_async_copy(weight_hbm.at[:, pl.ds(lax.axis_index("tp") * width, width)], own_ref, sem)
    own.start()
    z = lax.axis_index("z")
    me = lax.axis_index("y") * lax.axis_size("core") + lax.axis_index("core")
    rate = rate_ref[...]
    drop = jnp.exp(-plane_rows * rate)
    behind = jnp.zeros(rate.shape, F32)
    for i in range(planes_ref.shape[0]):
        behind = jnp.where(i < z, behind * drop + planes_ref[i].astype(F32), behind)
    carried = before_ref[...] + jnp.exp(-(rows * me).astype(F32) * rate) * behind
    carry[0] = carried
    carry[1] = carried + jnp.exp((taps - 1) * rate) * late_ref[...]
    parts, copies = out_hbm.shape[0], []
    sub = lax.broadcasted_iota(jnp.int32, (SUBS, LANES), 0)
    ahead = sub.astype(F32) * float(steps)
    for half in range(halves):
        lanes = pl.ds(half * LANES, LANES)
        rates = [row_of(rate_ref, m, lanes) for m in range(modes)]
        retain = [wide(jnp.exp(-x)) for x in rates]
        amp = [wide(row_of(amp_ref, m, lanes)) for m in range(modes)]
        skip = wide(row_of(skip_ref, 0, lanes))
        state = [
            begin_ref[m, :, lanes]
            + jnp.exp(-ahead * rates[m])
            * jnp.where(sub >= 1, row_of(carry.at[1], m, lanes), row_of(carry.at[0], m, lanes))
            for m in range(modes)
        ]
        for step in range(steps):
            at = pl.ds(step, SUBS, stride=steps)
            g = gated_ref[half, at, :]
            query = query_ref[half, at, :]
            if step < taps - 1:
                query = jnp.where(sub >= 1, query, top_ref[0, pl.ds(step, 1), lanes])
                g = jnp.where(sub >= 1, g, top_ref[1, pl.ds(step, 1), lanes])
            state = [a * s + g for a, s in zip(retain, state)]
            terms = [a * s for a, s in zip(amp, state)] + [skip * g]
            while len(terms) > 1:
                terms = [x + y for x, y in zip(terms[::2], terms[1::2])] + terms[len(terms) // 2 * 2 :]
            hyena[half, at, :] = query * terms[0]
        left[:, lanes] = hyena[half].astype(BF16)
        copies += fetch([left.at[:, lanes]] * parts, [out_hbm.at[i, :, lanes] for i in range(parts)], sems.at[half])
    for copy in copies:
        copy.wait()
    own.wait()


def order_body(left_ref, _side, _across, out_ref, _same_side, _same_across):
    parts, _, channels = left_ref.shape
    here = lax.axis_index("tp")
    for d in range(parts):
        out_ref[:, pl.ds(d * channels, channels)] = left_ref[lax.rem(here + parts - d, parts)]


def project_body(left_ref, *rest):
    *rights, out_hbm, done, sems = rest
    blocks, _, block = done.shape
    channels = rights[0].shape[0]
    copies = []
    for b in range(blocks):
        at = pl.ds(b * block, block)
        total = jnp.zeros(done.shape[1:], F32)
        for d, right in enumerate(rights):
            total += jnp.dot(left_ref[:, pl.ds(d * channels, channels)], right[:, at], preferred_element_type=F32)
        done[b] = total.astype(BF16)
        copies.append(pltpu.make_async_copy(done.at[b], out_hbm.at[:, at], sems.at[b]))
        copies[-1].start()
    for copy in copies:
        copy.wait()


def local(query_in, key_in, value_in, short_weight, residue, rate, skip, out_weight):
    rows, channels = query_in.shape
    modes = rate.shape[0]
    taps = short_weight.shape[1]
    planes = lax.axis_size("z")
    plane = lax.axis_size("y") * lax.axis_size("core")
    parts = lax.axis_size("tp")
    width = out_weight.shape[1] // parts
    order = ("z", "y", "core")
    devices = planes * plane
    by_half = (channels // LANES, rows, LANES)
    skip = skip.reshape(1, -1)
    query_in, key_in, value_in, short_weight, residue, rate, skip, out_weight = (
        pltpu.with_memory_space_constraint(x, pltpu.HBM)
        for x in (query_in, key_in, value_in, short_weight, residue, rate, skip, out_weight)
    )
    rims = call(
        rim_body, [HBM] * 3, shape((3 * RIM, channels), BF16), "rims", [pltpu.SemaphoreType.DMA((3,))]
    )(query_in, key_in, value_in)
    rims = lax.ppermute(rims, order, [(i, i + 1) for i in range(devices - 1)])
    queries, gated, begin, states, heads, taps_here, rate, amplitude, skip, *blocks = call(
        gate_body,
        [HBM] * 8,
        (
            shape(by_half, F32),
            shape(by_half, F32),
            shape((modes, SUBS, channels), F32),
            shape((modes, channels), F32),
            shape((3, HEAD, channels), F32),
            shape(short_weight.shape, F32),
            shape((modes, channels), F32),
            shape((modes, channels), F32),
            shape((1, channels), F32),
            *[shape((channels, width), BF16)] * (parts - 1),
        ),
        "gate",
        [
            pltpu.VMEM((3, rows, channels), BF16),
            pltpu.VMEM((modes, channels), F32),
            pltpu.VMEM((3, HEAD + rows, channels), F32),
            pltpu.SemaphoreType.DMA((7 + parts - 1,)),
        ],
    )(query_in, key_in, value_in, short_weight, rate, residue, skip, out_weight)
    def to_next(block, d):
        return lax.ppermute(block, "tp", [(i, (i + d) % parts) for i in range(parts)])

    blocks = [to_next(blocks[0], 1), to_next(blocks[1], 2), blocks[2]]
    states, late, top = call(
        lambda *refs: join_body(rows, *refs),
        [VMEM] * 5,
        (
            shape((plane, modes, channels), BF16),
            shape((modes, channels), F32),
            shape((2, HEAD, channels), F32),
        ),
        "join",
        [
            pltpu.VMEM((3, 2 * HEAD, channels), F32),
            pltpu.VMEM((modes, channels), BF16),
            pltpu.SemaphoreType.DMA((plane,)),
        ],
        out_spec=(HBM, VMEM, VMEM),
    )(rims, heads, taps_here, rate, states)
    states = lax.all_to_all(states, ("y", "core"), 0, 0, tiled=True)
    before, totals, blocks[2] = call(
        lambda *refs: plane_body(rows, *refs),
        [VMEM] * 2 + [ANY],
        (shape((modes, channels), F32), shape((planes, modes, channels), BF16), shape((channels, width), BF16)),
        "plane",
        [pltpu.VMEM((modes, channels), BF16), pltpu.SemaphoreType.DMA((planes,))],
        out_spec=(VMEM, HBM, ANY),
        aliases={2: 2},
    )(states, rate, blocks[2])
    blocks[2] = to_next(blocks[2], 3)
    totals = lax.all_to_all(totals, "z", 0, 0, tiled=True)
    hyena, own = call(
        lambda *refs: mix_body(taps, rows * plane, *refs),
        [VMEM] * 10 + [HBM],
        (shape((parts, rows, channels), BF16), shape((channels, width), BF16)),
        "mix",
        [
            pltpu.VMEM(by_half, F32),
            pltpu.VMEM((rows, channels), BF16),
            pltpu.VMEM((2, modes, channels), F32),
            pltpu.SemaphoreType.DMA,
            pltpu.SemaphoreType.DMA((channels // LANES, parts)),
        ],
        out_spec=(HBM, VMEM),
    )(queries, gated, begin, late, top, before, totals, rate, amplitude, skip, out_weight)
    hyena = lax.all_to_all(hyena, "tp", 0, 0, tiled=True)
    hyena, *blocks[:2] = call(
        order_body,
        [VMEM] + [ANY] * 2,
        (shape((rows, parts * channels), BF16), *[shape((channels, width), BF16)] * 2),
        "order",
        out_spec=(VMEM, ANY, ANY),
        aliases={1: 1, 2: 2},
        us=2,
    )(hyena, *blocks[:2])
    block = 256
    return call(
        project_body,
        [VMEM] * 5,
        shape((rows, width), BF16),
        "project",
        [pltpu.VMEM((width // block, rows, block), BF16), pltpu.SemaphoreType.DMA((width // block,))],
        out_spec=HBM,
    )(hyena, own, *blocks)


def solution(mesh):
    fine = Mesh(mesh.devices.reshape(8, 8, 2, 4), ("z", "y", "core", "tp"))
    seq = ("z", "y", "core")
    in_specs = (
        P(seq, "tp"),
        P(seq, "tp"),
        P(seq, "tp"),
        P(None, None, "tp"),
        P(None, "tp"),
        P(None, "tp"),
        P("tp"),
        P("tp", None),
    )
    return jax.shard_map(local, mesh=fine, in_specs=in_specs, out_specs=P(seq, "tp"), check_vma=False)
```

```python
import jax
import jax.numpy as jnp
from jax import lax
from jax.experimental import pallas as pl
from jax.experimental.pallas import tpu as pltpu
from jax.sharding import Mesh, PartitionSpec as P

F32 = jnp.float32
BF16 = jnp.bfloat16
LANES = 128
SUBS = 8
RIM = 16
HEAD = 8
MIB = 1 << 20
RATE = 1.15e9


def shape(dims, dtype):
    return jax.ShapeDtypeStruct(dims, dtype)


VMEM = pl.BlockSpec(memory_space=pltpu.VMEM)
ANY = pl.BlockSpec(memory_space=pl.ANY)
HBM = pl.BlockSpec(memory_space=pltpu.HBM)


def call(body, specs, outs, name, scratch=(), mib=4, out_spec=VMEM, aliases=None, us=0):
    return pl.pallas_call(
        body,
        in_specs=specs,
        out_specs=out_spec if isinstance(out_spec, tuple) else jax.tree.map(lambda _: out_spec, outs),
        input_output_aliases=aliases or {},
        cost_estimate=pl.CostEstimate(flops=int(us * RATE), bytes_accessed=0, transcendentals=0) if us else None,
        out_shape=outs,
        scratch_shapes=list(scratch),
        compiler_params=pltpu.CompilerParams(vmem_limit_bytes=mib * MIB),
        name=name,
    )


def fetch(sources, targets, sems):
    copies = [pltpu.make_async_copy(s, t, sems.at[i]) for i, (s, t) in enumerate(zip(sources, targets))]
    for copy in copies:
        copy.start()
    return copies


def row_of(ref, m, lanes):
    return ref[pl.ds(m, 1), lanes]


def wide(row):
    return jnp.broadcast_to(row, (SUBS, LANES))


def one_minus_exp(x):
    series = 1.0 / 362880.0
    for n in (40320, 5040, 720, 120, 24, 6, 2, 1):
        series = 1.0 / n - x * series
    return jnp.where(x < 0.25, x * series, 1.0 - jnp.exp(-x))


def rim_body(q_ref, k_ref, v_ref, out_ref, sems):
    rows = q_ref.shape[0]
    refs = (q_ref, k_ref, v_ref)
    copies = fetch(
        [ref.at[pl.ds(rows - RIM, RIM), :] for ref in refs],
        [out_ref.at[pl.ds(i * RIM, RIM), :] for i in range(3)],
        sems,
    )
    for copy in copies:
        copy.wait()


def gate_body(
    q_hbm, k_hbm, v_hbm, taps_hbm, rate_hbm, residue_hbm, skip_hbm, weight_hbm,
    query_ref, gated_ref, begin_ref, state_ref, head_ref, taps_ref, rate_ref, amp_ref, skip_ref, *rest,
):
    *blocks, own_ref, streams, residue_ref, pad, sems = rest
    here, parts = lax.axis_index("tp"), lax.axis_size("tp")
    width = blocks[0].shape[1]
    _, rows, channels = streams.shape
    modes = rate_ref.shape[0]
    taps = taps_ref.shape[1]
    steps = rows // SUBS
    copies = fetch(
        (q_hbm, k_hbm, v_hbm, taps_hbm, rate_hbm, residue_hbm, skip_hbm),
        (streams.at[0], streams.at[1], streams.at[2], taps_ref, rate_ref, residue_ref, skip_ref),
        sems,
    )
    sent = fetch(
        [weight_hbm.at[:, pl.ds(lax.rem(here + d, parts) * width, width)] for d in range(1, parts)],
        blocks,
        sems.at[pl.ds(7, parts - 1)],
    )
    sent += fetch([weight_hbm.at[:, pl.ds(here * width, width)]], [own_ref], sems.at[pl.ds(6 + parts, 1)])
    for copy in copies:
        copy.wait()
    amp_ref[...] = residue_ref[...] * jnp.sqrt(one_minus_exp(2.0 * rate_ref[...]))
    for i in range(3):
        pad[i, pl.ds(0, HEAD), :] = jnp.zeros((HEAD, channels), F32)
        pad[i, pl.ds(HEAD, rows), :] = streams[i].astype(F32)
    block = 32
    for half in range(channels // LANES):
        lanes = pl.ds(half * LANES, LANES)
        for r in range(0, rows, block):
            sums = []
            for i in range(3):
                total = jnp.zeros((block, LANES), F32)
                for t in range(taps):
                    total = total + taps_ref[i, pl.ds(t, 1), lanes] * pad[i, pl.ds(HEAD + r - t, block), lanes]
                sums.append(total)
                if r == 0:
                    head_ref[i, :, lanes] = total[:HEAD]
            query_ref[half, pl.ds(r, block), :] = sums[0]
            gated_ref[half, pl.ds(r, block), :] = sums[1] * sums[2]
    sub = lax.broadcasted_iota(jnp.int32, (SUBS, LANES), 0)
    for half in range(channels // LANES):
        lanes = pl.ds(half * LANES, LANES)
        rates = [row_of(rate_ref, m, lanes) for m in range(modes)]
        retain = [wide(jnp.exp(-x)) for x in rates]
        state = [jnp.zeros((SUBS, LANES), F32) for _ in range(modes)]
        for step in range(steps):
            g = gated_ref[half, pl.ds(step, SUBS, stride=steps), :]
            state = [a * s + g for a, s in zip(retain, state)]
        for m in range(modes):
            s = state[m]
            for d in (1, 2, 4):
                drop = wide(jnp.exp(-(steps * d) * rates[m]))
                s = s + jnp.where(sub >= d, drop * pltpu.roll(s, d, 0), 0.0)
            state_ref[pl.ds(m, 1), lanes] = s[SUBS - 1 :]
            begin_ref[m, :, lanes] = jnp.where(sub >= 1, pltpu.roll(s, 1, 0), 0.0)
    for copy in sent:
        copy.wait()


def join_body(rows, rim_ref, head_ref, taps_ref, rate_ref, state_ref, out_ref, late_ref, top_ref, pad):
    modes, channels = rate_ref.shape
    taps = taps_ref.shape[1]
    sums = []
    for i in range(3):
        pad[i, pl.ds(0, HEAD), :] = rim_ref[pl.ds(i * RIM, RIM), :].astype(F32)[RIM - HEAD :]
        pad[i, pl.ds(HEAD, HEAD), :] = jnp.zeros((HEAD, channels), F32)
        total = head_ref[i]
        for t in range(1, taps):
            total = total + taps_ref[i, pl.ds(t, 1), :] * pad[i, pl.ds(HEAD - t, HEAD), :]
        sums.append(total)
    gated = sums[1] * sums[2]
    top_ref[0] = sums[0]
    top_ref[1] = gated
    more = gated - head_ref[1] * head_ref[2]
    rate = rate_ref[...]
    retain = jnp.exp(-rate)
    late = jnp.broadcast_to(more[:1], rate.shape)
    for i in range(1, taps - 1):
        late = retain * late + more[i : i + 1]
    late_ref[...] = late
    whole = (state_ref[...] + jnp.exp(-(rows - taps + 1) * rate) * late).astype(BF16)
    for i in range(out_ref.shape[0]):
        out_ref[i] = whole


def plane_body(rows, parts_ref, rate_ref, _block, before_ref, total_ref, _same_block):
    me = lax.axis_index("y") * lax.axis_size("core") + lax.axis_index("core")
    drop = jnp.exp(-rows * rate_ref[...])
    before = jnp.zeros(rate_ref.shape, F32)
    total = jnp.zeros(rate_ref.shape, F32)
    for i in range(parts_ref.shape[0]):
        part = parts_ref[i].astype(F32)
        before = jnp.where(i < me, before * drop + part, before)
        total = total * drop + part
    before_ref[...] = before
    for i in range(total_ref.shape[0]):
        total_ref[i] = total.astype(BF16)


def mix(taps, carried, refs, out_hbm, hyena, left, carry, sems):
    query_ref, gated_ref, begin_ref, late_ref, top_ref, rate_ref, amp_ref, skip_ref = refs
    halves, rows, _ = query_ref.shape
    modes = rate_ref.shape[0]
    steps = rows // SUBS
    carry[0] = carried
    carry[1] = carried + jnp.exp((taps - 1) * rate_ref[...]) * late_ref[...]
    parts, copies = out_hbm.shape[0], []
    sub = lax.broadcasted_iota(jnp.int32, (SUBS, LANES), 0)
    ahead = sub.astype(F32) * float(steps)
    for half in range(halves):
        lanes = pl.ds(half * LANES, LANES)
        rates = [row_of(rate_ref, m, lanes) for m in range(modes)]
        retain = [wide(jnp.exp(-x)) for x in rates]
        amp = [wide(row_of(amp_ref, m, lanes)) for m in range(modes)]
        skip = wide(row_of(skip_ref, 0, lanes))
        state = [
            begin_ref[m, :, lanes]
            + jnp.exp(-ahead * rates[m])
            * jnp.where(sub >= 1, row_of(carry.at[1], m, lanes), row_of(carry.at[0], m, lanes))
            for m in range(modes)
        ]
        for step in range(steps):
            at = pl.ds(step, SUBS, stride=steps)
            g = gated_ref[half, at, :]
            query = query_ref[half, at, :]
            if step < taps - 1:
                query = jnp.where(sub >= 1, query, top_ref[0, pl.ds(step, 1), lanes])
                g = jnp.where(sub >= 1, g, top_ref[1, pl.ds(step, 1), lanes])
            state = [a * s + g for a, s in zip(retain, state)]
            terms = [a * s for a, s in zip(amp, state)] + [skip * g]
            while len(terms) > 1:
                terms = [x + y for x, y in zip(terms[::2], terms[1::2])] + terms[len(terms) // 2 * 2 :]
            hyena[half, at, :] = query * terms[0]
        left[:, lanes] = hyena[half].astype(BF16)
        copies += fetch([left.at[:, lanes]] * parts, [out_hbm.at[i, :, lanes] for i in range(parts)], sems.at[half])
    for copy in copies:
        copy.wait()


def plane_body(taps, rows, parts_ref, _block, *refs):
    *refs, before_ref, total_ref, _same_block, out_hbm, hyena, left, carry, sems = refs
    rate_ref = refs[5]
    me = lax.axis_index("y") * lax.axis_size("core") + lax.axis_index("core")
    drop = jnp.exp(-rows * rate_ref[...])
    before = jnp.zeros(rate_ref.shape, F32)
    total = jnp.zeros(rate_ref.shape, F32)
    for i in range(parts_ref.shape[0]):
        part = parts_ref[i].astype(F32)
        before = jnp.where(i < me, before * drop + part, before)
        total = total * drop + part
    before_ref[...] = before
    for i in range(total_ref.shape[0]):
        total_ref[i] = total.astype(BF16)

    @pl.when(lax.axis_index("z") == 0)
    def _():
        mix(taps, before, refs, out_hbm, hyena, left, carry, sems)


def mix_body(taps, plane_rows, before_ref, planes_ref, _hyena, *refs):
    *refs, out_hbm, hyena, left, carry, sems = refs
    query_ref, rate_ref = refs[0], refs[5]
    rows = query_ref.shape[1]
    z = lax.axis_index("z")

    @pl.when(z > 0)
    def _():
        me = lax.axis_index("y") * lax.axis_size("core") + lax.axis_index("core")
        rate = rate_ref[...]
        drop = jnp.exp(-plane_rows * rate)
        behind = jnp.zeros(rate.shape, F32)
        for i in range(planes_ref.shape[0]):
            behind = jnp.where(i < z, behind * drop + planes_ref[i].astype(F32), behind)
        carried = before_ref[...] + jnp.exp(-(rows * me).astype(F32) * rate) * behind
        mix(taps, carried, refs, out_hbm, hyena, left, carry, sems)


def order_body(left_ref, _side, _across, out_ref, _same_side, _same_across):
    parts, _, channels = left_ref.shape
    here = lax.axis_index("tp")
    for d in range(parts):
        out_ref[:, pl.ds(d * channels, channels)] = left_ref[lax.rem(here + parts - d, parts)]


def project_body(left_ref, *rest):
    *rights, out_hbm, done, sems = rest
    blocks, _, block = done.shape
    channels = rights[0].shape[0]
    copies = []
    for b in range(blocks):
        at = pl.ds(b * block, block)
        total = jnp.zeros(done.shape[1:], F32)
        for d, right in enumerate(rights):
            total += jnp.dot(left_ref[:, pl.ds(d * channels, channels)], right[:, at], preferred_element_type=F32)
        done[b] = total.astype(BF16)
        copies.append(pltpu.make_async_copy(done.at[b], out_hbm.at[:, at], sems.at[b]))
        copies[-1].start()
    for copy in copies:
        copy.wait()


def local(query_in, key_in, value_in, short_weight, residue, rate, skip, out_weight):
    rows, channels = query_in.shape
    modes = rate.shape[0]
    taps = short_weight.shape[1]
    planes = lax.axis_size("z")
    plane = lax.axis_size("y") * lax.axis_size("core")
    parts = lax.axis_size("tp")
    width = out_weight.shape[1] // parts
    order = ("z", "y", "core")
    devices = planes * plane
    by_half = (channels // LANES, rows, LANES)
    skip = skip.reshape(1, -1)
    query_in, key_in, value_in, short_weight, residue, rate, skip, out_weight = (
        pltpu.with_memory_space_constraint(x, pltpu.HBM)
        for x in (query_in, key_in, value_in, short_weight, residue, rate, skip, out_weight)
    )
    rims = call(
        rim_body, [HBM] * 3, shape((3 * RIM, channels), BF16), "rims", [pltpu.SemaphoreType.DMA((3,))]
    )(query_in, key_in, value_in)
    rims = lax.ppermute(rims, order, [(i, i + 1) for i in range(devices - 1)])
    queries, gated, begin, states, heads, taps_here, rate, amplitude, skip, *blocks, own = call(
        gate_body,
        [HBM] * 8,
        (
            shape(by_half, F32),
            shape(by_half, F32),
            shape((modes, SUBS, channels), F32),
            shape((modes, channels), F32),
            shape((3, HEAD, channels), F32),
            shape(short_weight.shape, F32),
            shape((modes, channels), F32),
            shape((modes, channels), F32),
            shape((1, channels), F32),
            *[shape((channels, width), BF16)] * (parts - 1),
            pltpu.VMEM((channels, width), BF16),
        ),
        "gate",
        [
            pltpu.VMEM((3, rows, channels), BF16),
            pltpu.VMEM((modes, channels), F32),
            pltpu.VMEM((3, HEAD + rows, channels), F32),
            pltpu.SemaphoreType.DMA((7 + parts,)),
        ],
    )(query_in, key_in, value_in, short_weight, rate, residue, skip, out_weight)
    def to_next(block, d):
        return lax.ppermute(block, "tp", [(i, (i + d) % parts) for i in range(parts)])

    blocks = [to_next(blocks[0], 1), to_next(blocks[1], 2), blocks[2]]
    states, late, top = call(
        lambda *refs: join_body(rows, *refs),
        [VMEM] * 5,
        (
            shape((plane, modes, channels), BF16),
            shape((modes, channels), F32),
            shape((2, HEAD, channels), F32),
        ),
        "join",
        [pltpu.VMEM((3, 2 * HEAD, channels), F32)],
    )(rims, heads, taps_here, rate, states)
    states = lax.all_to_all(states, ("y", "core"), 0, 0, tiled=True)
    shared = (queries, gated, begin, late, top, rate, amplitude, skip)
    scratch = [
        pltpu.VMEM(by_half, F32),
        pltpu.VMEM((rows, channels), BF16),
        pltpu.VMEM((2, modes, channels), F32),
        pltpu.SemaphoreType.DMA((channels // LANES, parts)),
    ]
    before, totals, blocks[2], hyena = call(
        lambda *refs: plane_body(taps, rows, *refs),
        [VMEM, ANY] + [VMEM] * len(shared),
        (
            shape((modes, channels), F32),
            shape((planes, modes, channels), BF16),
            shape((channels, width), BF16),
            pltpu.HBM((parts, rows, channels), BF16),
        ),
        "plane",
        scratch,
        out_spec=(VMEM, VMEM, ANY, HBM),
        aliases={1: 2},
    )(states, blocks[2], *shared)
    blocks[2] = to_next(blocks[2], 3)
    totals = lax.all_to_all(totals, "z", 0, 0, tiled=True)
    hyena = call(
        lambda *refs: mix_body(taps, rows * plane, *refs),
        [VMEM] * 2 + [HBM] + [VMEM] * len(shared),
        pltpu.HBM((parts, rows, channels), BF16),
        "mix",
        scratch,
        out_spec=HBM,
        aliases={2: 0},
    )(before, totals, hyena, *shared)
    hyena = lax.all_to_all(hyena, "tp", 0, 0, tiled=True)
    hyena, *blocks[:2] = call(
        order_body,
        [VMEM] + [ANY] * 2,
        (shape((rows, parts * channels), BF16), *[shape((channels, width), BF16)] * 2),
        "order",
        out_spec=(VMEM, ANY, ANY),
        aliases={1: 1, 2: 2},
        us=2,
    )(hyena, *blocks[:2])
    block = 256
    return call(
        project_body,
        [VMEM] * 5,
        shape((rows, width), BF16),
        "project",
        [pltpu.VMEM((width // block, rows, block), BF16), pltpu.SemaphoreType.DMA((width // block,))],
        out_spec=HBM,
    )(hyena, own, *blocks)


def solution(mesh):
    fine = Mesh(mesh.devices.reshape(8, 8, 2, 4), ("z", "y", "core", "tp"))
    seq = ("z", "y", "core")
    in_specs = (
        P(seq, "tp"),
        P(seq, "tp"),
        P(seq, "tp"),
        P(None, None, "tp"),
        P(None, "tp"),
        P(None, "tp"),
        P("tp"),
        P("tp", None),
    )
    return jax.shard_map(local, mesh=fine, in_specs=in_specs, out_specs=P(seq, "tp"), check_vma=False)
```

```python
import jax
import jax.numpy as jnp
from jax import lax
from jax.experimental import pallas as pl
from jax.experimental.pallas import tpu as pltpu
from jax.sharding import Mesh, PartitionSpec as P

F32 = jnp.float32
BF16 = jnp.bfloat16
LANES = 128
SUBS = 8
RIM = 16
HEAD = 8
MIB = 1 << 20
RATE = 1.15e9


def shape(dims, dtype):
    return jax.ShapeDtypeStruct(dims, dtype)


VMEM = pl.BlockSpec(memory_space=pltpu.VMEM)
ANY = pl.BlockSpec(memory_space=pl.ANY)
HBM = pl.BlockSpec(memory_space=pltpu.HBM)


def call(body, specs, outs, name, scratch=(), mib=4, out_spec=VMEM, aliases=None, us=0):
    return pl.pallas_call(
        body,
        in_specs=specs,
        out_specs=out_spec if isinstance(out_spec, tuple) else jax.tree.map(lambda _: out_spec, outs),
        input_output_aliases=aliases or {},
        cost_estimate=pl.CostEstimate(flops=int(us * RATE), bytes_accessed=0, transcendentals=0) if us else None,
        out_shape=outs,
        scratch_shapes=list(scratch),
        compiler_params=pltpu.CompilerParams(vmem_limit_bytes=mib * MIB),
        name=name,
    )


def fetch(sources, targets, sems):
    copies = [pltpu.make_async_copy(s, t, sems.at[i]) for i, (s, t) in enumerate(zip(sources, targets))]
    for copy in copies:
        copy.start()
    return copies


def row_of(ref, m, lanes):
    return ref[pl.ds(m, 1), lanes]


def wide(row):
    return jnp.broadcast_to(row, (SUBS, LANES))


def one_minus_exp(x):
    series = 1.0 / 362880.0
    for n in (40320, 5040, 720, 120, 24, 6, 2, 1):
        series = 1.0 / n - x * series
    return jnp.where(x < 0.25, x * series, 1.0 - jnp.exp(-x))


def rim_body(q_ref, k_ref, v_ref, out_ref, sems):
    rows = q_ref.shape[0]
    refs = (q_ref, k_ref, v_ref)
    copies = fetch(
        [ref.at[pl.ds(rows - RIM, RIM), :] for ref in refs],
        [out_ref.at[pl.ds(i * RIM, RIM), :] for i in range(3)],
        sems,
    )
    for copy in copies:
        copy.wait()


def gate_body(
    q_hbm, k_hbm, v_hbm, taps_hbm, rate_hbm, residue_hbm, skip_hbm, weight_hbm,
    query_ref, gated_ref, begin_ref, state_ref, head_ref, taps_ref, rate_ref, amp_ref, skip_ref, *rest,
):
    *blocks, own_ref, streams, residue_ref, pad, sems = rest
    here, parts = lax.axis_index("tp"), lax.axis_size("tp")
    width = blocks[0].shape[1]
    _, rows, channels = streams.shape
    modes = rate_ref.shape[0]
    taps = taps_ref.shape[1]
    steps = rows // SUBS
    copies = fetch(
        (q_hbm, k_hbm, v_hbm, taps_hbm, rate_hbm, residue_hbm, skip_hbm),
        (streams.at[0], streams.at[1], streams.at[2], taps_ref, rate_ref, residue_ref, skip_ref),
        sems,
    )
    core = lax.axis_index("core")
    height = blocks[1].shape[0]
    side = lax.rem(here + jnp.where(core == 0, 1, parts - 1), parts)
    sent = fetch(
        (
            weight_hbm.at[:, pl.ds(pl.multiple_of(side * width, LANES), width)],
            weight_hbm.at[
                pl.ds(pl.multiple_of(core * height, height), height),
                pl.ds(pl.multiple_of(lax.rem(here + 2, parts) * width, LANES), width),
            ],
        ),
        blocks,
        sems.at[pl.ds(7, 2)],
    )
    sent += fetch([weight_hbm.at[:, pl.ds(here * width, width)]], [own_ref], sems.at[pl.ds(9, 1)])
    for copy in copies:
        copy.wait()
    amp_ref[...] = residue_ref[...] * jnp.sqrt(one_minus_exp(2.0 * rate_ref[...]))
    for i in range(3):
        pad[i, pl.ds(0, HEAD), :] = jnp.zeros((HEAD, channels), F32)
        pad[i, pl.ds(HEAD, rows), :] = streams[i].astype(F32)
    block = 32
    for half in range(channels // LANES):
        lanes = pl.ds(half * LANES, LANES)
        for r in range(0, rows, block):
            sums = []
            for i in range(3):
                total = jnp.zeros((block, LANES), F32)
                for t in range(taps):
                    total = total + taps_ref[i, pl.ds(t, 1), lanes] * pad[i, pl.ds(HEAD + r - t, block), lanes]
                sums.append(total)
                if r == 0:
                    head_ref[i, :, lanes] = total[:HEAD]
            query_ref[half, pl.ds(r, block), :] = sums[0]
            gated_ref[half, pl.ds(r, block), :] = sums[1] * sums[2]
    sub = lax.broadcasted_iota(jnp.int32, (SUBS, LANES), 0)
    for half in range(channels // LANES):
        lanes = pl.ds(half * LANES, LANES)
        rates = [row_of(rate_ref, m, lanes) for m in range(modes)]
        retain = [wide(jnp.exp(-x)) for x in rates]
        state = [jnp.zeros((SUBS, LANES), F32) for _ in range(modes)]
        for step in range(steps):
            g = gated_ref[half, pl.ds(step, SUBS, stride=steps), :]
            state = [a * s + g for a, s in zip(retain, state)]
        for m in range(modes):
            s = state[m]
            for d in (1, 2, 4):
                drop = wide(jnp.exp(-(steps * d) * rates[m]))
                s = s + jnp.where(sub >= d, drop * pltpu.roll(s, d, 0), 0.0)
            state_ref[pl.ds(m, 1), lanes] = s[SUBS - 1 :]
            begin_ref[m, :, lanes] = jnp.where(sub >= 1, pltpu.roll(s, 1, 0), 0.0)
    for copy in sent:
        copy.wait()


def join_body(rows, rim_ref, head_ref, taps_ref, rate_ref, state_ref, out_ref, late_ref, top_ref, pad):
    modes, channels = rate_ref.shape
    taps = taps_ref.shape[1]
    sums = []
    for i in range(3):
        pad[i, pl.ds(0, HEAD), :] = rim_ref[pl.ds(i * RIM, RIM), :].astype(F32)[RIM - HEAD :]
        pad[i, pl.ds(HEAD, HEAD), :] = jnp.zeros((HEAD, channels), F32)
        total = head_ref[i]
        for t in range(1, taps):
            total = total + taps_ref[i, pl.ds(t, 1), :] * pad[i, pl.ds(HEAD - t, HEAD), :]
        sums.append(total)
    gated = sums[1] * sums[2]
    top_ref[0] = sums[0]
    top_ref[1] = gated
    more = gated - head_ref[1] * head_ref[2]
    rate = rate_ref[...]
    retain = jnp.exp(-rate)
    late = jnp.broadcast_to(more[:1], rate.shape)
    for i in range(1, taps - 1):
        late = retain * late + more[i : i + 1]
    late_ref[...] = late
    whole = (state_ref[...] + jnp.exp(-(rows - taps + 1) * rate) * late).astype(BF16)
    for i in range(out_ref.shape[0]):
        out_ref[i] = whole


def plane_body(rows, parts_ref, rate_ref, _block, before_ref, total_ref, _same_block):
    me = lax.axis_index("y") * lax.axis_size("core") + lax.axis_index("core")
    drop = jnp.exp(-rows * rate_ref[...])
    before = jnp.zeros(rate_ref.shape, F32)
    total = jnp.zeros(rate_ref.shape, F32)
    for i in range(parts_ref.shape[0]):
        part = parts_ref[i].astype(F32)
        before = jnp.where(i < me, before * drop + part, before)
        total = total * drop + part
    before_ref[...] = before
    for i in range(total_ref.shape[0]):
        total_ref[i] = total.astype(BF16)


def mix(taps, carried, refs, out_hbm, hyena, left, carry, sems):
    query_ref, gated_ref, begin_ref, late_ref, top_ref, rate_ref, amp_ref, skip_ref = refs
    halves, rows, _ = query_ref.shape
    modes = rate_ref.shape[0]
    steps = rows // SUBS
    carry[0] = carried
    carry[1] = carried + jnp.exp((taps - 1) * rate_ref[...]) * late_ref[...]
    parts, copies = out_hbm.shape[0], []
    sub = lax.broadcasted_iota(jnp.int32, (SUBS, LANES), 0)
    ahead = sub.astype(F32) * float(steps)
    for half in range(halves):
        lanes = pl.ds(half * LANES, LANES)
        rates = [row_of(rate_ref, m, lanes) for m in range(modes)]
        retain = [wide(jnp.exp(-x)) for x in rates]
        amp = [wide(row_of(amp_ref, m, lanes)) for m in range(modes)]
        skip = wide(row_of(skip_ref, 0, lanes))
        state = [
            begin_ref[m, :, lanes]
            + jnp.exp(-ahead * rates[m])
            * jnp.where(sub >= 1, row_of(carry.at[1], m, lanes), row_of(carry.at[0], m, lanes))
            for m in range(modes)
        ]
        for step in range(steps):
            at = pl.ds(step, SUBS, stride=steps)
            g = gated_ref[half, at, :]
            query = query_ref[half, at, :]
            if step < taps - 1:
                query = jnp.where(sub >= 1, query, top_ref[0, pl.ds(step, 1), lanes])
                g = jnp.where(sub >= 1, g, top_ref[1, pl.ds(step, 1), lanes])
            state = [a * s + g for a, s in zip(retain, state)]
            terms = [a * s for a, s in zip(amp, state)] + [skip * g]
            while len(terms) > 1:
                terms = [x + y for x, y in zip(terms[::2], terms[1::2])] + terms[len(terms) // 2 * 2 :]
            hyena[half, at, :] = query * terms[0]
        left[:, lanes] = hyena[half].astype(BF16)
        copies += fetch([left.at[:, lanes]] * parts, [out_hbm.at[i, :, lanes] for i in range(parts)], sems.at[half])
    for copy in copies:
        copy.wait()


def plane_body(taps, rows, parts_ref, *refs):
    *refs, before_ref, total_ref, out_hbm, hyena, left, carry, sems = refs
    rate_ref = refs[5]
    me = lax.axis_index("y") * lax.axis_size("core") + lax.axis_index("core")
    drop = jnp.exp(-rows * rate_ref[...])
    before = jnp.zeros(rate_ref.shape, F32)
    total = jnp.zeros(rate_ref.shape, F32)
    for i in range(parts_ref.shape[0]):
        part = parts_ref[i].astype(F32)
        before = jnp.where(i < me, before * drop + part, before)
        total = total * drop + part
    before_ref[...] = before
    for i in range(total_ref.shape[0]):
        total_ref[i] = total.astype(BF16)

    @pl.when(lax.axis_index("z") == 0)
    def _():
        mix(taps, before, refs, out_hbm, hyena, left, carry, sems)


def mix_body(taps, plane_rows, before_ref, planes_ref, _hyena, _side, _half, *refs):
    *refs, out_hbm, _same_side, _same_half, hyena, left, carry, sems = refs
    query_ref, rate_ref = refs[0], refs[5]
    rows = query_ref.shape[1]
    z = lax.axis_index("z")

    @pl.when(z > 0)
    def _():
        me = lax.axis_index("y") * lax.axis_size("core") + lax.axis_index("core")
        rate = rate_ref[...]
        drop = jnp.exp(-plane_rows * rate)
        behind = jnp.zeros(rate.shape, F32)
        for i in range(planes_ref.shape[0]):
            behind = jnp.where(i < z, behind * drop + planes_ref[i].astype(F32), behind)
        carried = before_ref[...] + jnp.exp(-(rows * me).astype(F32) * rate) * behind
        mix(taps, carried, refs, out_hbm, hyena, left, carry, sems)


def order_body(left_ref, out_ref):
    parts, _, channels = left_ref.shape
    here, core = lax.axis_index("tp"), lax.axis_index("core")
    ahead, behind = lax.rem(here + 1, parts), lax.rem(here + parts - 1, parts)
    across = lax.rem(here + 2, parts)
    height = channels // 2
    out_ref[:, :channels] = left_ref[here]
    out_ref[:, channels : 2 * channels] = left_ref[jnp.where(core == 0, behind, ahead)]
    out_ref[:, 2 * channels : 3 * channels] = left_ref[jnp.where(core == 0, ahead, behind)]
    for i, half in enumerate((core, 1 - core)):
        columns = pl.ds(pl.multiple_of(half * height, height), height)
        out_ref[:, pl.ds(3 * channels + i * height, height)] = left_ref[across, :, columns]


def project_body(left_ref, *rest):
    *rights, out_hbm, done, sems = rest
    blocks, _, block = done.shape
    copies = []
    for b in range(blocks):
        at = pl.ds(b * block, block)
        total = jnp.zeros(done.shape[1:], F32)
        begin = 0
        for right in rights:
            depth = right.shape[0]
            total += jnp.dot(left_ref[:, pl.ds(begin, depth)], right[:, at], preferred_element_type=F32)
            begin += depth
        done[b] = total.astype(BF16)
        copies.append(pltpu.make_async_copy(done.at[b], out_hbm.at[:, at], sems.at[b]))
        copies[-1].start()
    for copy in copies:
        copy.wait()


def local(query_in, key_in, value_in, short_weight, residue, rate, skip, out_weight):
    rows, channels = query_in.shape
    modes = rate.shape[0]
    taps = short_weight.shape[1]
    planes = lax.axis_size("z")
    plane = lax.axis_size("y") * lax.axis_size("core")
    parts = lax.axis_size("tp")
    width = out_weight.shape[1] // parts
    order = ("z", "y", "core")
    devices = planes * plane
    by_half = (channels // LANES, rows, LANES)
    skip = skip.reshape(1, -1)
    query_in, key_in, value_in, short_weight, residue, rate, skip, out_weight = (
        pltpu.with_memory_space_constraint(x, pltpu.HBM)
        for x in (query_in, key_in, value_in, short_weight, residue, rate, skip, out_weight)
    )
    rims = call(
        rim_body, [HBM] * 3, shape((3 * RIM, channels), BF16), "rims", [pltpu.SemaphoreType.DMA((3,))]
    )(query_in, key_in, value_in)
    rims = lax.ppermute(rims, order, [(i, i + 1) for i in range(devices - 1)])
    queries, gated, begin, states, heads, taps_here, rate, amplitude, skip, *blocks, own = call(
        gate_body,
        [HBM] * 8,
        (
            shape(by_half, F32),
            shape(by_half, F32),
            shape((modes, SUBS, channels), F32),
            shape((modes, channels), F32),
            shape((3, HEAD, channels), F32),
            shape(short_weight.shape, F32),
            shape((modes, channels), F32),
            shape((modes, channels), F32),
            shape((1, channels), F32),
            shape((channels, width), BF16),
            shape((channels // 2, width), BF16),
            pltpu.VMEM((channels, width), BF16),
        ),
        "gate",
        [
            pltpu.VMEM((3, rows, channels), BF16),
            pltpu.VMEM((modes, channels), F32),
            pltpu.VMEM((3, HEAD + rows, channels), F32),
            pltpu.SemaphoreType.DMA((10,)),
        ],
    )(query_in, key_in, value_in, short_weight, rate, residue, skip, out_weight)
    side, half = blocks
    side = lax.ppermute(
        side,
        ("core", "tp"),
        [(c * parts + t, c * parts + (t + 1 - 2 * c) % parts) for c in range(2) for t in range(parts)],
    )
    half = lax.ppermute(half, "tp", [(t, (t + 2) % parts) for t in range(parts)])
    states, late, top = call(
        lambda *refs: join_body(rows, *refs),
        [VMEM] * 5,
        (
            shape((plane, modes, channels), BF16),
            shape((modes, channels), F32),
            shape((2, HEAD, channels), F32),
        ),
        "join",
        [pltpu.VMEM((3, 2 * HEAD, channels), F32)],
    )(rims, heads, taps_here, rate, states)
    states = lax.all_to_all(states, ("y", "core"), 0, 0, tiled=True)
    shared = (queries, gated, begin, late, top, rate, amplitude, skip)
    scratch = [
        pltpu.VMEM(by_half, F32),
        pltpu.VMEM((rows, channels), BF16),
        pltpu.VMEM((2, modes, channels), F32),
        pltpu.SemaphoreType.DMA((channels // LANES, parts)),
    ]
    before, totals, hyena = call(
        lambda *refs: plane_body(taps, rows, *refs),
        [VMEM] * (1 + len(shared)),
        (
            shape((modes, channels), F32),
            shape((planes, modes, channels), BF16),
            pltpu.HBM((parts, rows, channels), BF16),
        ),
        "plane",
        scratch,
        out_spec=(VMEM, VMEM, HBM),
        us=2,
    )(states, *shared)
    totals = lax.all_to_all(totals, "z", 0, 0, tiled=True)
    hyena, side, half = call(
        lambda *refs: mix_body(taps, rows * plane, *refs),
        [VMEM] * 2 + [HBM] + [ANY] * 2 + [VMEM] * len(shared),
        (pltpu.HBM((parts, rows, channels), BF16), shape(side.shape, BF16), shape(half.shape, BF16)),
        "mix",
        scratch,
        out_spec=(HBM, ANY, ANY),
        aliases={2: 0, 3: 1, 4: 2},
    )(before, totals, hyena, side, half, *shared)
    swapped = [lax.ppermute(x, "core", [(0, 1), (1, 0)]) for x in (side, half)]
    hyena = lax.all_to_all(hyena, "tp", 0, 0, tiled=True)
    hyena = call(order_body, [VMEM], shape((rows, parts * channels), BF16), "order", us=4)(hyena)
    block = 256
    return call(
        project_body,
        [VMEM] * 6,
        shape((rows, width), BF16),
        "project",
        [pltpu.VMEM((width // block, rows, block), BF16), pltpu.SemaphoreType.DMA((width // block,))],
        out_spec=HBM,
    )(hyena, own, side, swapped[0], half, swapped[1])


def solution(mesh):
    fine = Mesh(mesh.devices.reshape(8, 8, 2, 4), ("z", "y", "core", "tp"))
    seq = ("z", "y", "core")
    in_specs = (
        P(seq, "tp"),
        P(seq, "tp"),
        P(seq, "tp"),
        P(None, None, "tp"),
        P(None, "tp"),
        P(None, "tp"),
        P("tp"),
        P("tp", None),
    )
    return jax.shard_map(local, mesh=fine, in_specs=in_specs, out_specs=P(seq, "tp"), check_vma=False)
```

```python
import jax
import jax.numpy as jnp
from jax import lax
from jax.experimental import pallas as pl
from jax.experimental.pallas import tpu as pltpu
from jax.sharding import Mesh, PartitionSpec as P

F32 = jnp.float32
BF16 = jnp.bfloat16
LANES = 128
SUBS = 8
RIM = 16
HEAD = 8
MIB = 1 << 20
RATE = 1.15e9


def shape(dims, dtype):
    return jax.ShapeDtypeStruct(dims, dtype)


VMEM = pl.BlockSpec(memory_space=pltpu.VMEM)
ANY = pl.BlockSpec(memory_space=pl.ANY)
HBM = pl.BlockSpec(memory_space=pltpu.HBM)


def call(body, specs, outs, name, scratch=(), mib=4, out_spec=VMEM, aliases=None, us=0):
    return pl.pallas_call(
        body,
        in_specs=specs,
        out_specs=out_spec if isinstance(out_spec, tuple) else jax.tree.map(lambda _: out_spec, outs),
        input_output_aliases=aliases or {},
        cost_estimate=pl.CostEstimate(flops=int(us * RATE), bytes_accessed=0, transcendentals=0) if us else None,
        out_shape=outs,
        scratch_shapes=list(scratch),
        compiler_params=pltpu.CompilerParams(vmem_limit_bytes=mib * MIB),
        name=name,
    )


def fetch(sources, targets, sems):
    copies = [pltpu.make_async_copy(s, t, sems.at[i]) for i, (s, t) in enumerate(zip(sources, targets))]
    for copy in copies:
        copy.start()
    return copies


def row_of(ref, m, lanes):
    return ref[pl.ds(m, 1), lanes]


def wide(row):
    return jnp.broadcast_to(row, (SUBS, LANES))


def one_minus_exp(x):
    series = 1.0 / 362880.0
    for n in (40320, 5040, 720, 120, 24, 6, 2, 1):
        series = 1.0 / n - x * series
    return jnp.where(x < 0.25, x * series, 1.0 - jnp.exp(-x))


def rim_body(q_ref, k_ref, v_ref, out_ref, sems):
    rows = q_ref.shape[0]
    refs = (q_ref, k_ref, v_ref)
    copies = fetch(
        [ref.at[pl.ds(rows - RIM, RIM), :] for ref in refs],
        [out_ref.at[pl.ds(i * RIM, RIM), :] for i in range(3)],
        sems,
    )
    for copy in copies:
        copy.wait()


def gate_body(
    q_hbm, k_hbm, v_hbm, taps_hbm, rate_hbm, residue_hbm, skip_hbm, weight_hbm,
    query_ref, gated_ref, begin_ref, state_ref, head_ref, taps_ref, rate_ref, amp_ref, skip_ref, *rest,
):
    *blocks, own_ref, streams, residue_ref, pad, sems = rest
    here, parts = lax.axis_index("tp"), lax.axis_size("tp")
    width = blocks[0].shape[1]
    _, rows, channels = streams.shape
    modes = rate_ref.shape[0]
    taps = taps_ref.shape[1]
    steps = rows // SUBS
    copies = fetch(
        (q_hbm, k_hbm, v_hbm, taps_hbm, rate_hbm, residue_hbm, skip_hbm),
        (streams.at[0], streams.at[1], streams.at[2], taps_ref, rate_ref, residue_ref, skip_ref),
        sems,
    )
    core = lax.axis_index("core")
    height = blocks[1].shape[0]
    side = lax.rem(here + jnp.where(core == 0, 1, parts - 1), parts)
    sent = fetch(
        (
            weight_hbm.at[:, pl.ds(pl.multiple_of(side * width, LANES), width)],
            weight_hbm.at[
                pl.ds(pl.multiple_of(core * height, height), height),
                pl.ds(pl.multiple_of(lax.rem(here + 2, parts) * width, LANES), width),
            ],
        ),
        blocks,
        sems.at[pl.ds(7, 2)],
    )
    sent += fetch([weight_hbm.at[:, pl.ds(here * width, width)]], [own_ref], sems.at[pl.ds(9, 1)])
    for copy in copies:
        copy.wait()
    amp_ref[...] = residue_ref[...] * jnp.sqrt(one_minus_exp(2.0 * rate_ref[...]))
    for i in range(3):
        pad[i, pl.ds(0, HEAD), :] = jnp.zeros((HEAD, channels), F32)
        pad[i, pl.ds(HEAD, rows), :] = streams[i].astype(F32)
    block = 32
    for half in range(channels // LANES):
        lanes = pl.ds(half * LANES, LANES)
        for r in range(0, rows, block):
            sums = []
            for i in range(3):
                total = jnp.zeros((block, LANES), F32)
                for t in range(taps):
                    total = total + taps_ref[i, pl.ds(t, 1), lanes] * pad[i, pl.ds(HEAD + r - t, block), lanes]
                sums.append(total)
                if r == 0:
                    head_ref[i, :, lanes] = total[:HEAD]
            query_ref[half, pl.ds(r, block), :] = sums[0]
            gated_ref[half, pl.ds(r, block), :] = sums[1] * sums[2]
    sub = lax.broadcasted_iota(jnp.int32, (SUBS, LANES), 0)
    for half in range(channels // LANES):
        lanes = pl.ds(half * LANES, LANES)
        rates = [row_of(rate_ref, m, lanes) for m in range(modes)]
        retain = [wide(jnp.exp(-x)) for x in rates]
        state = [jnp.zeros((SUBS, LANES), F32) for _ in range(modes)]
        for step in range(steps):
            g = gated_ref[half, pl.ds(step, SUBS, stride=steps), :]
            state = [a * s + g for a, s in zip(retain, state)]
        for m in range(modes):
            s = state[m]
            for d in (1, 2, 4):
                drop = wide(jnp.exp(-(steps * d) * rates[m]))
                s = s + jnp.where(sub >= d, drop * pltpu.roll(s, d, 0), 0.0)
            state_ref[pl.ds(m, 1), lanes] = s[SUBS - 1 :]
            begin_ref[m, :, lanes] = jnp.where(sub >= 1, pltpu.roll(s, 1, 0), 0.0)
    for copy in sent:
        copy.wait()


def join_body(rows, rim_ref, head_ref, taps_ref, rate_ref, state_ref, out_ref, late_ref, top_ref, pad):
    modes, channels = rate_ref.shape
    taps = taps_ref.shape[1]
    sums = []
    for i in range(3):
        pad[i, pl.ds(0, HEAD), :] = rim_ref[pl.ds(i * RIM, RIM), :].astype(F32)[RIM - HEAD :]
        pad[i, pl.ds(HEAD, HEAD), :] = jnp.zeros((HEAD, channels), F32)
        total = head_ref[i]
        for t in range(1, taps):
            total = total + taps_ref[i, pl.ds(t, 1), :] * pad[i, pl.ds(HEAD - t, HEAD), :]
        sums.append(total)
    gated = sums[1] * sums[2]
    top_ref[0] = sums[0]
    top_ref[1] = gated
    more = gated - head_ref[1] * head_ref[2]
    rate = rate_ref[...]
    retain = jnp.exp(-rate)
    late = jnp.broadcast_to(more[:1], rate.shape)
    for i in range(1, taps - 1):
        late = retain * late + more[i : i + 1]
    late_ref[...] = late
    whole = (state_ref[...] + jnp.exp(-(rows - taps + 1) * rate) * late).astype(BF16)
    for i in range(out_ref.shape[0]):
        out_ref[i] = whole


def plane_body(rows, parts_ref, rate_ref, _block, before_ref, total_ref, _same_block):
    me = lax.axis_index("y") * lax.axis_size("core") + lax.axis_index("core")
    drop = jnp.exp(-rows * rate_ref[...])
    before = jnp.zeros(rate_ref.shape, F32)
    total = jnp.zeros(rate_ref.shape, F32)
    for i in range(parts_ref.shape[0]):
        part = parts_ref[i].astype(F32)
        before = jnp.where(i < me, before * drop + part, before)
        total = total * drop + part
    before_ref[...] = before
    for i in range(total_ref.shape[0]):
        total_ref[i] = total.astype(BF16)


def mix(taps, carried, refs, out_hbm, hyena, left, carry, sems):
    query_ref, gated_ref, begin_ref, late_ref, top_ref, rate_ref, amp_ref, skip_ref = refs
    halves, rows, _ = query_ref.shape
    modes = rate_ref.shape[0]
    steps = rows // SUBS
    carry[0] = carried
    carry[1] = carried + jnp.exp((taps - 1) * rate_ref[...]) * late_ref[...]
    parts, copies = out_hbm.shape[0], []
    sub = lax.broadcasted_iota(jnp.int32, (SUBS, LANES), 0)
    ahead = sub.astype(F32) * float(steps)
    for half in range(halves):
        lanes = pl.ds(half * LANES, LANES)
        rates = [row_of(rate_ref, m, lanes) for m in range(modes)]
        retain = [wide(jnp.exp(-x)) for x in rates]
        amp = [wide(row_of(amp_ref, m, lanes)) for m in range(modes)]
        skip = wide(row_of(skip_ref, 0, lanes))
        state = [
            begin_ref[m, :, lanes]
            + jnp.exp(-ahead * rates[m])
            * jnp.where(sub >= 1, row_of(carry.at[1], m, lanes), row_of(carry.at[0], m, lanes))
            for m in range(modes)
        ]
        for step in range(steps):
            at = pl.ds(step, SUBS, stride=steps)
            g = gated_ref[half, at, :]
            query = query_ref[half, at, :]
            if step < taps - 1:
                query = jnp.where(sub >= 1, query, top_ref[0, pl.ds(step, 1), lanes])
                g = jnp.where(sub >= 1, g, top_ref[1, pl.ds(step, 1), lanes])
            state = [a * s + g for a, s in zip(retain, state)]
            terms = [a * s for a, s in zip(amp, state)] + [skip * g]
            while len(terms) > 1:
                terms = [x + y for x, y in zip(terms[::2], terms[1::2])] + terms[len(terms) // 2 * 2 :]
            hyena[half, at, :] = query * terms[0]
        left[:, lanes] = hyena[half].astype(BF16)
        copies += fetch([left.at[:, lanes]] * parts, [out_hbm.at[i, :, lanes] for i in range(parts)], sems.at[half])
    for copy in copies:
        copy.wait()


def plane_body(taps, rows, parts_ref, *refs):
    *refs, before_ref, total_ref, out_hbm, hyena, left, carry, sems = refs
    rate_ref = refs[5]
    me = lax.axis_index("y") * lax.axis_size("core") + lax.axis_index("core")
    drop = jnp.exp(-rows * rate_ref[...])
    before = jnp.zeros(rate_ref.shape, F32)
    total = jnp.zeros(rate_ref.shape, F32)
    for i in range(parts_ref.shape[0]):
        part = parts_ref[i].astype(F32)
        before = jnp.where(i < me, before * drop + part, before)
        total = total * drop + part
    before_ref[...] = before
    for i in range(total_ref.shape[0]):
        total_ref[i] = total.astype(BF16)

    @pl.when(lax.axis_index("z") == 0)
    def _():
        mix(taps, before, refs, out_hbm, hyena, left, carry, sems)


def mix_body(taps, plane_rows, before_ref, planes_ref, _hyena, _half, *refs):
    *refs, out_hbm, _same_half, hyena, left, carry, sems = refs
    query_ref, rate_ref = refs[0], refs[5]
    rows = query_ref.shape[1]
    z = lax.axis_index("z")

    @pl.when(z > 0)
    def _():
        me = lax.axis_index("y") * lax.axis_size("core") + lax.axis_index("core")
        rate = rate_ref[...]
        drop = jnp.exp(-plane_rows * rate)
        behind = jnp.zeros(rate.shape, F32)
        for i in range(planes_ref.shape[0]):
            behind = jnp.where(i < z, behind * drop + planes_ref[i].astype(F32), behind)
        carried = before_ref[...] + jnp.exp(-(rows * me).astype(F32) * rate) * behind
        mix(taps, carried, refs, out_hbm, hyena, left, carry, sems)


def order_body(left_ref, out_ref):
    parts, _, channels = left_ref.shape
    here, core = lax.axis_index("tp"), lax.axis_index("core")
    ahead, behind = lax.rem(here + 1, parts), lax.rem(here + parts - 1, parts)
    across = lax.rem(here + 2, parts)
    height = channels // 2
    out_ref[:, :channels] = left_ref[here]
    out_ref[:, channels : 2 * channels] = left_ref[jnp.where(core == 0, behind, ahead)]
    out_ref[:, 2 * channels : 3 * channels] = left_ref[jnp.where(core == 0, ahead, behind)]
    for i, half in enumerate((core, 1 - core)):
        columns = pl.ds(pl.multiple_of(half * height, height), height)
        out_ref[:, pl.ds(3 * channels + i * height, height)] = left_ref[across, :, columns]


def project_body(left_ref, *rest):
    *rights, out_hbm, done, sems = rest
    blocks, _, block = done.shape
    copies = []
    for b in range(blocks):
        at = pl.ds(b * block, block)
        total = jnp.zeros(done.shape[1:], F32)
        begin = 0
        for right in rights:
            depth = right.shape[0]
            total += jnp.dot(left_ref[:, pl.ds(begin, depth)], right[:, at], preferred_element_type=F32)
            begin += depth
        done[b] = total.astype(BF16)
        copies.append(pltpu.make_async_copy(done.at[b], out_hbm.at[:, at], sems.at[b]))
        copies[-1].start()
    for copy in copies:
        copy.wait()


def local(query_in, key_in, value_in, short_weight, residue, rate, skip, out_weight):
    rows, channels = query_in.shape
    modes = rate.shape[0]
    taps = short_weight.shape[1]
    planes = lax.axis_size("z")
    plane = lax.axis_size("y") * lax.axis_size("core")
    parts = lax.axis_size("tp")
    width = out_weight.shape[1] // parts
    order = ("z", "y", "core")
    devices = planes * plane
    by_half = (channels // LANES, rows, LANES)
    skip = skip.reshape(1, -1)
    query_in, key_in, value_in, short_weight, residue, rate, skip, out_weight = (
        pltpu.with_memory_space_constraint(x, pltpu.HBM)
        for x in (query_in, key_in, value_in, short_weight, residue, rate, skip, out_weight)
    )
    rims = call(
        rim_body, [HBM] * 3, shape((3 * RIM, channels), BF16), "rims", [pltpu.SemaphoreType.DMA((3,))]
    )(query_in, key_in, value_in)
    rims = lax.ppermute(rims, order, [(i, i + 1) for i in range(devices - 1)])
    queries, gated, begin, states, heads, taps_here, rate, amplitude, skip, *blocks, own = call(
        gate_body,
        [HBM] * 8,
        (
            shape(by_half, F32),
            shape(by_half, F32),
            shape((modes, SUBS, channels), F32),
            shape((modes, channels), F32),
            shape((3, HEAD, channels), F32),
            shape(short_weight.shape, F32),
            shape((modes, channels), F32),
            shape((modes, channels), F32),
            shape((1, channels), F32),
            shape((channels, width), BF16),
            shape((channels // 2, width), BF16),
            pltpu.VMEM((channels, width), BF16),
        ),
        "gate",
        [
            pltpu.VMEM((3, rows, channels), BF16),
            pltpu.VMEM((modes, channels), F32),
            pltpu.VMEM((3, HEAD + rows, channels), F32),
            pltpu.SemaphoreType.DMA((10,)),
        ],
    )(query_in, key_in, value_in, short_weight, rate, residue, skip, out_weight)
    side, half = blocks
    side = lax.ppermute(
        side,
        ("core", "tp"),
        [(c * parts + t, c * parts + (t + 1 - 2 * c) % parts) for c in range(2) for t in range(parts)],
    )
    half = lax.ppermute(half, "tp", [(t, (t + 2) % parts) for t in range(parts)])
    states, late, top = call(
        lambda *refs: join_body(rows, *refs),
        [VMEM] * 5,
        (
            shape((plane, modes, channels), BF16),
            shape((modes, channels), F32),
            shape((2, HEAD, channels), F32),
        ),
        "join",
        [pltpu.VMEM((3, 2 * HEAD, channels), F32)],
    )(rims, heads, taps_here, rate, states)
    states = lax.all_to_all(states, ("y", "core"), 0, 0, tiled=True)
    shared = (queries, gated, begin, late, top, rate, amplitude, skip)
    scratch = [
        pltpu.VMEM(by_half, F32),
        pltpu.VMEM((rows, channels), BF16),
        pltpu.VMEM((2, modes, channels), F32),
        pltpu.SemaphoreType.DMA((channels // LANES, parts)),
    ]
    before, totals, hyena = call(
        lambda *refs: plane_body(taps, rows, *refs),
        [VMEM] * (1 + len(shared)),
        (
            shape((modes, channels), F32),
            shape((planes, modes, channels), BF16),
            pltpu.HBM((parts, rows, channels), BF16),
        ),
        "plane",
        scratch,
        out_spec=(VMEM, VMEM, HBM),
        us=2,
    )(states, *shared)
    totals = lax.all_to_all(totals, "z", 0, 0, tiled=True)
    swapped = [lax.ppermute(side, "core", [(0, 1), (1, 0)])]
    hyena, half = call(
        lambda *refs: mix_body(taps, rows * plane, *refs),
        [VMEM] * 2 + [HBM, ANY] + [VMEM] * len(shared),
        (pltpu.HBM((parts, rows, channels), BF16), shape(half.shape, BF16)),
        "mix",
        scratch,
        out_spec=(HBM, ANY),
        aliases={2: 0, 3: 1},
    )(before, totals, hyena, half, *shared)
    swapped.append(lax.ppermute(half, "core", [(0, 1), (1, 0)]))
    hyena = lax.all_to_all(hyena, "tp", 0, 0, tiled=True)
    hyena = call(order_body, [VMEM], shape((rows, parts * channels), BF16), "order", us=3)(hyena)
    block = 256
    return call(
        project_body,
        [VMEM] * 6,
        shape((rows, width), BF16),
        "project",
        [pltpu.VMEM((width // block, rows, block), BF16), pltpu.SemaphoreType.DMA((width // block,))],
        out_spec=HBM,
    )(hyena, own, side, swapped[0], half, swapped[1])


def solution(mesh):
    fine = Mesh(mesh.devices.reshape(8, 8, 2, 4), ("z", "y", "core", "tp"))
    seq = ("z", "y", "core")
    in_specs = (
        P(seq, "tp"),
        P(seq, "tp"),
        P(seq, "tp"),
        P(None, None, "tp"),
        P(None, "tp"),
        P(None, "tp"),
        P("tp"),
        P("tp", None),
    )
    return jax.shard_map(local, mesh=fine, in_specs=in_specs, out_specs=P(seq, "tp"), check_vma=False)
```

```python
import jax
import jax.numpy as jnp
from jax import lax
from jax.experimental import pallas as pl
from jax.experimental.pallas import tpu as pltpu
from jax.sharding import Mesh, PartitionSpec as P

F32 = jnp.float32
BF16 = jnp.bfloat16
LANES = 128
SUBS = 8
RIM = 16
HEAD = 8
MIB = 1 << 20
RATE = 1.15e9


def shape(dims, dtype):
    return jax.ShapeDtypeStruct(dims, dtype)


VMEM = pl.BlockSpec(memory_space=pltpu.VMEM)
ANY = pl.BlockSpec(memory_space=pl.ANY)
HBM = pl.BlockSpec(memory_space=pltpu.HBM)


def call(body, specs, outs, name, scratch=(), mib=4, out_spec=VMEM, aliases=None, us=0):
    return pl.pallas_call(
        body,
        in_specs=specs,
        out_specs=out_spec if isinstance(out_spec, tuple) else jax.tree.map(lambda _: out_spec, outs),
        input_output_aliases=aliases or {},
        cost_estimate=pl.CostEstimate(flops=int(us * RATE), bytes_accessed=0, transcendentals=0) if us else None,
        out_shape=outs,
        scratch_shapes=list(scratch),
        compiler_params=pltpu.CompilerParams(vmem_limit_bytes=mib * MIB),
        name=name,
    )


def fetch(sources, targets, sems):
    copies = [pltpu.make_async_copy(s, t, sems.at[i]) for i, (s, t) in enumerate(zip(sources, targets))]
    for copy in copies:
        copy.start()
    return copies


def row_of(ref, m, lanes):
    return ref[pl.ds(m, 1), lanes]


def wide(row):
    return jnp.broadcast_to(row, (SUBS, LANES))


def one_minus_exp(x):
    series = 1.0 / 362880.0
    for n in (40320, 5040, 720, 120, 24, 6, 2, 1):
        series = 1.0 / n - x * series
    return jnp.where(x < 0.25, x * series, 1.0 - jnp.exp(-x))


def rim_body(q_ref, k_ref, v_ref, out_ref, sems):
    rows = q_ref.shape[0]
    refs = (q_ref, k_ref, v_ref)
    copies = fetch(
        [ref.at[pl.ds(rows - RIM, RIM), :] for ref in refs],
        [out_ref.at[pl.ds(i * RIM, RIM), :] for i in range(3)],
        sems,
    )
    for copy in copies:
        copy.wait()


def gate_body(
    q_hbm, k_hbm, v_hbm, taps_hbm, rate_hbm, residue_hbm, skip_hbm, weight_hbm,
    query_ref, gated_ref, begin_ref, state_ref, head_ref, taps_ref, rate_ref, amp_ref, skip_ref, *rest,
):
    *blocks, own_ref, streams, residue_ref, pad, sems = rest
    here, parts = lax.axis_index("tp"), lax.axis_size("tp")
    width = blocks[0].shape[1]
    _, rows, channels = streams.shape
    modes = rate_ref.shape[0]
    taps = taps_ref.shape[1]
    steps = rows // SUBS
    copies = fetch(
        (q_hbm, k_hbm, v_hbm, taps_hbm, rate_hbm, residue_hbm, skip_hbm),
        (streams.at[0], streams.at[1], streams.at[2], taps_ref, rate_ref, residue_ref, skip_ref),
        sems,
    )
    core = lax.axis_index("core")
    height = blocks[1].shape[0]
    side = lax.rem(here + jnp.where(core == 0, 1, parts - 1), parts)
    sent = fetch(
        (
            weight_hbm.at[:, pl.ds(pl.multiple_of(side * width, LANES), width)],
            weight_hbm.at[
                pl.ds(pl.multiple_of(core * height, height), height),
                pl.ds(pl.multiple_of(lax.rem(here + 2, parts) * width, LANES), width),
            ],
        ),
        blocks,
        sems.at[pl.ds(7, 2)],
    )
    sent += fetch([weight_hbm.at[:, pl.ds(here * width, width)]], [own_ref], sems.at[pl.ds(9, 1)])
    for copy in copies:
        copy.wait()
    amp_ref[...] = residue_ref[...] * jnp.sqrt(one_minus_exp(2.0 * rate_ref[...]))
    for i in range(3):
        pad[i, pl.ds(0, HEAD), :] = jnp.zeros((HEAD, channels), F32)
        pad[i, pl.ds(HEAD, rows), :] = streams[i].astype(F32)
    block = 32
    for half in range(channels // LANES):
        lanes = pl.ds(half * LANES, LANES)
        for r in range(0, rows, block):
            sums = []
            for i in range(3):
                total = jnp.zeros((block, LANES), F32)
                for t in range(taps):
                    total = total + taps_ref[i, pl.ds(t, 1), lanes] * pad[i, pl.ds(HEAD + r - t, block), lanes]
                sums.append(total)
                if r == 0:
                    head_ref[i, :, lanes] = total[:HEAD]
            query_ref[half, pl.ds(r, block), :] = sums[0]
            gated_ref[half, pl.ds(r, block), :] = sums[1] * sums[2]
    sub = lax.broadcasted_iota(jnp.int32, (SUBS, LANES), 0)
    for half in range(channels // LANES):
        lanes = pl.ds(half * LANES, LANES)
        rates = [row_of(rate_ref, m, lanes) for m in range(modes)]
        retain = [wide(jnp.exp(-x)) for x in rates]
        state = [jnp.zeros((SUBS, LANES), F32) for _ in range(modes)]
        for step in range(steps):
            g = gated_ref[half, pl.ds(step, SUBS, stride=steps), :]
            state = [a * s + g for a, s in zip(retain, state)]
        for m in range(modes):
            s = state[m]
            for d in (1, 2, 4):
                drop = wide(jnp.exp(-(steps * d) * rates[m]))
                s = s + jnp.where(sub >= d, drop * pltpu.roll(s, d, 0), 0.0)
            state_ref[pl.ds(m, 1), lanes] = s[SUBS - 1 :]
            begin_ref[m, :, lanes] = jnp.where(sub >= 1, pltpu.roll(s, 1, 0), 0.0)
    for copy in sent:
        copy.wait()


def join_body(rows, rim_ref, head_ref, taps_ref, rate_ref, state_ref, out_ref, late_ref, top_ref, pad):
    modes, channels = rate_ref.shape
    taps = taps_ref.shape[1]
    sums = []
    for i in range(3):
        pad[i, pl.ds(0, HEAD), :] = rim_ref[pl.ds(i * RIM, RIM), :].astype(F32)[RIM - HEAD :]
        pad[i, pl.ds(HEAD, HEAD), :] = jnp.zeros((HEAD, channels), F32)
        total = head_ref[i]
        for t in range(1, taps):
            total = total + taps_ref[i, pl.ds(t, 1), :] * pad[i, pl.ds(HEAD - t, HEAD), :]
        sums.append(total)
    gated = sums[1] * sums[2]
    top_ref[0] = sums[0]
    top_ref[1] = gated
    more = gated - head_ref[1] * head_ref[2]
    rate = rate_ref[...]
    retain = jnp.exp(-rate)
    late = jnp.broadcast_to(more[:1], rate.shape)
    for i in range(1, taps - 1):
        late = retain * late + more[i : i + 1]
    late_ref[...] = late
    whole = (state_ref[...] + jnp.exp(-(rows - taps + 1) * rate) * late).astype(BF16)
    for i in range(out_ref.shape[0]):
        out_ref[i] = whole


def plane_body(rows, parts_ref, rate_ref, _block, before_ref, total_ref, _same_block):
    me = lax.axis_index("y") * lax.axis_size("core") + lax.axis_index("core")
    drop = jnp.exp(-rows * rate_ref[...])
    before = jnp.zeros(rate_ref.shape, F32)
    total = jnp.zeros(rate_ref.shape, F32)
    for i in range(parts_ref.shape[0]):
        part = parts_ref[i].astype(F32)
        before = jnp.where(i < me, before * drop + part, before)
        total = total * drop + part
    before_ref[...] = before
    for i in range(total_ref.shape[0]):
        total_ref[i] = total.astype(BF16)


def mix(taps, carried, refs, out_hbm, hyena, left, carry, sems):
    query_ref, gated_ref, begin_ref, late_ref, top_ref, rate_ref, amp_ref, skip_ref = refs
    halves, rows, _ = query_ref.shape
    modes = rate_ref.shape[0]
    steps = rows // SUBS
    carry[0] = carried
    carry[1] = carried + jnp.exp((taps - 1) * rate_ref[...]) * late_ref[...]
    parts, copies = out_hbm.shape[0], []
    sub = lax.broadcasted_iota(jnp.int32, (SUBS, LANES), 0)
    ahead = sub.astype(F32) * float(steps)
    for half in range(halves):
        lanes = pl.ds(half * LANES, LANES)
        rates = [row_of(rate_ref, m, lanes) for m in range(modes)]
        retain = [wide(jnp.exp(-x)) for x in rates]
        amp = [wide(row_of(amp_ref, m, lanes)) for m in range(modes)]
        skip = wide(row_of(skip_ref, 0, lanes))
        state = [
            begin_ref[m, :, lanes]
            + jnp.exp(-ahead * rates[m])
            * jnp.where(sub >= 1, row_of(carry.at[1], m, lanes), row_of(carry.at[0], m, lanes))
            for m in range(modes)
        ]
        for step in range(steps):
            at = pl.ds(step, SUBS, stride=steps)
            g = gated_ref[half, at, :]
            query = query_ref[half, at, :]
            if step < taps - 1:
                query = jnp.where(sub >= 1, query, top_ref[0, pl.ds(step, 1), lanes])
                g = jnp.where(sub >= 1, g, top_ref[1, pl.ds(step, 1), lanes])
            state = [a * s + g for a, s in zip(retain, state)]
            terms = [a * s for a, s in zip(amp, state)] + [skip * g]
            while len(terms) > 1:
                terms = [x + y for x, y in zip(terms[::2], terms[1::2])] + terms[len(terms) // 2 * 2 :]
            hyena[half, at, :] = query * terms[0]
        left[:, lanes] = hyena[half].astype(BF16)
        copies += fetch([left.at[:, lanes]] * parts, [out_hbm.at[i, :, lanes] for i in range(parts)], sems.at[half])
    for copy in copies:
        copy.wait()


def plane_body(taps, rows, parts_ref, *refs):
    *refs, before_ref, total_ref, out_hbm, hyena, left, carry, sems = refs
    rate_ref = refs[5]
    me = lax.axis_index("y") * lax.axis_size("core") + lax.axis_index("core")
    drop = jnp.exp(-rows * rate_ref[...])
    before = jnp.zeros(rate_ref.shape, F32)
    total = jnp.zeros(rate_ref.shape, F32)
    for i in range(parts_ref.shape[0]):
        part = parts_ref[i].astype(F32)
        before = jnp.where(i < me, before * drop + part, before)
        total = total * drop + part
    before_ref[...] = before
    for i in range(total_ref.shape[0]):
        total_ref[i] = total.astype(BF16)

    @pl.when(lax.axis_index("z") == 0)
    def _():
        mix(taps, before, refs, out_hbm, hyena, left, carry, sems)


def mix_body(taps, plane_rows, before_ref, planes_ref, _hyena, *refs):
    *refs, out_hbm, hyena, left, carry, sems = refs
    query_ref, rate_ref = refs[0], refs[5]
    rows = query_ref.shape[1]
    z = lax.axis_index("z")

    @pl.when(z > 0)
    def _():
        me = lax.axis_index("y") * lax.axis_size("core") + lax.axis_index("core")
        rate = rate_ref[...]
        drop = jnp.exp(-plane_rows * rate)
        behind = jnp.zeros(rate.shape, F32)
        for i in range(planes_ref.shape[0]):
            behind = jnp.where(i < z, behind * drop + planes_ref[i].astype(F32), behind)
        carried = before_ref[...] + jnp.exp(-(rows * me).astype(F32) * rate) * behind
        mix(taps, carried, refs, out_hbm, hyena, left, carry, sems)


def order_body(left_ref, out_ref):
    parts, _, channels = left_ref.shape
    here, core = lax.axis_index("tp"), lax.axis_index("core")
    ahead, behind = lax.rem(here + 1, parts), lax.rem(here + parts - 1, parts)
    across = lax.rem(here + 2, parts)
    height = channels // 2
    out_ref[:, :channels] = left_ref[here]
    out_ref[:, channels : 2 * channels] = left_ref[jnp.where(core == 0, behind, ahead)]
    out_ref[:, 2 * channels : 3 * channels] = left_ref[jnp.where(core == 0, ahead, behind)]
    for i, half in enumerate((core, 1 - core)):
        columns = pl.ds(pl.multiple_of(half * height, height), height)
        out_ref[:, pl.ds(3 * channels + i * height, height)] = left_ref[across, :, columns]


def project_body(left_ref, *rest):
    *rights, out_hbm, done, sems = rest
    blocks, _, block = done.shape
    copies = []
    for b in range(blocks):
        at = pl.ds(b * block, block)
        total = jnp.zeros(done.shape[1:], F32)
        begin = 0
        for right in rights:
            depth = right.shape[0]
            total += jnp.dot(left_ref[:, pl.ds(begin, depth)], right[:, at], preferred_element_type=F32)
            begin += depth
        done[b] = total.astype(BF16)
        copies.append(pltpu.make_async_copy(done.at[b], out_hbm.at[:, at], sems.at[b]))
        copies[-1].start()
    for copy in copies:
        copy.wait()


def local(query_in, key_in, value_in, short_weight, residue, rate, skip, out_weight):
    rows, channels = query_in.shape
    modes = rate.shape[0]
    taps = short_weight.shape[1]
    planes = lax.axis_size("z")
    plane = lax.axis_size("y") * lax.axis_size("core")
    parts = lax.axis_size("tp")
    width = out_weight.shape[1] // parts
    order = ("z", "y", "core")
    devices = planes * plane
    by_half = (channels // LANES, rows, LANES)
    skip = skip.reshape(1, -1)
    query_in, key_in, value_in, short_weight, residue, rate, skip, out_weight = (
        pltpu.with_memory_space_constraint(x, pltpu.HBM)
        for x in (query_in, key_in, value_in, short_weight, residue, rate, skip, out_weight)
    )
    rims = call(
        rim_body, [HBM] * 3, shape((3 * RIM, channels), BF16), "rims", [pltpu.SemaphoreType.DMA((3,))]
    )(query_in, key_in, value_in)
    rims = lax.ppermute(rims, order, [(i, i + 1) for i in range(devices - 1)])
    queries, gated, begin, states, heads, taps_here, rate, amplitude, skip, *blocks, own = call(
        gate_body,
        [HBM] * 8,
        (
            shape(by_half, F32),
            shape(by_half, F32),
            shape((modes, SUBS, channels), F32),
            shape((modes, channels), F32),
            shape((3, HEAD, channels), F32),
            shape(short_weight.shape, F32),
            shape((modes, channels), F32),
            shape((modes, channels), F32),
            shape((1, channels), F32),
            shape((channels, width), BF16),
            shape((channels // 2, width), BF16),
            pltpu.VMEM((channels, width), BF16),
        ),
        "gate",
        [
            pltpu.VMEM((3, rows, channels), BF16),
            pltpu.VMEM((modes, channels), F32),
            pltpu.VMEM((3, HEAD + rows, channels), F32),
            pltpu.SemaphoreType.DMA((10,)),
        ],
    )(query_in, key_in, value_in, short_weight, rate, residue, skip, out_weight)
    side, half = blocks
    side = lax.ppermute(
        side,
        ("core", "tp"),
        [(c * parts + t, c * parts + (t + 1 - 2 * c) % parts) for c in range(2) for t in range(parts)],
    )
    half = lax.ppermute(half, "tp", [(t, (t + 2) % parts) for t in range(parts)])
    states, late, top = call(
        lambda *refs: join_body(rows, *refs),
        [VMEM] * 5,
        (
            shape((plane, modes, channels), BF16),
            shape((modes, channels), F32),
            shape((2, HEAD, channels), F32),
        ),
        "join",
        [pltpu.VMEM((3, 2 * HEAD, channels), F32)],
    )(rims, heads, taps_here, rate, states)
    states = lax.all_to_all(states, ("y", "core"), 0, 0, tiled=True)
    shared = (queries, gated, begin, late, top, rate, amplitude, skip)
    scratch = [
        pltpu.VMEM(by_half, F32),
        pltpu.VMEM((rows, channels), BF16),
        pltpu.VMEM((2, modes, channels), F32),
        pltpu.SemaphoreType.DMA((channels // LANES, parts)),
    ]
    before, totals, hyena = call(
        lambda *refs: plane_body(taps, rows, *refs),
        [VMEM] * (1 + len(shared)),
        (
            shape((modes, channels), F32),
            shape((planes, modes, channels), BF16),
            shape((parts, rows, channels), BF16),
        ),
        "plane",
        scratch,
        out_spec=(VMEM, VMEM, ANY),
        us=4,
    )(states, *shared)
    totals = lax.all_to_all(totals, "z", 0, 0, tiled=True)
    swapped = [lax.ppermute(x, "core", [(0, 1), (1, 0)]) for x in (side, half)]
    hyena = call(
        lambda *refs: mix_body(taps, rows * plane, *refs),
        [VMEM] * 2 + [ANY] + [VMEM] * len(shared),
        shape((parts, rows, channels), BF16),
        "mix",
        scratch,
        out_spec=ANY,
        aliases={2: 0},
        us=2,
    )(before, totals, hyena, *shared)
    hyena = lax.all_to_all(hyena, "tp", 0, 0, tiled=True)
    hyena = call(order_body, [VMEM], shape((rows, parts * channels), BF16), "order", us=0)(hyena)
    block = 256
    return call(
        project_body,
        [VMEM] * 6,
        shape((rows, width), BF16),
        "project",
        [pltpu.VMEM((width // block, rows, block), BF16), pltpu.SemaphoreType.DMA((width // block,))],
        out_spec=HBM,
    )(hyena, own, side, swapped[0], half, swapped[1])


def solution(mesh):
    fine = Mesh(mesh.devices.reshape(8, 8, 2, 4), ("z", "y", "core", "tp"))
    seq = ("z", "y", "core")
    in_specs = (
        P(seq, "tp"),
        P(seq, "tp"),
        P(seq, "tp"),
        P(None, None, "tp"),
        P(None, "tp"),
        P(None, "tp"),
        P("tp"),
        P("tp", None),
    )
    return jax.shard_map(local, mesh=fine, in_specs=in_specs, out_specs=P(seq, "tp"), check_vma=False)
```

```python
import jax
import jax.numpy as jnp
from jax import lax
from jax.experimental import pallas as pl
from jax.experimental.pallas import tpu as pltpu
from jax.sharding import Mesh, PartitionSpec as P

F32 = jnp.float32
BF16 = jnp.bfloat16
LANES = 128
SUBS = 8
RIM = 16
HEAD = 8
MIB = 1 << 20
RATE = 1.15e9


def shape(dims, dtype):
    return jax.ShapeDtypeStruct(dims, dtype)


VMEM = pl.BlockSpec(memory_space=pltpu.VMEM)
ANY = pl.BlockSpec(memory_space=pl.ANY)
HBM = pl.BlockSpec(memory_space=pltpu.HBM)


def call(body, specs, outs, name, scratch=(), mib=4, out_spec=VMEM, aliases=None, us=0):
    return pl.pallas_call(
        body,
        in_specs=specs,
        out_specs=out_spec if isinstance(out_spec, tuple) else jax.tree.map(lambda _: out_spec, outs),
        input_output_aliases=aliases or {},
        cost_estimate=pl.CostEstimate(flops=int(us * RATE), bytes_accessed=0, transcendentals=0) if us else None,
        out_shape=outs,
        scratch_shapes=list(scratch),
        compiler_params=pltpu.CompilerParams(vmem_limit_bytes=mib * MIB),
        name=name,
    )


def fetch(sources, targets, sems):
    copies = [pltpu.make_async_copy(s, t, sems.at[i]) for i, (s, t) in enumerate(zip(sources, targets))]
    for copy in copies:
        copy.start()
    return copies


def row_of(ref, m, lanes):
    return ref[pl.ds(m, 1), lanes]


def wide(row):
    return jnp.broadcast_to(row, (SUBS, LANES))


def one_minus_exp(x):
    series = 1.0 / 362880.0
    for n in (40320, 5040, 720, 120, 24, 6, 2, 1):
        series = 1.0 / n - x * series
    return jnp.where(x < 0.25, x * series, 1.0 - jnp.exp(-x))


def rim_body(q_ref, k_ref, v_ref, out_ref, sems):
    rows = q_ref.shape[0]
    refs = (q_ref, k_ref, v_ref)
    copies = fetch(
        [ref.at[pl.ds(rows - RIM, RIM), :] for ref in refs],
        [out_ref.at[pl.ds(i * RIM, RIM), :] for i in range(3)],
        sems,
    )
    for copy in copies:
        copy.wait()


def gate_body(
    q_hbm, k_hbm, v_hbm, taps_hbm, rate_hbm, residue_hbm, skip_hbm, weight_hbm,
    query_ref, gated_ref, begin_ref, state_ref, head_ref, taps_ref, rate_ref, amp_ref, skip_ref, *rest,
):
    *blocks, own_ref, streams, residue_ref, pad, sems = rest
    here, parts = lax.axis_index("tp"), lax.axis_size("tp")
    width = blocks[0].shape[1]
    _, rows, channels = streams.shape
    modes = rate_ref.shape[0]
    taps = taps_ref.shape[1]
    steps = rows // SUBS
    copies = fetch(
        (q_hbm, k_hbm, v_hbm, taps_hbm, rate_hbm, residue_hbm, skip_hbm),
        (streams.at[0], streams.at[1], streams.at[2], taps_ref, rate_ref, residue_ref, skip_ref),
        sems,
    )
    core = lax.axis_index("core")
    height = blocks[1].shape[0]
    side = lax.rem(here + jnp.where(core == 0, 1, parts - 1), parts)
    sent = fetch(
        (
            weight_hbm.at[:, pl.ds(pl.multiple_of(side * width, LANES), width)],
            weight_hbm.at[
                pl.ds(pl.multiple_of(core * height, height), height),
                pl.ds(pl.multiple_of(lax.rem(here + 2, parts) * width, LANES), width),
            ],
        ),
        blocks,
        sems.at[pl.ds(7, 2)],
    )
    sent += fetch([weight_hbm.at[:, pl.ds(here * width, width)]], [own_ref], sems.at[pl.ds(9, 1)])
    for copy in copies:
        copy.wait()
    amp_ref[...] = residue_ref[...] * jnp.sqrt(one_minus_exp(2.0 * rate_ref[...]))
    for i in range(3):
        pad[i, pl.ds(0, HEAD), :] = jnp.zeros((HEAD, channels), F32)
        pad[i, pl.ds(HEAD, rows), :] = streams[i].astype(F32)
    block = 32
    for half in range(channels // LANES):
        lanes = pl.ds(half * LANES, LANES)
        for r in range(0, rows, block):
            sums = []
            for i in range(3):
                total = jnp.zeros((block, LANES), F32)
                for t in range(taps):
                    total = total + taps_ref[i, pl.ds(t, 1), lanes] * pad[i, pl.ds(HEAD + r - t, block), lanes]
                sums.append(total)
                if r == 0:
                    head_ref[i, :, lanes] = total[:HEAD]
            query_ref[half, pl.ds(r, block), :] = sums[0]
            gated_ref[half, pl.ds(r, block), :] = sums[1] * sums[2]
    sub = lax.broadcasted_iota(jnp.int32, (SUBS, LANES), 0)
    for half in range(channels // LANES):
        lanes = pl.ds(half * LANES, LANES)
        rates = [row_of(rate_ref, m, lanes) for m in range(modes)]
        retain = [wide(jnp.exp(-x)) for x in rates]
        state = [jnp.zeros((SUBS, LANES), F32) for _ in range(modes)]
        for step in range(steps):
            g = gated_ref[half, pl.ds(step, SUBS, stride=steps), :]
            state = [a * s + g for a, s in zip(retain, state)]
        for m in range(modes):
            s = state[m]
            for d in (1, 2, 4):
                drop = wide(jnp.exp(-(steps * d) * rates[m]))
                s = s + jnp.where(sub >= d, drop * pltpu.roll(s, d, 0), 0.0)
            state_ref[pl.ds(m, 1), lanes] = s[SUBS - 1 :]
            begin_ref[m, :, lanes] = jnp.where(sub >= 1, pltpu.roll(s, 1, 0), 0.0)
    for copy in sent:
        copy.wait()


def join_body(rows, rim_ref, head_ref, taps_ref, rate_ref, state_ref, out_ref, late_ref, top_ref, pad):
    modes, channels = rate_ref.shape
    taps = taps_ref.shape[1]
    sums = []
    for i in range(3):
        pad[i, pl.ds(0, HEAD), :] = rim_ref[pl.ds(i * RIM, RIM), :].astype(F32)[RIM - HEAD :]
        pad[i, pl.ds(HEAD, HEAD), :] = jnp.zeros((HEAD, channels), F32)
        total = head_ref[i]
        for t in range(1, taps):
            total = total + taps_ref[i, pl.ds(t, 1), :] * pad[i, pl.ds(HEAD - t, HEAD), :]
        sums.append(total)
    gated = sums[1] * sums[2]
    top_ref[0] = sums[0]
    top_ref[1] = gated
    more = gated - head_ref[1] * head_ref[2]
    rate = rate_ref[...]
    retain = jnp.exp(-rate)
    late = jnp.broadcast_to(more[:1], rate.shape)
    for i in range(1, taps - 1):
        late = retain * late + more[i : i + 1]
    late_ref[...] = late
    out_ref[...] = (state_ref[...] + jnp.exp(-(rows - taps + 1) * rate) * late).astype(BF16)


def mix(taps, carried, refs, out_hbm, hyena, left, carry, sems):
    query_ref, gated_ref, begin_ref, late_ref, top_ref, rate_ref, amp_ref, skip_ref = refs
    halves, rows, _ = query_ref.shape
    modes = rate_ref.shape[0]
    steps = rows // SUBS
    carry[0] = carried
    carry[1] = carried + jnp.exp((taps - 1) * rate_ref[...]) * late_ref[...]
    parts, copies = out_hbm.shape[0], []
    sub = lax.broadcasted_iota(jnp.int32, (SUBS, LANES), 0)
    ahead = sub.astype(F32) * float(steps)
    for half in range(halves):
        lanes = pl.ds(half * LANES, LANES)
        rates = [row_of(rate_ref, m, lanes) for m in range(modes)]
        retain = [wide(jnp.exp(-x)) for x in rates]
        amp = [wide(row_of(amp_ref, m, lanes)) for m in range(modes)]
        skip = wide(row_of(skip_ref, 0, lanes))
        state = [
            begin_ref[m, :, lanes]
            + jnp.exp(-ahead * rates[m])
            * jnp.where(sub >= 1, row_of(carry.at[1], m, lanes), row_of(carry.at[0], m, lanes))
            for m in range(modes)
        ]
        for step in range(steps):
            at = pl.ds(step, SUBS, stride=steps)
            g = gated_ref[half, at, :]
            query = query_ref[half, at, :]
            if step < taps - 1:
                query = jnp.where(sub >= 1, query, top_ref[0, pl.ds(step, 1), lanes])
                g = jnp.where(sub >= 1, g, top_ref[1, pl.ds(step, 1), lanes])
            state = [a * s + g for a, s in zip(retain, state)]
            terms = [a * s for a, s in zip(amp, state)] + [skip * g]
            while len(terms) > 1:
                terms = [x + y for x, y in zip(terms[::2], terms[1::2])] + terms[len(terms) // 2 * 2 :]
            hyena[half, at, :] = query * terms[0]
        left[:, lanes] = hyena[half].astype(BF16)
        copies += fetch([left.at[:, lanes]] * parts, [out_hbm.at[i, :, lanes] for i in range(parts)], sems.at[half])
    for copy in copies:
        copy.wait()


def pair_body(rows, pair_ref, rate_ref, out_ref):
    drop = jnp.exp(-rows * rate_ref[...])
    whole = (pair_ref[0].astype(F32) * drop + pair_ref[1].astype(F32)).astype(BF16)
    for i in range(out_ref.shape[0]):
        out_ref[i] = whole


def plane_body(taps, rows, parts_ref, pair_ref, *refs):
    *refs, before_ref, total_ref, out_hbm, hyena, left, carry, sems = refs
    rate_ref = refs[5]
    y = lax.axis_index("y")
    drop = jnp.exp(-2 * rows * rate_ref[...])
    before = jnp.zeros(rate_ref.shape, F32)
    total = jnp.zeros(rate_ref.shape, F32)
    for i in range(parts_ref.shape[0]):
        part = parts_ref[i].astype(F32)
        before = jnp.where(i < y, before * drop + part, before)
        total = total * drop + part
    second = before * jnp.exp(-rows * rate_ref[...]) + pair_ref[0].astype(F32)
    before = jnp.where(lax.axis_index("core") == 0, before, second)
    before_ref[...] = before
    for i in range(total_ref.shape[0]):
        total_ref[i] = total.astype(BF16)

    @pl.when(lax.axis_index("z") == 0)
    def _():
        mix(taps, before, refs, out_hbm, hyena, left, carry, sems)


def mix_body(taps, plane_rows, before_ref, planes_ref, _hyena, *refs):
    *refs, out_hbm, hyena, left, carry, sems = refs
    query_ref, rate_ref = refs[0], refs[5]
    rows = query_ref.shape[1]
    z = lax.axis_index("z")

    @pl.when(z > 0)
    def _():
        me = lax.axis_index("y") * lax.axis_size("core") + lax.axis_index("core")
        rate = rate_ref[...]
        drop = jnp.exp(-plane_rows * rate)
        behind = jnp.zeros(rate.shape, F32)
        for i in range(planes_ref.shape[0]):
            behind = jnp.where(i < z, behind * drop + planes_ref[i].astype(F32), behind)
        carried = before_ref[...] + jnp.exp(-(rows * me).astype(F32) * rate) * behind
        mix(taps, carried, refs, out_hbm, hyena, left, carry, sems)


def order_body(left_ref, out_ref):
    parts, _, channels = left_ref.shape
    here, core = lax.axis_index("tp"), lax.axis_index("core")
    ahead, behind = lax.rem(here + 1, parts), lax.rem(here + parts - 1, parts)
    across = lax.rem(here + 2, parts)
    height = channels // 2
    out_ref[:, :channels] = left_ref[here]
    out_ref[:, channels : 2 * channels] = left_ref[jnp.where(core == 0, behind, ahead)]
    out_ref[:, 2 * channels : 3 * channels] = left_ref[jnp.where(core == 0, ahead, behind)]
    for i, half in enumerate((core, 1 - core)):
        columns = pl.ds(pl.multiple_of(half * height, height), height)
        out_ref[:, pl.ds(3 * channels + i * height, height)] = left_ref[across, :, columns]


def project_body(left_ref, *rest):
    *rights, out_hbm, done, sems = rest
    blocks, _, block = done.shape
    copies = []
    for b in range(blocks):
        at = pl.ds(b * block, block)
        total = jnp.zeros(done.shape[1:], F32)
        begin = 0
        for right in rights:
            depth = right.shape[0]
            total += jnp.dot(left_ref[:, pl.ds(begin, depth)], right[:, at], preferred_element_type=F32)
            begin += depth
        done[b] = total.astype(BF16)
        copies.append(pltpu.make_async_copy(done.at[b], out_hbm.at[:, at], sems.at[b]))
        copies[-1].start()
    for copy in copies:
        copy.wait()


def local(query_in, key_in, value_in, short_weight, residue, rate, skip, out_weight):
    rows, channels = query_in.shape
    modes = rate.shape[0]
    taps = short_weight.shape[1]
    planes = lax.axis_size("z")
    plane = lax.axis_size("y") * lax.axis_size("core")
    parts = lax.axis_size("tp")
    width = out_weight.shape[1] // parts
    order = ("z", "y", "core")
    devices = planes * plane
    by_half = (channels // LANES, rows, LANES)
    skip = skip.reshape(1, -1)
    query_in, key_in, value_in, short_weight, residue, rate, skip, out_weight = (
        pltpu.with_memory_space_constraint(x, pltpu.HBM)
        for x in (query_in, key_in, value_in, short_weight, residue, rate, skip, out_weight)
    )
    rims = call(
        rim_body, [HBM] * 3, shape((3 * RIM, channels), BF16), "rims", [pltpu.SemaphoreType.DMA((3,))]
    )(query_in, key_in, value_in)
    rims = lax.ppermute(rims, order, [(i, i + 1) for i in range(devices - 1)])
    queries, gated, begin, states, heads, taps_here, rate, amplitude, skip, *blocks, own = call(
        gate_body,
        [HBM] * 8,
        (
            shape(by_half, F32),
            shape(by_half, F32),
            shape((modes, SUBS, channels), F32),
            shape((modes, channels), F32),
            shape((3, HEAD, channels), F32),
            shape(short_weight.shape, F32),
            shape((modes, channels), F32),
            shape((modes, channels), F32),
            shape((1, channels), F32),
            shape((channels, width), BF16),
            shape((channels // 2, width), BF16),
            pltpu.VMEM((channels, width), BF16),
        ),
        "gate",
        [
            pltpu.VMEM((3, rows, channels), BF16),
            pltpu.VMEM((modes, channels), F32),
            pltpu.VMEM((3, HEAD + rows, channels), F32),
            pltpu.SemaphoreType.DMA((10,)),
        ],
    )(query_in, key_in, value_in, short_weight, rate, residue, skip, out_weight)
    side, half = blocks
    side = lax.ppermute(
        side,
        ("core", "tp"),
        [(c * parts + t, c * parts + (t + 1 - 2 * c) % parts) for c in range(2) for t in range(parts)],
    )
    half = lax.ppermute(half, "tp", [(t, (t + 2) % parts) for t in range(parts)])
    states, late, top = call(
        lambda *refs: join_body(rows, *refs),
        [VMEM] * 5,
        (
            shape((modes, channels), BF16),
            shape((modes, channels), F32),
            shape((2, HEAD, channels), F32),
        ),
        "join",
        [pltpu.VMEM((3, 2 * HEAD, channels), F32)],
    )(rims, heads, taps_here, rate, states)
    pair = lax.all_gather(states, "core")
    states = call(
        lambda *refs: pair_body(rows, *refs), [VMEM] * 2, shape((plane // 2, modes, channels), BF16), "pair"
    )(pair, rate)
    states = lax.all_to_all(states, "y", 0, 0, tiled=True)
    shared = (queries, gated, begin, late, top, rate, amplitude, skip)
    scratch = [
        pltpu.VMEM(by_half, F32),
        pltpu.VMEM((rows, channels), BF16),
        pltpu.VMEM((2, modes, channels), F32),
        pltpu.SemaphoreType.DMA((channels // LANES, parts)),
    ]
    before, totals, hyena = call(
        lambda *refs: plane_body(taps, rows, *refs),
        [VMEM] * (2 + len(shared)),
        (
            shape((modes, channels), F32),
            shape((planes, modes, channels), BF16),
            shape((parts, rows, channels), BF16),
        ),
        "plane",
        scratch,
        out_spec=(VMEM, VMEM, ANY),
        us=4,
    )(states, pair, *shared)
    totals = lax.all_to_all(totals, "z", 0, 0, tiled=True)
    swapped = [lax.ppermute(x, "core", [(0, 1), (1, 0)]) for x in (side, half)]
    hyena = call(
        lambda *refs: mix_body(taps, rows * plane, *refs),
        [VMEM] * 2 + [ANY] + [VMEM] * len(shared),
        shape((parts, rows, channels), BF16),
        "mix",
        scratch,
        out_spec=ANY,
        aliases={2: 0},
        us=2,
    )(before, totals, hyena, *shared)
    hyena = lax.all_to_all(hyena, "tp", 0, 0, tiled=True)
    hyena = call(order_body, [VMEM], shape((rows, parts * channels), BF16), "order", us=0)(hyena)
    block = 256
    return call(
        project_body,
        [VMEM] * 6,
        shape((rows, width), BF16),
        "project",
        [pltpu.VMEM((width // block, rows, block), BF16), pltpu.SemaphoreType.DMA((width // block,))],
        out_spec=HBM,
    )(hyena, own, side, swapped[0], half, swapped[1])


def solution(mesh):
    fine = Mesh(mesh.devices.reshape(8, 8, 2, 4), ("z", "y", "core", "tp"))
    seq = ("z", "y", "core")
    in_specs = (
        P(seq, "tp"),
        P(seq, "tp"),
        P(seq, "tp"),
        P(None, None, "tp"),
        P(None, "tp"),
        P(None, "tp"),
        P("tp"),
        P("tp", None),
    )
    return jax.shard_map(local, mesh=fine, in_specs=in_specs, out_specs=P(seq, "tp"), check_vma=False)
```

```python
import jax
import jax.numpy as jnp
from jax import lax
from jax.experimental import pallas as pl
from jax.experimental.pallas import tpu as pltpu
from jax.sharding import Mesh, PartitionSpec as P

F32 = jnp.float32
BF16 = jnp.bfloat16
LANES = 128
SUBS = 8
RIM = 16
HEAD = 8
MIB = 1 << 20
RATE = 1.15e9


def shape(dims, dtype):
    return jax.ShapeDtypeStruct(dims, dtype)


VMEM = pl.BlockSpec(memory_space=pltpu.VMEM)
ANY = pl.BlockSpec(memory_space=pl.ANY)
HBM = pl.BlockSpec(memory_space=pltpu.HBM)


def call(body, specs, outs, name, scratch=(), mib=4, out_spec=VMEM, aliases=None, us=0):
    return pl.pallas_call(
        body,
        in_specs=specs,
        out_specs=out_spec if isinstance(out_spec, tuple) else jax.tree.map(lambda _: out_spec, outs),
        input_output_aliases=aliases or {},
        cost_estimate=pl.CostEstimate(flops=int(us * RATE), bytes_accessed=0, transcendentals=0) if us else None,
        out_shape=outs,
        scratch_shapes=list(scratch),
        compiler_params=pltpu.CompilerParams(vmem_limit_bytes=mib * MIB),
        name=name,
    )


def fetch(sources, targets, sems):
    copies = [pltpu.make_async_copy(s, t, sems.at[i]) for i, (s, t) in enumerate(zip(sources, targets))]
    for copy in copies:
        copy.start()
    return copies


def row_of(ref, m, lanes):
    return ref[pl.ds(m, 1), lanes]


def wide(row):
    return jnp.broadcast_to(row, (SUBS, LANES))


def one_minus_exp(x):
    series = 1.0 / 362880.0
    for n in (40320, 5040, 720, 120, 24, 6, 2, 1):
        series = 1.0 / n - x * series
    return jnp.where(x < 0.25, x * series, 1.0 - jnp.exp(-x))


def rim_body(q_ref, k_ref, v_ref, out_ref, sems):
    rows = q_ref.shape[0]
    refs = (q_ref, k_ref, v_ref)
    copies = fetch(
        [ref.at[pl.ds(rows - RIM, RIM), :] for ref in refs],
        [out_ref.at[pl.ds(i * RIM, RIM), :] for i in range(3)],
        sems,
    )
    for copy in copies:
        copy.wait()


def gate_body(
    q_hbm, k_hbm, v_hbm, taps_hbm, rate_hbm, residue_hbm, skip_hbm, weight_hbm,
    query_ref, gated_ref, begin_ref, state_ref, head_ref, taps_ref, rate_ref, amp_ref, skip_ref, *rest,
):
    *blocks, own_ref, streams, residue_ref, pad, sems = rest
    here, parts = lax.axis_index("tp"), lax.axis_size("tp")
    width = blocks[0].shape[1]
    _, rows, channels = streams.shape
    modes = rate_ref.shape[0]
    taps = taps_ref.shape[1]
    steps = rows // SUBS
    copies = fetch(
        (q_hbm, k_hbm, v_hbm, taps_hbm, rate_hbm, residue_hbm, skip_hbm),
        (streams.at[0], streams.at[1], streams.at[2], taps_ref, rate_ref, residue_ref, skip_ref),
        sems,
    )
    core = lax.axis_index("core")
    height = blocks[1].shape[0]
    side = lax.rem(here + jnp.where(core == 0, 1, parts - 1), parts)
    sent = fetch(
        (
            weight_hbm.at[:, pl.ds(pl.multiple_of(side * width, LANES), width)],
            weight_hbm.at[
                pl.ds(pl.multiple_of(core * height, height), height),
                pl.ds(pl.multiple_of(lax.rem(here + 2, parts) * width, LANES), width),
            ],
        ),
        blocks,
        sems.at[pl.ds(7, 2)],
    )
    sent += fetch([weight_hbm.at[:, pl.ds(here * width, width)]], [own_ref], sems.at[pl.ds(9, 1)])
    for copy in copies:
        copy.wait()
    amp_ref[...] = residue_ref[...] * jnp.sqrt(one_minus_exp(2.0 * rate_ref[...]))
    for i in range(3):
        pad[i, pl.ds(0, HEAD), :] = jnp.zeros((HEAD, channels), F32)
        pad[i, pl.ds(HEAD, rows), :] = streams[i].astype(F32)
    block = 32
    for half in range(channels // LANES):
        lanes = pl.ds(half * LANES, LANES)
        for r in range(0, rows, block):
            sums = []
            for i in range(3):
                total = jnp.zeros((block, LANES), F32)
                for t in range(taps):
                    total = total + taps_ref[i, pl.ds(t, 1), lanes] * pad[i, pl.ds(HEAD + r - t, block), lanes]
                sums.append(total)
                if r == 0:
                    head_ref[i, :, lanes] = total[:HEAD]
            query_ref[half, pl.ds(r, block), :] = sums[0]
            gated_ref[half, pl.ds(r, block), :] = sums[1] * sums[2]
    sub = lax.broadcasted_iota(jnp.int32, (SUBS, LANES), 0)
    for half in range(channels // LANES):
        lanes = pl.ds(half * LANES, LANES)
        rates = [row_of(rate_ref, m, lanes) for m in range(modes)]
        retain = [wide(jnp.exp(-x)) for x in rates]
        state = [jnp.zeros((SUBS, LANES), F32) for _ in range(modes)]
        for step in range(steps):
            g = gated_ref[half, pl.ds(step, SUBS, stride=steps), :]
            state = [a * s + g for a, s in zip(retain, state)]
        for m in range(modes):
            s = state[m]
            for d in (1, 2, 4):
                drop = wide(jnp.exp(-(steps * d) * rates[m]))
                s = s + jnp.where(sub >= d, drop * pltpu.roll(s, d, 0), 0.0)
            state_ref[pl.ds(m, 1), lanes] = s[SUBS - 1 :]
            begin_ref[m, :, lanes] = jnp.where(sub >= 1, pltpu.roll(s, 1, 0), 0.0)
    for copy in sent:
        copy.wait()


def join_body(rows, rim_ref, head_ref, taps_ref, rate_ref, state_ref, out_ref, late_ref, top_ref, pad):
    modes, channels = rate_ref.shape
    taps = taps_ref.shape[1]
    sums = []
    for i in range(3):
        pad[i, pl.ds(0, HEAD), :] = rim_ref[pl.ds(i * RIM, RIM), :].astype(F32)[RIM - HEAD :]
        pad[i, pl.ds(HEAD, HEAD), :] = jnp.zeros((HEAD, channels), F32)
        total = head_ref[i]
        for t in range(1, taps):
            total = total + taps_ref[i, pl.ds(t, 1), :] * pad[i, pl.ds(HEAD - t, HEAD), :]
        sums.append(total)
    gated = sums[1] * sums[2]
    top_ref[0] = sums[0]
    top_ref[1] = gated
    more = gated - head_ref[1] * head_ref[2]
    rate = rate_ref[...]
    retain = jnp.exp(-rate)
    late = jnp.broadcast_to(more[:1], rate.shape)
    for i in range(1, taps - 1):
        late = retain * late + more[i : i + 1]
    late_ref[...] = late
    whole = (state_ref[...] + jnp.exp(-(rows - taps + 1) * rate) * late).astype(BF16)
    for i in range(out_ref.shape[0]):
        out_ref[i] = whole


def mix(taps, carried, refs, out_hbm, own_part, hyena, left, carry, sems):
    query_ref, gated_ref, begin_ref, late_ref, top_ref, rate_ref, amp_ref, skip_ref, own_ref = refs
    halves, rows, _ = query_ref.shape
    modes = rate_ref.shape[0]
    steps = rows // SUBS
    carry[0] = carried
    carry[1] = carried + jnp.exp((taps - 1) * rate_ref[...]) * late_ref[...]
    parts, copies = out_hbm.shape[0], []
    sub = lax.broadcasted_iota(jnp.int32, (SUBS, LANES), 0)
    ahead = sub.astype(F32) * float(steps)
    for half in range(halves):
        lanes = pl.ds(half * LANES, LANES)
        rates = [row_of(rate_ref, m, lanes) for m in range(modes)]
        retain = [wide(jnp.exp(-x)) for x in rates]
        amp = [wide(row_of(amp_ref, m, lanes)) for m in range(modes)]
        skip = wide(row_of(skip_ref, 0, lanes))
        state = [
            begin_ref[m, :, lanes]
            + jnp.exp(-ahead * rates[m])
            * jnp.where(sub >= 1, row_of(carry.at[1], m, lanes), row_of(carry.at[0], m, lanes))
            for m in range(modes)
        ]
        for step in range(steps):
            at = pl.ds(step, SUBS, stride=steps)
            g = gated_ref[half, at, :]
            query = query_ref[half, at, :]
            if step < taps - 1:
                query = jnp.where(sub >= 1, query, top_ref[0, pl.ds(step, 1), lanes])
                g = jnp.where(sub >= 1, g, top_ref[1, pl.ds(step, 1), lanes])
            state = [a * s + g for a, s in zip(retain, state)]
            terms = [a * s for a, s in zip(amp, state)] + [skip * g]
            while len(terms) > 1:
                terms = [x + y for x, y in zip(terms[::2], terms[1::2])] + terms[len(terms) // 2 * 2 :]
            hyena[half, at, :] = query * terms[0]
        left[:, lanes] = hyena[half].astype(BF16)
        copies += fetch([left.at[:, lanes]] * parts, [out_hbm.at[i, :, lanes] for i in range(parts)], sems.at[half])
    for c in range(0, own_part.shape[1], 256):
        at = pl.ds(c, 256)
        own_part[:, at] = jnp.dot(left[...], own_ref[:, at], preferred_element_type=F32).astype(BF16)
    for copy in copies:
        copy.wait()


def plane_body(taps, rows, parts_ref, *refs):
    *refs, before_ref, total_ref, out_hbm, own_part, hyena, left, carry, sems = refs
    rate_ref = refs[5]
    me = lax.axis_index("y") * lax.axis_size("core") + lax.axis_index("core")
    drop = jnp.exp(-rows * rate_ref[...])
    before = jnp.zeros(rate_ref.shape, F32)
    total = jnp.zeros(rate_ref.shape, F32)
    for i in range(parts_ref.shape[0]):
        part = parts_ref[i].astype(F32)
        before = jnp.where(i < me, before * drop + part, before)
        total = total * drop + part
    before_ref[...] = before
    for i in range(total_ref.shape[0]):
        total_ref[i] = total.astype(BF16)

    @pl.when(lax.axis_index("z") == 0)
    def _():
        mix(taps, before, refs, out_hbm, own_part, hyena, left, carry, sems)


def mix_body(taps, plane_rows, before_ref, planes_ref, _hyena, _own_part, *refs):
    *refs, out_hbm, own_part, hyena, left, carry, sems = refs
    query_ref, rate_ref = refs[0], refs[5]
    rows = query_ref.shape[1]
    z = lax.axis_index("z")

    @pl.when(z > 0)
    def _():
        me = lax.axis_index("y") * lax.axis_size("core") + lax.axis_index("core")
        rate = rate_ref[...]
        drop = jnp.exp(-plane_rows * rate)
        behind = jnp.zeros(rate.shape, F32)
        for i in range(planes_ref.shape[0]):
            behind = jnp.where(i < z, behind * drop + planes_ref[i].astype(F32), behind)
        carried = before_ref[...] + jnp.exp(-(rows * me).astype(F32) * rate) * behind
        mix(taps, carried, refs, out_hbm, own_part, hyena, left, carry, sems)


def order_body(left_ref, out_ref):
    parts, _, channels = left_ref.shape
    here, core = lax.axis_index("tp"), lax.axis_index("core")
    ahead, behind = lax.rem(here + 1, parts), lax.rem(here + parts - 1, parts)
    across = lax.rem(here + 2, parts)
    height = channels // 2
    out_ref[:, :channels] = left_ref[here]
    out_ref[:, channels : 2 * channels] = left_ref[jnp.where(core == 0, behind, ahead)]
    out_ref[:, 2 * channels : 3 * channels] = left_ref[jnp.where(core == 0, ahead, behind)]
    for i, half in enumerate((core, 1 - core)):
        columns = pl.ds(pl.multiple_of(half * height, height), height)
        out_ref[:, pl.ds(3 * channels + i * height, height)] = left_ref[across, :, columns]


def project_body(left_ref, own_part, *rest):
    *rights, out_hbm, done, sems = rest
    blocks, _, block = done.shape
    copies = []
    for b in range(blocks):
        at = pl.ds(b * block, block)
        total = own_part[:, at].astype(F32)
        begin = rights[0].shape[0]
        for right in rights:
            depth = right.shape[0]
            total += jnp.dot(left_ref[:, pl.ds(begin, depth)], right[:, at], preferred_element_type=F32)
            begin += depth
        done[b] = total.astype(BF16)
        copies.append(pltpu.make_async_copy(done.at[b], out_hbm.at[:, at], sems.at[b]))
        copies[-1].start()
    for copy in copies:
        copy.wait()


def local(query_in, key_in, value_in, short_weight, residue, rate, skip, out_weight):
    rows, channels = query_in.shape
    modes = rate.shape[0]
    taps = short_weight.shape[1]
    planes = lax.axis_size("z")
    plane = lax.axis_size("y") * lax.axis_size("core")
    parts = lax.axis_size("tp")
    width = out_weight.shape[1] // parts
    order = ("z", "y", "core")
    devices = planes * plane
    by_half = (channels // LANES, rows, LANES)
    skip = skip.reshape(1, -1)
    query_in, key_in, value_in, short_weight, residue, rate, skip, out_weight = (
        pltpu.with_memory_space_constraint(x, pltpu.HBM)
        for x in (query_in, key_in, value_in, short_weight, residue, rate, skip, out_weight)
    )
    rims = call(
        rim_body, [HBM] * 3, shape((3 * RIM, channels), BF16), "rims", [pltpu.SemaphoreType.DMA((3,))]
    )(query_in, key_in, value_in)
    rims = lax.ppermute(rims, order, [(i, i + 1) for i in range(devices - 1)])
    queries, gated, begin, states, heads, taps_here, rate, amplitude, skip, *blocks, own = call(
        gate_body,
        [HBM] * 8,
        (
            shape(by_half, F32),
            shape(by_half, F32),
            shape((modes, SUBS, channels), F32),
            shape((modes, channels), F32),
            shape((3, HEAD, channels), F32),
            shape(short_weight.shape, F32),
            shape((modes, channels), F32),
            shape((modes, channels), F32),
            shape((1, channels), F32),
            shape((channels, width), BF16),
            shape((channels // 2, width), BF16),
            pltpu.VMEM((channels, width), BF16),
        ),
        "gate",
        [
            pltpu.VMEM((3, rows, channels), BF16),
            pltpu.VMEM((modes, channels), F32),
            pltpu.VMEM((3, HEAD + rows, channels), F32),
            pltpu.SemaphoreType.DMA((10,)),
        ],
    )(query_in, key_in, value_in, short_weight, rate, residue, skip, out_weight)
    side, half = blocks
    side = lax.ppermute(
        side,
        ("core", "tp"),
        [(c * parts + t, c * parts + (t + 1 - 2 * c) % parts) for c in range(2) for t in range(parts)],
    )
    half = lax.ppermute(half, "tp", [(t, (t + 2) % parts) for t in range(parts)])
    states, late, top = call(
        lambda *refs: join_body(rows, *refs),
        [VMEM] * 5,
        (
            shape((plane, modes, channels), BF16),
            shape((modes, channels), F32),
            shape((2, HEAD, channels), F32),
        ),
        "join",
        [pltpu.VMEM((3, 2 * HEAD, channels), F32)],
    )(rims, heads, taps_here, rate, states)
    states = lax.all_to_all(states, ("y", "core"), 0, 0, tiled=True)
    shared = (queries, gated, begin, late, top, rate, amplitude, skip, own)
    scratch = [
        pltpu.VMEM(by_half, F32),
        pltpu.VMEM((rows, channels), BF16),
        pltpu.VMEM((2, modes, channels), F32),
        pltpu.SemaphoreType.DMA((channels // LANES, parts)),
    ]
    before, totals, hyena, own_part = call(
        lambda *refs: plane_body(taps, rows, *refs),
        [VMEM] * (1 + len(shared)),
        (
            shape((modes, channels), F32),
            shape((planes, modes, channels), BF16),
            shape((parts, rows, channels), BF16),
            shape((rows, width), BF16),
        ),
        "plane",
        scratch,
        out_spec=(VMEM, VMEM, ANY, VMEM),
        us=4,
    )(states, *shared)
    totals = lax.all_to_all(totals, "z", 0, 0, tiled=True)
    swapped = [lax.ppermute(x, "core", [(0, 1), (1, 0)]) for x in (side, half)]
    hyena, own_part = call(
        lambda *refs: mix_body(taps, rows * plane, *refs),
        [VMEM] * 2 + [ANY] + [VMEM] * (1 + len(shared)),
        (shape((parts, rows, channels), BF16), shape((rows, width), BF16)),
        "mix",
        scratch,
        out_spec=(ANY, VMEM),
        aliases={2: 0, 3: 1},
        us=2,
    )(before, totals, hyena, own_part, *shared)
    hyena = lax.all_to_all(hyena, "tp", 0, 0, tiled=True)
    hyena = call(order_body, [VMEM], shape((rows, parts * channels), BF16), "order", us=0)(hyena)
    block = 256
    return call(
        project_body,
        [VMEM] * 6,
        shape((rows, width), BF16),
        "project",
        [pltpu.VMEM((width // block, rows, block), BF16), pltpu.SemaphoreType.DMA((width // block,))],
        out_spec=HBM,
    )(hyena, own_part, side, swapped[0], half, swapped[1])


def solution(mesh):
    fine = Mesh(mesh.devices.reshape(8, 8, 2, 4), ("z", "y", "core", "tp"))
    seq = ("z", "y", "core")
    in_specs = (
        P(seq, "tp"),
        P(seq, "tp"),
        P(seq, "tp"),
        P(None, None, "tp"),
        P(None, "tp"),
        P(None, "tp"),
        P("tp"),
        P("tp", None),
    )
    return jax.shard_map(local, mesh=fine, in_specs=in_specs, out_specs=P(seq, "tp"), check_vma=False)
```
